32 devices in a mesh: dp: 2 (over x), ctx: 4 (over z), exp: 4 (over y, core).
Axes of the slice: x: 2, y: 2, z: 4, core: 2. Of those that a mesh axis runs over, the one named last changes fastest.
Arguments:
- tokens: bfloat16 [8, 2048, 1536], P(('dp', 'exp'), 'ctx'), may hold values from -6 to 6
- attn_gain: float32 [1536], replicated, may hold values from 0.5 to 1.5
- w_query: bfloat16 [1536, 1536], replicated, may hold values from -0.15625 to 0.15625
- key_matrix: bfloat16 [1536, 256], replicated, may hold values from -0.15625 to 0.15625
- value_matrix: bfloat16 [1536, 256], replicated, may hold values from -0.15625 to 0.15625
- w_out: bfloat16 [1536, 1536], replicated, may hold values from -2 to 2
- ffn_gain: float32 [1536], replicated, may hold values from 0.5 to 1.5
- expert_gate_up: bfloat16 [8, 1536, 1536], P('exp'), may hold values from -0.15625 to 0.15625
- expert_down: bfloat16 [8, 768, 1536], P('exp'), may hold values from -0.21875 to 0.21875
- expert_ids: int32 [8, 2048, 4], P(('dp', 'exp'), 'ctx'), may hold values from 0 to 7, all different within a row; in each aligned block of 512 rows (0 to 511, 512 to 1023, ..., all dimensions but the last counted through in order) at most 320 rows name the same one
- gate_weights: float32 [8, 2048, 4], P(('dp', 'exp'), 'ctx'), may hold values from 0.2 to 0.6
- span_order: int32 [8, 8], P(('dp', 'exp')), may hold values from 0 to 7, each once within a row
- out_grad: bfloat16 [8, 2048, 1536], P(('dp', 'exp'), 'ctx'), may hold values from -6 to 6
Outputs:
- layer_output: bfloat16 [8, 2048, 1536], P(('dp', 'exp'), 'ctx')
- tokens_grad: bfloat16 [8, 2048, 1536], P(('dp', 'exp'), 'ctx')
- attn_gain_grad: float32 [1536], P(('dp', 'ctx', 'exp'))
- w_query_grad: float32 [1536, 1536], P(('dp', 'ctx', 'exp'))
- w_key_grad: float32 [1536, 256], P(('dp', 'ctx', 'exp'))
- w_value_grad: float32 [1536, 256], P(('dp', 'ctx', 'exp'))
- w_out_grad: float32 [1536, 1536], P(('dp', 'ctx', 'exp'))
- ffn_gain_grad: float32 [1536], P(('dp', 'ctx', 'exp'))
- expert_gate_up_grad: float32 [8, 1536, 1536], P('exp', ('dp', 'ctx'))
- expert_down_grad: float32 [8, 768, 1536], P('exp', ('dp', 'ctx'))
The draws below stay inside these ranges and needn't reach their ends.
Inputs may be any that keep to these rules, and one draw needn't show every extreme that they name: `expert_ids`: within the 512 rows of one device, each row names 4 different experts and no expert is named by more than 320 of them; in every draw some expert is named by exactly 320 rows of some such block. `span_order`: each row is a permutation of the 2 * 4 spans of 256 positions of its sequence.
All inputs are finite; a program needn't handle non-finite values.
Results may differ from the reference program's by a relative error of at most 0.028.
Values may be sent and summed in bfloat16 or wider, within the bound.
A program may use at most 320 MiB of HBM per device.

```python
import math
import jax
import jax.numpy as jnp
import numpy as np
from jax import lax

MODEL_WIDTH = 1536
QUERY_HEADS = 12
KEY_VALUE_HEADS = 2
HEAD_SIZE = 128
FF = 768
TOPK = 4
TOK_DEV = 512
HALF = 256
SEQ_LEN = 2048
SEQS = 8
EXPERTS = 8
CAP = 320
N_CTX = 4


def levels(rng, extent, cuts, low, top_value):
    gain = 1.0
    for position, shards_of in cuts:
        steps = jax.random.uniform(jax.random.fold_in(jax.random.fold_in(rng, 6), position), (shards_of,), jnp.float32, low / len(cuts), top_value / len(cuts))
        gain = gain * jnp.repeat(jnp.exp(steps), extent[position] // shards_of).reshape((-1,) + (1,) * (len(extent) - 1 - position))
    return gain


def assign_block(own_key, own, number, rows, count, top, limit, lean):
    ranking = jax.random.permutation(own_key, count)
    packed, usual = portions_of(count, rows * top, limit, lean, True), portions_of(count, rows * top, limit, lean, False)
    places = jnp.arange(count)

    def named(tallies, offset_by):
        used = int((tallies > 0).sum())
        fixed = max(1, used // 4)
        moved = fixed + (places - fixed + offset_by * (used - fixed)) % max(1, count - fixed)
        return jnp.zeros((count,), jnp.int32).at[ranking[jnp.where(places < fixed, places, moved)]].set(jnp.asarray(tallies, jnp.int32))

    tallies = jnp.where(number % 4 == 0, named(packed, number // 4), named(usual, number - number // 4 - 1))
    mixed = jax.random.permutation(jax.random.fold_in(own, 3), count)
    donor, taker = mixed[0:count // 2 * 2:2], mixed[1:count // 2 * 2:2]
    room = jnp.minimum(tallies[donor] - 1, limit - tallies[taker]) // 2
    room = jnp.where((donor == ranking[0]) | (taker == ranking[0]) | (tallies[taker] == 0), 0, jnp.maximum(room, 0))
    moved = jax.random.randint(jax.random.fold_in(own, 4), (count // 2,), 0, 1 << 20) % (room + 1)
    tallies = tallies.at[donor].add(-moved).at[taker].add(moved)
    members = jnp.searchsorted(jnp.cumsum(tallies), jnp.arange(rows * top), side="right").astype(jnp.int32)
    table = members.reshape(top, rows).T
    table = table[jax.random.permutation(jax.random.fold_in(own, 1), rows)]
    offset_by = jax.random.randint(jax.random.fold_in(own, 2), (rows, 1), 0, top)
    return jnp.take_along_axis(table, (jnp.arange(top)[None, :] + offset_by) % top, axis=1)


def portions_of(count, total, bound, lean, full):
    portions = [(1 << 20) // math.isqrt(grade ** lean) + 1 for grade in range(1, count + 1)]
    largest = bound if full else min(bound, max(-(-total // count), total * portions[0] // sum(portions)))
    least = 1 if total - largest >= count - 1 else 0
    given, spare = [largest] + [least] * (count - 1), total - largest - least * (count - 1)
    while spare > 0:
        movable = [i for i in range(1, count) if given[i] < largest] or [i for i in range(1, count) if given[i] < bound]
        pool, budget = sum([portions[i] for i in movable]), spare
        for i in movable:
            extra = min(bound - given[i], max(1, budget * portions[i] // pool), spare)
            given[i] = given[i] + extra
            spare = spare - extra
    return np.array(given)


def scatter_about(own_key, extent, scale, limit, cuts=(), kind=jnp.bfloat16):
    array = scale * jax.random.normal(own_key, extent, jnp.float32)
    if cuts:
        array = array * levels(own_key, extent, cuts, -0.22, 0.18)
    return jnp.clip(array, -limit, limit).astype(kind)


def setup_inputs(seed: int = 0) -> dict:
    streams_of = jax.random.split(jax.random.key(seed), 14)
    tokens = scatter_about(streams_of[0], (SEQS, SEQ_LEN, MODEL_WIDTH), 1.0, 6.0, ((0, 8), (1, 4)))
    attn_gain = jnp.clip(1.0 + 0.1 * jax.random.normal(streams_of[1], (MODEL_WIDTH,), jnp.float32), 0.5, 1.5)
    w_query = scatter_about(streams_of[2], (MODEL_WIDTH, QUERY_HEADS * HEAD_SIZE), MODEL_WIDTH ** -0.5, 0.15625)
    key_matrix = scatter_about(streams_of[3], (MODEL_WIDTH, KEY_VALUE_HEADS * HEAD_SIZE), MODEL_WIDTH ** -0.5, 0.15625)
    value_matrix = scatter_about(streams_of[4], (MODEL_WIDTH, KEY_VALUE_HEADS * HEAD_SIZE), MODEL_WIDTH ** -0.5, 0.15625)
    w_out = scatter_about(streams_of[5], (QUERY_HEADS * HEAD_SIZE, MODEL_WIDTH), 8 ** -0.5, 2.0)
    ffn_gain = jnp.clip(1.0 + 0.1 * jax.random.normal(streams_of[6], (MODEL_WIDTH,), jnp.float32), 0.5, 1.5)
    expert_gate_up = scatter_about(streams_of[7], (EXPERTS, MODEL_WIDTH, 2 * FF), MODEL_WIDTH ** -0.5, 0.15625, ((0, 4),))
    expert_down = scatter_about(streams_of[8], (EXPERTS, FF, MODEL_WIDTH), FF ** -0.5, 0.21875, ((0, 4),))
    expert_ids_keys = jax.random.split(jax.random.fold_in(streams_of[9], 1), SEQS * SEQ_LEN // TOK_DEV)
    expert_ids_turns = jax.random.permutation(jax.random.fold_in(streams_of[9], 3), SEQS * SEQ_LEN // TOK_DEV)
    expert_ids = jax.vmap(lambda own, number: assign_block(jax.random.fold_in(streams_of[9], 2), own, number, TOK_DEV, EXPERTS, TOPK, CAP, 1))(expert_ids_keys, expert_ids_turns).reshape((SEQS, SEQ_LEN, TOPK))
    gate_weights = jnp.clip(jnp.exp(math.log(0.6) - 1.0986123 * jax.random.uniform(streams_of[10], (SEQS, SEQ_LEN, TOPK), jnp.float32) ** levels(streams_of[10], (SEQS, SEQ_LEN, TOPK), ((0, 8), (1, 4)), -0.2, 0.2)), 0.2, 0.6)
    span_order = jax.vmap(lambda own: jax.random.permutation(own, 2 * N_CTX))(jax.random.split(streams_of[11], SEQS)).reshape((SEQS, 2 * N_CTX)).astype(jnp.int32)
    out_grad = scatter_about(streams_of[12], (SEQS, SEQ_LEN, MODEL_WIDTH), 1.0, 6.0, ((0, 8), (1, 4)))
    return dict(tokens=tokens, attn_gain=attn_gain, w_query=w_query, key_matrix=key_matrix, value_matrix=value_matrix, w_out=w_out, ffn_gain=ffn_gain, expert_gate_up=expert_gate_up, expert_down=expert_down, expert_ids=expert_ids, gate_weights=gate_weights, span_order=span_order, out_grad=out_grad)


epsilon = 1e-06
rope_base = 1000000.0
causal_masked_score = -1e+30

@jax.custom_vjp
def reduced_precision(v):
    return lax.optimization_barrier(v.astype(jnp.bfloat16)).astype(jnp.float32)

@jax.custom_vjp
def reduced_precision_back(v):
    return v

def low_keep(v):
    return (reduced_precision(v), None)

def low_pass(kept, grad):
    return (grad,)

def back_keep(v):
    return (v, None)

def back_low(kept, grad):
    return (reduced_precision(grad),)
reduced_precision.defvjp(low_keep, low_pass)
reduced_precision_back.defvjp(back_keep, back_low)

def precise_product(left_side, right_side):
    return jnp.dot(left_side, right_side, precision=lax.Precision.HIGHEST)

def rms_scale(values, gain_vector):
    return values * lax.rsqrt(lax.optimization_barrier(jnp.mean(values * values, axis=-1, keepdims=True)) + epsilon) * gain_vector

def apply_rotary(values, rotary_angles):
    middle = values.shape[-1] // 2
    cosine = jnp.cos(rotary_angles)[:, None, :]
    sine_part = jnp.sin(rotary_angles)[:, None, :]
    front_half = values[..., :middle]
    back_half = values[..., middle:]
    return jnp.concatenate([front_half * cosine - back_half * sine_part, back_half * cosine + front_half * sine_part], axis=-1)

def angle_table(positions):
    exponent = jnp.arange(HEAD_SIZE // 2, dtype=jnp.float32) * (-2.0 / HEAD_SIZE)
    frequency = jnp.power(jnp.float32(rope_base), exponent)
    return positions.astype(jnp.float32)[:, None] * frequency[None, :]

def sequence_layer(sequence_input, sequence_ids, sequence_gates, span_row, weights):
    attn_gain, w_query, key_matrix, value_matrix, w_out, ffn_gain, gate_up, down_proj = weights
    sequence_length = sequence_input.shape[0]
    query_group_count = QUERY_HEADS // KEY_VALUE_HEADS
    positions = (span_row[:, None] * HALF + jnp.arange(HALF, dtype=jnp.int32)[None, :]).reshape(-1).astype(jnp.int32)
    rotary_angles = angle_table(positions)
    normalized_input = reduced_precision(rms_scale(sequence_input, attn_gain))
    query_linear = reduced_precision_back(precise_product(normalized_input, w_query)).reshape(sequence_length, QUERY_HEADS, HEAD_SIZE)
    key_linear = reduced_precision_back(precise_product(normalized_input, key_matrix)).reshape(sequence_length, KEY_VALUE_HEADS, HEAD_SIZE)
    value_head_rows = reduced_precision(reduced_precision_back(precise_product(normalized_input, value_matrix))).reshape(sequence_length, KEY_VALUE_HEADS, HEAD_SIZE)
    query_rows = reduced_precision(apply_rotary(query_linear, rotary_angles)).reshape(sequence_length, KEY_VALUE_HEADS, query_group_count, HEAD_SIZE)
    key_heads = reduced_precision(apply_rotary(key_linear, rotary_angles))
    block_rows = min(512, sequence_length)

    def attend(start_row):
        query_block = lax.dynamic_slice_in_dim(query_rows, start_row, block_rows, 0)
        block_positions = lax.dynamic_slice_in_dim(positions, start_row, block_rows, 0)
        raw_scores = reduced_precision_back(jnp.einsum('qkgd,skd->kgqs', query_block, key_heads, precision=lax.Precision.HIGHEST))
        allowed = (positions[None, :] <= block_positions[:, None])[None, None]
        scores = jnp.where(allowed, raw_scores * HEAD_SIZE ** (-0.5), causal_masked_score)
        row_max = lax.optimization_barrier(jnp.max(scores, axis=-1, keepdims=True))
        weights_exp = jnp.exp(scores - row_max)
        probabilities = reduced_precision(weights_exp / lax.optimization_barrier(jnp.sum(weights_exp, axis=-1, keepdims=True)))
        mixture = jnp.einsum('kgqs,skd->qkgd', probabilities, value_head_rows, precision=lax.Precision.HIGHEST)
        return mixture.reshape(block_rows, QUERY_HEADS * HEAD_SIZE)
    starts = jnp.arange(sequence_length // block_rows, dtype=jnp.int32) * block_rows
    attention_output = lax.map(jax.checkpoint(attend), starts).reshape(sequence_length, QUERY_HEADS * HEAD_SIZE)
    attended_low = reduced_precision(reduced_precision_back(attention_output))
    residual_mid = sequence_input + reduced_precision_back(precise_product(attended_low, w_out))
    normed_ffn = reduced_precision(rms_scale(residual_mid, ffn_gain))
    blocks_here = sequence_length // TOK_DEV
    routes = TOK_DEV * TOPK
    experts = gate_up.shape[0]
    flat_ids = sequence_ids.reshape(blocks_here, routes).astype(jnp.int32)
    expert_match = (flat_ids[:, :, None] == jnp.arange(experts, dtype=jnp.int32)[None, None, :]).astype(jnp.int32)
    rank_in_block = lax.optimization_barrier(jnp.sum((jnp.cumsum(expert_match, axis=1) - 1) * expert_match, axis=-1))
    block_index = jnp.arange(blocks_here, dtype=jnp.int32)[:, None]
    slot_index = (flat_ids * (blocks_here * CAP) + block_index * CAP + rank_in_block).reshape(-1).astype(jnp.int32)
    route_owner = jnp.arange(sequence_length * TOPK, dtype=jnp.int32) // TOPK
    slot_owner = jnp.full((experts * blocks_here * CAP,), sequence_length, dtype=jnp.int32).at[slot_index].set(route_owner)
    padded = jnp.concatenate([normed_ffn, jnp.zeros((1, MODEL_WIDTH), dtype=jnp.float32)], axis=0)
    routed_rows = reduced_precision_back(padded[slot_owner]).reshape(experts, blocks_here * CAP, MODEL_WIDTH)

    def expert(inputs):
        expert_rows, expert_gate_up, expert_down = inputs
        projected = reduced_precision_back(precise_product(expert_rows, expert_gate_up))
        hidden = reduced_precision(jax.nn.gelu(projected[:, :FF]) * projected[:, FF:])
        return reduced_precision(reduced_precision_back(precise_product(hidden, expert_down)))
    results = lax.map(jax.checkpoint(expert), (routed_rows, gate_up, down_proj))
    routed = results.reshape(-1, MODEL_WIDTH)[slot_index].reshape(sequence_length, TOPK, MODEL_WIDTH)
    mixed_experts = lax.optimization_barrier(jnp.sum(routed * sequence_gates[:, :, None], axis=1))
    return residual_mid + mixed_experts

def reference(tokens, attn_gain, w_query, key_matrix, value_matrix, w_out, ffn_gain, expert_gate_up, expert_down, expert_ids, gate_weights, span_order, out_grad):

    def forward(layer_input, norm_one, query_weight, key_weight, value_weight, output_weight, norm_two, gate_up_weight, down_weight):
        weights = (norm_one, query_weight, key_weight, value_weight, output_weight, norm_two, gate_up_weight, down_weight)

        def one_sequence(pieces):
            sequence_input, sequence_ids, sequence_gates, span_row = pieces
            return sequence_layer(sequence_input, sequence_ids, sequence_gates, span_row, weights)
        return lax.map(jax.checkpoint(one_sequence), (layer_input, expert_ids, gate_weights, span_order))
    result, pullback = jax.vjp(forward, tokens.astype(jnp.float32), attn_gain, w_query.astype(jnp.float32), key_matrix.astype(jnp.float32), value_matrix.astype(jnp.float32), w_out.astype(jnp.float32), ffn_gain, expert_gate_up.astype(jnp.float32), expert_down.astype(jnp.float32))
    grads = pullback(out_grad.astype(jnp.float32))
    return (result.astype(jnp.bfloat16), grads[0].astype(jnp.bfloat16), grads[1], grads[2], grads[3], grads[4], grads[5], grads[6], grads[7], grads[8])
```

```python
import functools
import math

import jax
import jax.numpy as jnp
from jax import lax
from jax.experimental import pallas as pl
from jax.experimental.pallas import tpu as pltpu
from jax.sharding import PartitionSpec as P

MODEL_WIDTH = 1536
QUERY_HEADS = 12
KEY_VALUE_HEADS = 2
GROUP = QUERY_HEADS // KEY_VALUE_HEADS
HEAD_SIZE = 128
KV_WIDTH = KEY_VALUE_HEADS * HEAD_SIZE
FF = 768
TOPK = 4
EXP_DEV = 2
TOK_DEV = 512
HALF = 256

epsilon = 1e-06
rope_base = 1000000.0
masked_score = -1e30
score_scale = HEAD_SIZE ** (-0.5)
score_to_log2 = score_scale * math.log2(math.e)
gelu_c = math.sqrt(2.0 / math.pi)

f32 = jnp.float32
bf16 = jnp.bfloat16
NT = (((1,), (1,)), ((), ()))
TN = (((0,), (0,)), ((), ()))
VMEM_BYTES = 60 * 1024 * 1024


def dot(a, b):
    return jnp.dot(a, b, preferred_element_type=f32)


def dot_nt(a, b):
    return lax.dot_general(a, b, NT, preferred_element_type=f32)


def dot_tn(a, b):
    return lax.dot_general(a, b, TN, preferred_element_type=f32)


def params(**more):
    return pltpu.CompilerParams(vmem_limit_bytes=VMEM_BYTES, **more)


def cost(flops, size, exps=0):
    return pl.CostEstimate(flops=int(flops), bytes_accessed=int(size), transcendentals=int(exps))


def whole(shape):
    return pl.BlockSpec(shape, lambda *_: (0,) * len(shape))


def rotate(values, cosine, signed_sine):
    return values * cosine + pltpu.roll(values, HEAD_SIZE // 2, 1) * signed_sine


def rotate_back(values, cosine, signed_sine):
    return values * cosine - pltpu.roll(values, HEAD_SIZE // 2, 1) * signed_sine


def norm_kv_kernel(x_ref, gain_ref, wk_ref, wv_ref, cos_ref, sin_ref, normed_ref, kv_ref):
    x = x_ref[...].astype(f32)
    r = lax.rsqrt(jnp.mean(x * x, axis=-1, keepdims=True) + epsilon)
    normed = (x * r * gain_ref[...]).astype(bf16)
    normed_ref[...] = normed
    keys = dot(normed, wk_ref[...])
    cosine, sine = cos_ref[...], sin_ref[...]
    for head in range(KEY_VALUE_HEADS):
        span = slice(head * HEAD_SIZE, (head + 1) * HEAD_SIZE)
        kv_ref[:, span] = rotate(keys[:, span], cosine, sine).astype(bf16)
    kv_ref[:, KV_WIDTH:] = dot(normed, wv_ref[...]).astype(bf16)


def norm_kv(x, gain, wk, wv, cosine, sine):
    rows = x.shape[0]
    return pl.pallas_call(
        norm_kv_kernel,
        out_shape=(
            jax.ShapeDtypeStruct((rows, MODEL_WIDTH), bf16),
            jax.ShapeDtypeStruct((rows, 2 * KV_WIDTH), bf16),
        ),
        compiler_params=params(),
        cost_estimate=cost(4 * rows * MODEL_WIDTH * KV_WIDTH, 5e6),
        name="norm_kv",
    )(x, gain, wk, wv, cosine, sine)


Q_TILE = 512


def query_kernel(normed_ref, wq_ref, cos_ref, sin_ref, q_ref):
    lin = dot(normed_ref[...], wq_ref[...])
    cosine, sine = cos_ref[...], sin_ref[...]
    for head in range(Q_TILE // HEAD_SIZE):
        span = slice(head * HEAD_SIZE, (head + 1) * HEAD_SIZE)
        q_ref[:, span] = rotate(lin[:, span], cosine, sine).astype(bf16)


def query_projection(normed, wq, cosine, sine):
    rows = normed.shape[0]
    return pl.pallas_call(
        query_kernel,
        grid=(MODEL_WIDTH // Q_TILE,),
        in_specs=[
            whole((rows, MODEL_WIDTH)),
            pl.BlockSpec((MODEL_WIDTH, Q_TILE), lambda t: (0, t)),
            whole((rows, HEAD_SIZE)),
            whole((rows, HEAD_SIZE)),
        ],
        out_specs=pl.BlockSpec((rows, Q_TILE), lambda t: (0, t)),
        out_shape=jax.ShapeDtypeStruct((rows, MODEL_WIDTH), bf16),
        compiler_params=params(),
        cost_estimate=cost(2 * rows * MODEL_WIDTH * MODEL_WIDTH, 8e6),
        name="query_projection",
    )(normed, wq, cosine, sine)


def attention_kernel(
    q_ref, k_ref, v_ref, qpos_ref, kpos_ref, wo_ref, x_ref, gain_ref,
    att_ref, att_low_ref, lse_ref, mid_ref, nf_ref, lse_cols,
):
    head = pl.program_id(0)
    rows = q_ref.shape[0]
    half = rows // 2
    keys, values = k_ref[...], v_ref[...]
    lane = lax.broadcasted_iota(jnp.int32, (half, HEAD_SIZE), 1)
    for part in range(2):
        band = slice(part * half, (part + 1) * half)
        scores = dot_nt(q_ref[band, :], keys)
        scores = jnp.where(kpos_ref[...] <= qpos_ref[band, :], scores, masked_score)
        top = jnp.max(scores, axis=-1, keepdims=True) * score_to_log2
        weights = jnp.exp2(scores * score_to_log2 - top)
        total = jnp.sum(weights, axis=-1, keepdims=True)
        out = dot(weights.astype(bf16), values) / total
        columns = pl.ds(pl.multiple_of(head * HEAD_SIZE, HEAD_SIZE), HEAD_SIZE)
        att_ref[band, columns] = out
        att_low_ref[band, columns] = out.astype(bf16)
        lse = top + jnp.log2(total)
        lse_cols[band, :] = jnp.where(lane == head, lse, lse_cols[band, :])

    @pl.when(head == QUERY_HEADS - 1)
    def _():
        lse_ref[...] = lse_cols[...].T[: lse_ref.shape[0], :]
        for part in range(2):
            band = slice(part * half, (part + 1) * half)
            mid = x_ref[band, :].astype(f32) + dot(att_low_ref[band, :], wo_ref[...])
            mid_ref[band, :] = mid
            r = lax.rsqrt(jnp.mean(mid * mid, axis=-1, keepdims=True) + epsilon)
            nf_ref[band, :] = (mid * r * gain_ref[...]).astype(bf16)


HEAD_ROWS = 16


def attention_forward(q, kv_all, qpos_col, kpos_row, wo, x, gain):
    rows, keys = q.shape[0], kv_all.shape[0]
    return pl.pallas_call(
        attention_kernel,
        grid=(QUERY_HEADS,),
        in_specs=[
            pl.BlockSpec((rows, HEAD_SIZE), lambda h: (0, h)),
            pl.BlockSpec((keys, HEAD_SIZE), lambda h: (0, h // GROUP)),
            pl.BlockSpec((keys, HEAD_SIZE), lambda h: (0, KEY_VALUE_HEADS + h // GROUP)),
            whole((rows, 1)),
            whole((1, keys)),
            whole((MODEL_WIDTH, MODEL_WIDTH)),
            whole((rows, MODEL_WIDTH)),
            whole((1, MODEL_WIDTH)),
        ],
        out_specs=(
            whole((rows, MODEL_WIDTH)),
            whole((rows, MODEL_WIDTH)),
            whole((HEAD_ROWS, rows)),
            whole((rows, MODEL_WIDTH)),
            whole((rows, MODEL_WIDTH)),
        ),
        out_shape=(
            jax.ShapeDtypeStruct((rows, MODEL_WIDTH), f32),
            jax.ShapeDtypeStruct((rows, MODEL_WIDTH), bf16),
            jax.ShapeDtypeStruct((HEAD_ROWS, rows), f32),
            jax.ShapeDtypeStruct((rows, MODEL_WIDTH), f32),
            jax.ShapeDtypeStruct((rows, MODEL_WIDTH), bf16),
        ),
        scratch_shapes=[pltpu.VMEM((rows, HEAD_SIZE), f32)],
        compiler_params=params(),
        cost_estimate=cost(8 * rows * keys * MODEL_WIDTH, 2e7, rows * keys * QUERY_HEADS),
        name="attention_forward",
    )(q, kv_all, kv_all, qpos_col, kpos_row, wo, x, gain)


def expert_kernel(
    pos_row_ref, pos_col_ref, gate_row_ref, x_ref, g_ref, wgu_ref, wd_ref, *rest
):
    (y_ref, dx_ref, rows_ref, hidden_ref, slot_grad_ref, pg_ref, y_acc, dx_acc) = rest[-8:]
    expert = pl.program_id(0)
    capacity = rows_ref.shape[-2]
    tokens = x_ref.shape[0]
    slot_r = lax.broadcasted_iota(jnp.int32, (capacity, tokens), 0)
    match = slot_r == pos_row_ref[0]
    pick = match.astype(bf16)
    slot_c = lax.broadcasted_iota(jnp.int32, (tokens, capacity), 1)
    place = (slot_c == pos_col_ref[0]).astype(bf16)
    gates = jnp.sum(jnp.where(match, gate_row_ref[0], 0.0), axis=1, keepdims=True)
    rows = dot(pick, x_ref[...]).astype(bf16)
    slot_grad = (dot(pick, g_ref[...]) * gates).astype(bf16)
    rows_ref[0, 0] = rows
    slot_grad_ref[0, 0] = slot_grad
    projected = dot(rows, wgu_ref[0])
    gate, up = projected[:, :FF], projected[:, FF:]
    square = gate * gate
    tangent = jnp.tanh(gelu_c * (gate + 0.044715 * (square * gate)))
    half_plus = 0.5 + 0.5 * tangent
    activated = gate * half_plus
    slope = half_plus + 0.5 * gate * (1.0 - tangent * tangent) * (
        gelu_c * (1.0 + (3.0 * 0.044715) * square)
    )
    hidden = (activated * up).astype(bf16)
    hidden_ref[0, 0] = hidden
    result = (dot(hidden, wd_ref[0]) * gates).astype(bf16)
    hidden_grad = dot_nt(slot_grad, wd_ref[0])
    pg_ref[0, 0, :, :FF] = (hidden_grad * up * slope).astype(bf16)
    pg_ref[0, 0, :, FF:] = (hidden_grad * activated).astype(bf16)
    rows_grad = dot_nt(pg_ref[0, 0], wgu_ref[0]).astype(bf16)
    y_part = dot(place, result)
    dx_part = dot(place, rows_grad)

    @pl.when(expert == 0)
    def _():
        y_acc[...] = y_part
        dx_acc[...] = dx_part

    @pl.when(expert != 0)
    def _():
        y_acc[...] += y_part
        dx_acc[...] += dx_part

    @pl.when(expert == EXP_DEV - 1)
    def _():
        y_ref[...] = y_acc[...].astype(bf16)
        dx_ref[...] = dx_acc[...].astype(bf16)


def expert_block(block, blocks, capacity, pos, gates, x, g, wgu, wd, kept):
    tokens = x.shape[0]
    kept_shapes = tuple(
        jax.ShapeDtypeStruct((EXP_DEV, blocks, capacity, width), bf16)
        for width in (MODEL_WIDTH, FF, MODEL_WIDTH, 2 * FF)
    )
    kept_specs = tuple(
        pl.BlockSpec((1, 1, capacity, s.shape[-1]), lambda e: (e, block, 0, 0)) for s in kept_shapes
    )
    aliases = {} if kept is None else {7 + i: 2 + i for i in range(4)}
    flops = EXP_DEV * 2 * capacity * (4 * tokens * MODEL_WIDTH + 9 * MODEL_WIDTH * FF)
    out = pl.pallas_call(
        expert_kernel,
        grid=(EXP_DEV,),
        in_specs=[
            pl.BlockSpec((1, 1, tokens), lambda e: (e, 0, 0)),
            pl.BlockSpec((1, tokens, 1), lambda e: (e, 0, 0)),
            pl.BlockSpec((1, 1, tokens), lambda e: (e, 0, 0)),
            whole((tokens, MODEL_WIDTH)),
            whole((tokens, MODEL_WIDTH)),
            pl.BlockSpec((1, MODEL_WIDTH, 2 * FF), lambda e: (e, 0, 0)),
            pl.BlockSpec((1, FF, MODEL_WIDTH), lambda e: (e, 0, 0)),
        ]
        + [pl.BlockSpec(memory_space=pl.ANY) for _ in aliases],
        out_specs=(whole((tokens, MODEL_WIDTH)), whole((tokens, MODEL_WIDTH))) + kept_specs,
        out_shape=(
            jax.ShapeDtypeStruct((tokens, MODEL_WIDTH), bf16),
            jax.ShapeDtypeStruct((tokens, MODEL_WIDTH), bf16),
        )
        + kept_shapes,
        scratch_shapes=[pltpu.VMEM((tokens, MODEL_WIDTH), f32)] * 2,
        input_output_aliases=aliases,
        compiler_params=params(),
        cost_estimate=cost(flops, 3e7),
        name="expert_block",
    )(pos[:, None, :], pos[:, :, None], gates[:, None, :], x, g, wgu, wd, *(kept or ()))
    return out[0], out[1], out[2:]


def middle_kernel(*refs):
    count = len(refs) - 11
    parts = refs[:count]
    mid_ref, g_ref, gain_ref, wo_ref, att_ref = refs[count : count + 5]
    mg_ref, mgl_ref, ag_ref, delta_ref, dgain_ref, delta_cols = refs[count + 5 :]
    rows = mid_ref.shape[0]
    half = rows // 2
    lane = lax.broadcasted_iota(jnp.int32, (half, HEAD_SIZE), 1)
    dgain = jnp.zeros((1, MODEL_WIDTH), f32)
    for part in range(2):
        band = slice(part * half, (part + 1) * half)
        nf_grad = parts[0][band, :].astype(f32)
        for other in parts[1:]:
            nf_grad += other[band, :].astype(f32)
        mid = mid_ref[band, :]
        r = lax.rsqrt(jnp.mean(mid * mid, axis=-1, keepdims=True) + epsilon)
        u = nf_grad * gain_ref[...]
        inner = jnp.mean(u * mid, axis=-1, keepdims=True)
        grad = g_ref[band, :].astype(f32) + r * u - mid * (r * r * r * inner)
        dgain += jnp.sum(nf_grad * mid * r, axis=0, keepdims=True)
        mg_ref[band, :] = grad
        low = grad.astype(bf16)
        mgl_ref[band, :] = low
        att_grad = dot_nt(low, wo_ref[...]).astype(bf16)
        ag_ref[band, :] = att_grad
        delta = jnp.zeros((half, HEAD_SIZE), f32)
        for head in range(QUERY_HEADS):
            span = slice(head * HEAD_SIZE, (head + 1) * HEAD_SIZE)
            one = jnp.sum(att_grad[:, span].astype(f32) * att_ref[band, span], axis=-1, keepdims=True)
            delta = jnp.where(lane == head, one, delta)
        delta_cols[band, :] = delta
    dgain_ref[...] = dgain
    delta_ref[...] = delta_cols[...].T[: delta_ref.shape[0], :]


def middle_backward(parts, mid, g, gain, wo, att):
    rows = mid.shape[0]
    return pl.pallas_call(
        middle_kernel,
        out_shape=(
            jax.ShapeDtypeStruct((rows, MODEL_WIDTH), f32),
            jax.ShapeDtypeStruct((rows, MODEL_WIDTH), bf16),
            jax.ShapeDtypeStruct((rows, MODEL_WIDTH), bf16),
            jax.ShapeDtypeStruct((HEAD_ROWS, rows), f32),
            jax.ShapeDtypeStruct((1, MODEL_WIDTH), f32),
        ),
        scratch_shapes=[pltpu.VMEM((rows, HEAD_SIZE), f32)],
        compiler_params=params(),
        cost_estimate=cost(2 * rows * MODEL_WIDTH * MODEL_WIDTH, 2e7),
        name="middle_backward",
    )(*parts, mid, g, gain, wo, att)


def attention_back_kernel(first, *refs):
    (q_ref, ag_ref, k_ref, v_ref, lse_ref, delta_ref, kpos_ref, qpos_ref) = refs[:8]
    rest = refs[8:]
    if not first:
        dq_in, dkv_in = rest[:2]
        rest = rest[2:]
    dq_ref, dkv_ref, dk_acc, dv_acc = rest
    group, member = pl.program_id(0), pl.program_id(1)
    head = group * GROUP + member
    q, ag, keys, values = q_ref[...], ag_ref[...], k_ref[...], v_ref[...]
    scores = dot_nt(keys, q)
    weights = jnp.exp2(scores * score_to_log2 - lse_ref[pl.ds(head, 1), :])
    weights = jnp.where(kpos_ref[...] <= qpos_ref[...], weights, 0.0)
    weights_grad = dot_nt(values, ag)
    score_grad = (weights * (weights_grad - delta_ref[pl.ds(head, 1), :]) * score_scale).astype(bf16)
    dv = dot(weights.astype(bf16), ag)
    dk = dot(score_grad, q)
    dq = dot_tn(score_grad, keys)
    if not first:
        dq += dq_in[...]
    dq_ref[...] = dq

    @pl.when(member == 0)
    def _():
        dk_acc[...] = dk
        dv_acc[...] = dv

    @pl.when(member != 0)
    def _():
        dk_acc[...] += dk
        dv_acc[...] += dv

    @pl.when(member == GROUP - 1)
    def _():
        for place, total in ((group, dk_acc), (KEY_VALUE_HEADS + group, dv_acc)):
            columns = pl.ds(pl.multiple_of(place * HEAD_SIZE, HEAD_SIZE), HEAD_SIZE)
            value = total[...]
            if not first:
                value += dkv_in[:, columns].astype(f32)
            dkv_ref[:, columns] = value.astype(bf16)


def attention_backward(q, ag, kv, lse, delta, kpos_col, qpos_row, dq, dkv):
    first = dq is None
    rows, keys = q.shape[0], kv.shape[0]
    by_head = pl.BlockSpec((rows, HEAD_SIZE), lambda g, m: (0, g * GROUP + m))
    in_specs = [
        by_head,
        by_head,
        pl.BlockSpec((keys, HEAD_SIZE), lambda g, m: (0, g)),
        pl.BlockSpec((keys, HEAD_SIZE), lambda g, m: (0, KEY_VALUE_HEADS + g)),
        whole((HEAD_ROWS, rows)),
        whole((HEAD_ROWS, rows)),
        whole((keys, 1)),
        whole((1, rows)),
    ]
    args = [q, ag, kv, kv, lse, delta, kpos_col, qpos_row]
    if not first:
        in_specs += [by_head, whole((keys, 2 * KV_WIDTH))]
        args += [dq, dkv]
    return pl.pallas_call(
        functools.partial(attention_back_kernel, first),
        grid=(KEY_VALUE_HEADS, GROUP),
        in_specs=in_specs,
        out_specs=(by_head, whole((keys, 2 * KV_WIDTH))),
        out_shape=(
            jax.ShapeDtypeStruct((rows, MODEL_WIDTH), f32),
            jax.ShapeDtypeStruct((keys, 2 * KV_WIDTH), bf16),
        ),
        scratch_shapes=[pltpu.VMEM((keys, HEAD_SIZE), f32)] * 2,
        compiler_params=params(),
        cost_estimate=cost(10 * rows * keys * MODEL_WIDTH, 1e7, rows * keys * QUERY_HEADS),
        name="attention_backward",
    )(*args)


def unrotate_kernel(dq_ref, cos_ref, sin_ref, out_ref):
    cosine, sine = cos_ref[...], sin_ref[...]
    for head in range(QUERY_HEADS):
        span = slice(head * HEAD_SIZE, (head + 1) * HEAD_SIZE)
        out_ref[:, span] = rotate_back(dq_ref[:, span], cosine, sine).astype(bf16)


def unrotate(dq, cosine, sine):
    return pl.pallas_call(
        unrotate_kernel,
        out_shape=jax.ShapeDtypeStruct(dq.shape, bf16),
        compiler_params=params(),
        cost_estimate=cost(dq.size * 4, dq.size * 6),
        name="unrotate",
    )(dq, cosine, sine)


def input_kernel(
    dql_ref, dkv_ref, wq_ref, wk_ref, wv_ref, cos_ref, sin_ref, x_ref, gain_ref, mg_ref,
    dkvl_ref, dx_ref, dgain_ref,
):
    cosine, sine = cos_ref[...], sin_ref[...]
    for head in range(KEY_VALUE_HEADS):
        span = slice(head * HEAD_SIZE, (head + 1) * HEAD_SIZE)
        dkvl_ref[:, span] = rotate_back(dkv_ref[:, span].astype(f32), cosine, sine).astype(bf16)
    dkvl_ref[:, KV_WIDTH:] = dkv_ref[:, KV_WIDTH:]
    rows = x_ref.shape[0]
    half = rows // 2
    dgain = jnp.zeros((1, MODEL_WIDTH), f32)
    for part in range(2):
        band = slice(part * half, (part + 1) * half)
        grad = dot_nt(dql_ref[band, :], wq_ref[...])
        grad += dot_nt(dkvl_ref[band, :KV_WIDTH], wk_ref[...])
        grad += dot_nt(dkvl_ref[band, KV_WIDTH:], wv_ref[...])
        x = x_ref[band, :].astype(f32)
        r = lax.rsqrt(jnp.mean(x * x, axis=-1, keepdims=True) + epsilon)
        v = grad * gain_ref[...]
        inner = jnp.mean(v * x, axis=-1, keepdims=True)
        dgain += jnp.sum(grad * x * r, axis=0, keepdims=True)
        dx_ref[band, :] = (mg_ref[band, :] + r * v - x * (r * r * r * inner)).astype(bf16)
    dgain_ref[...] = dgain


def input_backward(dql, dkv, wq, wk, wv, cosine, sine, x, gain, mg):
    rows = x.shape[0]
    return pl.pallas_call(
        input_kernel,
        out_shape=(
            jax.ShapeDtypeStruct((rows, 2 * KV_WIDTH), bf16),
            jax.ShapeDtypeStruct((rows, MODEL_WIDTH), bf16),
            jax.ShapeDtypeStruct((1, MODEL_WIDTH), f32),
        ),
        compiler_params=params(),
        cost_estimate=cost(2 * rows * MODEL_WIDTH * (MODEL_WIDTH + 2 * KV_WIDTH), 2e7),
        name="input_backward",
    )(dql, dkv, wq, wk, wv, cosine, sine, x, gain, mg)


def shifted(value, axis, steps):
    count = lax.axis_size(axis)
    return lax.ppermute(value, axis, [(i, (i + steps) % count) for i in range(count)])


def core_swap(value):
    return lax.ppermute(value, "exp", [(i, i ^ 1) for i in range(lax.axis_size("exp"))])


def chip_shift(value, steps):
    count = lax.axis_size("exp")
    return lax.ppermute(value, "exp", [(i, (i + 2 * steps) % count) for i in range(count)])


def gather_blocks(own):
    out = [own, core_swap(own)]
    for steps in range(1, lax.axis_size("exp") // 2):
        same = chip_shift(own, steps)
        out += [core_swap(same), same]
    return out


def return_blocks(parts):
    terms = [parts[0], core_swap(parts[1])]
    for steps in range(1, lax.axis_size("exp") // 2):
        crossed = core_swap(parts[2 * steps])
        both = (crossed.astype(f32) + parts[2 * steps + 1].astype(f32)).astype(bf16)
        terms.append(chip_shift(both, -steps))
    return terms


def ring_scatter(parts, shift, index, count):
    def part(step):
        return lax.dynamic_index_in_dim(parts, (index - 1 - step) % count, 0, keepdims=False)

    total = part(0)
    for step in range(1, count):
        total = (shift(total).astype(f32) + part(step).astype(f32)).astype(bf16)
    return total


def scatter_all(array):
    dp, ctx, exp = (lax.axis_size(a) for a in ("dp", "ctx", "exp"))
    d, c, e = (lax.axis_index(a) for a in ("dp", "ctx", "exp"))
    chips = exp // 2
    rows, columns = array.shape
    share = rows // (dp * ctx * exp)
    parts = array.reshape(dp, ctx, chips, 2, share, columns)
    parts = jnp.transpose(parts, (3, 2, 0, 1, 4, 5))
    parts = ring_scatter(parts, core_swap, e % 2, 2)
    parts = ring_scatter(parts, lambda v: chip_shift(v, 1), e // 2, chips)
    parts = ring_scatter(parts, lambda v: shifted(v, "dp", 1), d, dp)
    return ring_scatter(parts, lambda v: shifted(v, "ctx", 1), c, ctx)


def per_device(
    tokens, attn_gain, w_query, key_matrix, value_matrix, w_out, ffn_gain, expert_gate_up,
    expert_down, expert_ids, gate_weights, span_order, out_grad,
):
    ctx_size, exp_size = lax.axis_size("ctx"), lax.axis_size("exp")
    ctx_here, exp_here = lax.axis_index("ctx"), lax.axis_index("exp")
    experts = EXP_DEV * exp_size
    x, g = tokens[0], out_grad[0]
    rows = x.shape[0]
    capacity = rows * TOPK * 5 // (4 * experts)
    gain_one, gain_two = attn_gain[None, :], ffn_gain[None, :]
    offsets = jnp.arange(HALF, dtype=jnp.int32)

    def device_positions(device):
        pair = lax.dynamic_slice_in_dim(span_order[0], 2 * device, 2, 0)
        return (pair[:, None] * HALF + offsets[None, :]).reshape(-1)

    sources = [(ctx_here - s) % ctx_size for s in range(ctx_size)]
    key_positions = [device_positions(s) for s in sources]
    positions = key_positions[0]
    exponent = jnp.arange(HEAD_SIZE // 2, dtype=f32) * (-2.0 / HEAD_SIZE)
    frequency = jnp.power(f32(rope_base), exponent)
    angles = positions.astype(f32)[:, None] * frequency[None, :]
    cosine, sine = jnp.cos(angles), jnp.sin(angles)
    cosine = jnp.concatenate([cosine, cosine], axis=1)
    sine = jnp.concatenate([-sine, sine], axis=1)

    normed, kv_own = norm_kv(x, gain_one, key_matrix, value_matrix, cosine, sine)
    kv_blocks = [kv_own] + [shifted(kv_own, "ctx", s) for s in range(1, ctx_size)]
    q = query_projection(normed, w_query, cosine, sine)

    named = expert_ids[0][:, :, None] == jnp.arange(experts, dtype=jnp.int32)
    member = jnp.any(named, axis=1)
    count = member.astype(jnp.int32)
    place = jnp.where(member, jnp.cumsum(count, axis=0) - count, -1)
    route_gate = jnp.sum(jnp.where(named, gate_weights[0][:, :, None], 0.0), axis=1)
    routing = jnp.stack([place.astype(f32), route_gate]).transpose(0, 2, 1)
    routing = gather_blocks(routing)

    def local_routing(block):
        pair = lax.dynamic_slice_in_dim(block, EXP_DEV * exp_here, EXP_DEV, 1)
        return pair[0].astype(jnp.int32), pair[1]

    routing = [local_routing(block) for block in routing]
    g_blocks = gather_blocks(g)

    kv_all = jnp.concatenate(kv_blocks, axis=0)
    kpos_row = jnp.concatenate(key_positions)[None, :]
    att, att_low, lse, mid, nf = attention_forward(
        q, kv_all, positions[:, None], kpos_row, w_out, x, gain_two
    )

    nf_blocks = gather_blocks(nf)
    y_parts, dx_parts, kept = [], [], None
    for block in range(exp_size):
        pos, gates = routing[block]
        y_part, dx_part, kept = expert_block(
            block, exp_size, capacity, pos, gates, nf_blocks[block], g_blocks[block],
            expert_gate_up, expert_down, kept,
        )
        y_parts.append(y_part)
        dx_parts.append(dx_part)
    nf_grad_terms = return_blocks(dx_parts)
    slot_rows, hidden, slot_grad, projected_grad = (
        a.reshape(EXP_DEV, exp_size * capacity, a.shape[-1]) for a in kept
    )
    down_grad = jnp.einsum("erf,erd->efd", hidden, slot_grad, preferred_element_type=f32).astype(bf16)
    gate_up_grad = jnp.einsum(
        "erd,erf->edf", slot_rows, projected_grad, preferred_element_type=f32
    ).astype(bf16)
    down_share = lax.psum_scatter(down_grad, ("dp", "ctx"), scatter_dimension=1, tiled=True)
    gate_up_share = lax.psum_scatter(gate_up_grad, ("dp", "ctx"), scatter_dimension=1, tiled=True)

    mid_grad, mid_grad_low, att_grad, delta, ffn_gain_part = middle_backward(
        nf_grad_terms, mid, g, gain_two, w_out, att
    )
    y_terms = return_blocks(y_parts)
    layer_output = mid
    for term in y_terms:
        layer_output = layer_output + term.astype(f32)
    layer_output = layer_output.astype(bf16)
    w_out_grad = dot_tn(att_low, mid_grad_low).astype(bf16)
    w_out_share = scatter_all(w_out_grad)

    dq, dkv = None, None
    for step in range(ctx_size):
        back = (step + 1) % ctx_size
        if step:
            dkv = shifted(dkv, "ctx", 1)
        dq, dkv = attention_backward(
            q, att_grad, kv_blocks[back], lse, delta, key_positions[back][:, None],
            positions[None, :], dq, dkv,
        )
    dql = unrotate(dq, cosine, sine)
    w_query_grad = dot_tn(normed, dql).astype(bf16)
    dkvl, tokens_grad, attn_gain_part = input_backward(
        dql, dkv, w_query, key_matrix, value_matrix, cosine, sine, x, gain_one, mid_grad
    )
    w_kv_grad = dot_tn(normed, dkvl).astype(bf16)
    w_query_share = scatter_all(w_query_grad)
    w_kv_share = scatter_all(w_kv_grad)
    gains = lax.psum_scatter(
        jnp.concatenate([attn_gain_part, ffn_gain_part], axis=0),
        ("dp", "ctx", "exp"), scatter_dimension=1, tiled=True,
    )
    return (
        layer_output[None],
        tokens_grad[None],
        gains[0],
        w_query_share.astype(f32),
        w_kv_share[:, :KV_WIDTH].astype(f32),
        w_kv_share[:, KV_WIDTH:].astype(f32),
        w_out_share.astype(f32),
        gains[1],
        gate_up_share.astype(f32),
        down_share.astype(f32),
    )


def solution(mesh):
    by_row = P(("dp", "exp"), "ctx", None)
    share = P(("dp", "ctx", "exp"))
    share_rows = P(("dp", "ctx", "exp"), None)
    return jax.shard_map(
        per_device,
        mesh=mesh,
        in_specs=(
            by_row, P(), P(), P(), P(), P(), P(), P("exp", None, None), P("exp", None, None),
            by_row, by_row, P(("dp", "exp"), None), by_row,
        ),
        out_specs=(
            by_row, by_row, share, share_rows, share_rows, share_rows, share_rows, share,
            P("exp", ("dp", "ctx"), None), P("exp", ("dp", "ctx"), None),
        ),
        check_vma=False,
    )
```

```python
import functools
import math

import jax
import jax.numpy as jnp
from jax import lax
from jax.experimental import pallas as pl
from jax.experimental.pallas import tpu as pltpu
from jax.sharding import PartitionSpec as P

MODEL_WIDTH = 1536
QUERY_HEADS = 12
KEY_VALUE_HEADS = 2
GROUP = QUERY_HEADS // KEY_VALUE_HEADS
HEAD_SIZE = 128
KV_WIDTH = KEY_VALUE_HEADS * HEAD_SIZE
FF = 768
TOPK = 4
EXP_DEV = 2
TOK_DEV = 512
HALF = 256

epsilon = 1e-06
rope_base = 1000000.0
masked_score = -1e30
score_scale = HEAD_SIZE ** (-0.5)
score_to_log2 = score_scale * math.log2(math.e)
gelu_c = math.sqrt(2.0 / math.pi)

f32 = jnp.float32
bf16 = jnp.bfloat16
NT = (((1,), (1,)), ((), ()))
TN = (((0,), (0,)), ((), ()))
VMEM_BYTES = 60 * 1024 * 1024


def dot(a, b):
    return jnp.dot(a, b, preferred_element_type=f32)


def dot_nt(a, b):
    return lax.dot_general(a, b, NT, preferred_element_type=f32)


def dot_tn(a, b):
    return lax.dot_general(a, b, TN, preferred_element_type=f32)


def params(**more):
    return pltpu.CompilerParams(vmem_limit_bytes=VMEM_BYTES, **more)


def cost(flops, size, exps=0):
    return pl.CostEstimate(flops=int(flops) // 32, bytes_accessed=int(size) // 32, transcendentals=int(exps) // 32)


def whole(shape):
    return pl.BlockSpec(shape, lambda *_: (0,) * len(shape))


def rotate(values, cosine, signed_sine):
    return values * cosine + pltpu.roll(values, HEAD_SIZE // 2, 1) * signed_sine


def rotate_back(values, cosine, signed_sine):
    return values * cosine - pltpu.roll(values, HEAD_SIZE // 2, 1) * signed_sine


def norm_kv_kernel(x_ref, gain_ref, wk_ref, wv_ref, cos_ref, sin_ref, normed_ref, kv_ref):
    x = x_ref[...].astype(f32)
    r = lax.rsqrt(jnp.mean(x * x, axis=-1, keepdims=True) + epsilon)
    normed = (x * r * gain_ref[...]).astype(bf16)
    normed_ref[...] = normed
    keys = dot(normed, wk_ref[...])
    cosine, sine = cos_ref[...], sin_ref[...]
    for head in range(KEY_VALUE_HEADS):
        span = slice(head * HEAD_SIZE, (head + 1) * HEAD_SIZE)
        kv_ref[:, span] = rotate(keys[:, span], cosine, sine).astype(bf16)
    kv_ref[:, KV_WIDTH:] = dot(normed, wv_ref[...]).astype(bf16)


def norm_kv(x, gain, wk, wv, cosine, sine):
    rows = x.shape[0]
    return pl.pallas_call(
        norm_kv_kernel,
        out_shape=(
            jax.ShapeDtypeStruct((rows, MODEL_WIDTH), bf16),
            jax.ShapeDtypeStruct((rows, 2 * KV_WIDTH), bf16),
        ),
        compiler_params=params(),
        cost_estimate=cost(4 * rows * MODEL_WIDTH * KV_WIDTH, 5e6),
        name="norm_kv",
    )(x, gain, wk, wv, cosine, sine)


Q_TILE = 512


def query_kernel(normed_ref, wq_ref, cos_ref, sin_ref, q_ref):
    lin = dot(normed_ref[...], wq_ref[...])
    cosine, sine = cos_ref[...], sin_ref[...]
    for head in range(Q_TILE // HEAD_SIZE):
        span = slice(head * HEAD_SIZE, (head + 1) * HEAD_SIZE)
        q_ref[:, span] = rotate(lin[:, span], cosine, sine).astype(bf16)


def query_projection(normed, wq, cosine, sine):
    rows = normed.shape[0]
    return pl.pallas_call(
        query_kernel,
        grid=(MODEL_WIDTH // Q_TILE,),
        in_specs=[
            whole((rows, MODEL_WIDTH)),
            pl.BlockSpec((MODEL_WIDTH, Q_TILE), lambda t: (0, t)),
            whole((rows, HEAD_SIZE)),
            whole((rows, HEAD_SIZE)),
        ],
        out_specs=pl.BlockSpec((rows, Q_TILE), lambda t: (0, t)),
        out_shape=jax.ShapeDtypeStruct((rows, MODEL_WIDTH), bf16),
        compiler_params=params(),
        cost_estimate=cost(2 * rows * MODEL_WIDTH * MODEL_WIDTH, 8e6),
        name="query_projection",
    )(normed, wq, cosine, sine)


def attention_kernel(
    q_ref, k_ref, v_ref, qpos_ref, kpos_ref, wo_ref, x_ref, gain_ref,
    att_ref, att_low_ref, lse_ref, mid_ref, nf_ref, lse_cols,
):
    head = pl.program_id(0)
    rows = q_ref.shape[0]
    half = rows // 2
    keys, values = k_ref[...], v_ref[...]
    lane = lax.broadcasted_iota(jnp.int32, (half, HEAD_SIZE), 1)
    for part in range(2):
        band = slice(part * half, (part + 1) * half)
        scores = dot_nt(q_ref[band, :], keys)
        scores = jnp.where(kpos_ref[...] <= qpos_ref[band, :], scores, masked_score)
        top = jnp.max(scores, axis=-1, keepdims=True) * score_to_log2
        weights = jnp.exp2(scores * score_to_log2 - top)
        total = jnp.sum(weights, axis=-1, keepdims=True)
        out = dot(weights.astype(bf16), values) / total
        columns = pl.ds(pl.multiple_of(head * HEAD_SIZE, HEAD_SIZE), HEAD_SIZE)
        att_ref[band, columns] = out
        att_low_ref[band, columns] = out.astype(bf16)
        lse = top + jnp.log2(total)
        lse_cols[band, :] = jnp.where(lane == head, lse, lse_cols[band, :])

    @pl.when(head == QUERY_HEADS - 1)
    def _():
        lse_ref[...] = lse_cols[...].T[: lse_ref.shape[0], :]
        for part in range(2):
            band = slice(part * half, (part + 1) * half)
            mid = x_ref[band, :].astype(f32) + dot(att_low_ref[band, :], wo_ref[...])
            mid_ref[band, :] = mid
            r = lax.rsqrt(jnp.mean(mid * mid, axis=-1, keepdims=True) + epsilon)
            nf_ref[band, :] = (mid * r * gain_ref[...]).astype(bf16)


HEAD_ROWS = 16


def attention_forward(q, kv_all, qpos_col, kpos_row, wo, x, gain):
    rows, keys = q.shape[0], kv_all.shape[0]
    return pl.pallas_call(
        attention_kernel,
        grid=(QUERY_HEADS,),
        in_specs=[
            pl.BlockSpec((rows, HEAD_SIZE), lambda h: (0, h)),
            pl.BlockSpec((keys, HEAD_SIZE), lambda h: (0, h // GROUP)),
            pl.BlockSpec((keys, HEAD_SIZE), lambda h: (0, KEY_VALUE_HEADS + h // GROUP)),
            whole((rows, 1)),
            whole((1, keys)),
            whole((MODEL_WIDTH, MODEL_WIDTH)),
            whole((rows, MODEL_WIDTH)),
            whole((1, MODEL_WIDTH)),
        ],
        out_specs=(
            whole((rows, MODEL_WIDTH)),
            whole((rows, MODEL_WIDTH)),
            whole((HEAD_ROWS, rows)),
            whole((rows, MODEL_WIDTH)),
            whole((rows, MODEL_WIDTH)),
        ),
        out_shape=(
            jax.ShapeDtypeStruct((rows, MODEL_WIDTH), f32),
            jax.ShapeDtypeStruct((rows, MODEL_WIDTH), bf16),
            jax.ShapeDtypeStruct((HEAD_ROWS, rows), f32),
            jax.ShapeDtypeStruct((rows, MODEL_WIDTH), f32),
            jax.ShapeDtypeStruct((rows, MODEL_WIDTH), bf16),
        ),
        scratch_shapes=[pltpu.VMEM((rows, HEAD_SIZE), f32)],
        compiler_params=params(),
        cost_estimate=cost(8 * rows * keys * MODEL_WIDTH, 2e7, rows * keys * QUERY_HEADS),
        name="attention_forward",
    )(q, kv_all, kv_all, qpos_col, kpos_row, wo, x, gain)


FF_TILE = 256
WIDTH_TILE = 512


def expert_kernel(count, pos_row_ref, pos_col_ref, gate_row_ref, *refs):
    x_refs, g_refs = refs[:count], refs[count : 2 * count]
    wgu_ref, wd_ref = refs[2 * count : 2 * count + 2]
    rows_ref, hidden_ref, slot_grad_ref, pg_ref, place, result, rows_grad = refs[-7:]
    y_refs, dx_refs = refs[-7 - 2 * count : -7 - count], refs[-7 - count : -7]
    block, expert = pl.program_id(0), pl.program_id(1)
    capacity = rows_ref.shape[-2]
    tokens = x_refs[0].shape[0]
    slot_r = lax.broadcasted_iota(jnp.int32, (capacity, tokens), 0)
    slot_c = lax.broadcasted_iota(jnp.int32, (tokens, capacity), 1)
    match = slot_r == pos_row_ref[0, 0]
    pick = match.astype(bf16)
    place[expert] = (slot_c == pos_col_ref[0, 0]).astype(bf16)
    gates = jnp.sum(jnp.where(match, gate_row_ref[0, 0], 0.0), axis=1, keepdims=True)
    for one in range(count):

        @pl.when(block == one)
        def _():
            for start in range(0, MODEL_WIDTH, WIDTH_TILE):
                span = slice(start, start + WIDTH_TILE)
                rows_ref[0, 0, :, span] = dot(pick, x_refs[one][:, span]).astype(bf16)
                slot_grad_ref[0, 0, :, span] = (dot(pick, g_refs[one][:, span]) * gates).astype(bf16)

    rows = rows_ref[0, 0]
    slot_grad = slot_grad_ref[0, 0]
    for start in range(0, FF, FF_TILE):
        span = slice(start, start + FF_TILE)
        up_span = slice(FF + start, FF + start + FF_TILE)
        gate = dot(rows, wgu_ref[0, :, span])
        up = dot(rows, wgu_ref[0, :, up_span])
        hidden_grad = dot_nt(slot_grad, wd_ref[0, span, :])
        square = gate * gate
        tangent = jnp.tanh(gate * (gelu_c + (gelu_c * 0.044715) * square))
        half_plus = 0.5 + 0.5 * tangent
        activated = gate * half_plus
        slope = half_plus + activated * (1.0 - tangent) * (
            gelu_c + (3.0 * 0.044715 * gelu_c) * square
        )
        hidden_ref[0, 0, :, span] = (activated * up).astype(bf16)
        pg_ref[0, 0, :, span] = (hidden_grad * up * slope).astype(bf16)
        pg_ref[0, 0, :, up_span] = (hidden_grad * activated).astype(bf16)
    hidden = hidden_ref[0, 0]
    projected_grad = pg_ref[0, 0]
    for start in range(0, MODEL_WIDTH, WIDTH_TILE):
        span = slice(start, start + WIDTH_TILE)
        result[expert, :, span] = (dot(hidden, wd_ref[0, :, span]) * gates).astype(bf16)
        rows_grad[expert, :, span] = dot_nt(projected_grad, wgu_ref[0, span, :]).astype(bf16)

    for one in range(count):

        @pl.when((expert == EXP_DEV - 1) & (block == one))
        def _():
            both = jnp.concatenate([place[e] for e in range(EXP_DEV)], axis=1)
            for start in range(0, MODEL_WIDTH, WIDTH_TILE):
                span = slice(start, start + WIDTH_TILE)
                for out_ref, terms in ((y_refs[one], result), (dx_refs[one], rows_grad)):
                    stacked = terms[:, :, span].reshape(EXP_DEV * capacity, WIDTH_TILE)
                    out_ref[:, span] = dot(both, stacked).astype(bf16)


def expert_blocks(first, blocks, capacity, pos, gates, xs, gs, wgu, wd, kept):
    count, tokens = len(xs), xs[0].shape[0]
    kept_shapes = tuple(
        jax.ShapeDtypeStruct((EXP_DEV, blocks, capacity, width), bf16)
        for width in (MODEL_WIDTH, FF, MODEL_WIDTH, 2 * FF)
    )
    kept_specs = tuple(
        pl.BlockSpec((1, 1, capacity, s.shape[-1]), lambda b, e: (e, first + b, 0, 0))
        for s in kept_shapes
    )
    args = [pos[:, :, None, :], pos[:, :, :, None], gates[:, :, None, :], *xs, *gs, wgu, wd]
    aliases = {} if kept is None else {len(args) + i: 2 * count + i for i in range(4)}
    flops = count * EXP_DEV * 2 * capacity * (4 * tokens * MODEL_WIDTH + 9 * MODEL_WIDTH * FF)
    result = jax.ShapeDtypeStruct((tokens, MODEL_WIDTH), bf16)
    once = pl.BlockSpec((tokens, MODEL_WIDTH), lambda b, e: (0, 0), pipeline_mode=pl.Buffered(1))
    out = pl.pallas_call(
        functools.partial(expert_kernel, count),
        grid=(count, EXP_DEV),
        in_specs=[
            pl.BlockSpec((1, 1, 1, tokens), lambda b, e: (b, e, 0, 0)),
            pl.BlockSpec((1, 1, tokens, 1), lambda b, e: (b, e, 0, 0)),
            pl.BlockSpec((1, 1, 1, tokens), lambda b, e: (b, e, 0, 0)),
        ]
        + [once] * (2 * count)
        + [
            pl.BlockSpec((1, MODEL_WIDTH, 2 * FF), lambda b, e: (e, 0, 0)),
            pl.BlockSpec((1, FF, MODEL_WIDTH), lambda b, e: (e, 0, 0)),
        ]
        + [pl.BlockSpec(memory_space=pl.ANY) for _ in aliases],
        out_specs=(once,) * (2 * count) + kept_specs,
        out_shape=(result,) * (2 * count) + kept_shapes,
        scratch_shapes=[
            pltpu.VMEM((EXP_DEV, tokens, capacity), bf16),
            pltpu.VMEM((EXP_DEV, capacity, MODEL_WIDTH), bf16),
            pltpu.VMEM((EXP_DEV, capacity, MODEL_WIDTH), bf16),
        ],
        input_output_aliases=aliases,
        compiler_params=params(),
        cost_estimate=cost(flops, 6e7),
        name="expert_blocks",
    )(*args, *(kept or ()))
    return out[:count], out[count : 2 * count], out[2 * count :]


GRAD_TILE = 384


def weight_grad_kernel(chunk_ref, a_ref, b_ref, out_ref):
    out_ref[0] = dot_tn(a_ref[0], b_ref[0]).astype(bf16)


def weight_grad(first, experts, chunk, size, a, b):
    slots, width = a.shape[1], b.shape[-1]
    tiles = size // GRAD_TILE
    return pl.pallas_call(
        weight_grad_kernel,
        grid_spec=pltpu.PrefetchScalarGridSpec(
            num_scalar_prefetch=1,
            grid=(experts, tiles),
            in_specs=[
                pl.BlockSpec((1, slots, GRAD_TILE), lambda e, t, c: (first + e, 0, c[0] * tiles + t)),
                pl.BlockSpec((1, slots, width), lambda e, t, c: (first + e, 0, 0)),
            ],
            out_specs=pl.BlockSpec((1, GRAD_TILE, width), lambda e, t, c: (e, t, 0)),
        ),
        out_shape=jax.ShapeDtypeStruct((experts, size, width), bf16),
        compiler_params=params(),
        cost_estimate=cost(2 * experts * slots * size * width, 2e7),
        name="weight_grad",
    )(chunk.reshape(1).astype(jnp.int32), a, b)


def middle_kernel(*refs):
    count = len(refs) - 11
    parts = refs[:count]
    mid_ref, g_ref, gain_ref, wo_ref, att_ref = refs[count : count + 5]
    mg_ref, mgl_ref, ag_ref, delta_ref, dgain_ref, delta_cols = refs[count + 5 :]
    rows = mid_ref.shape[0]
    half = rows // 2
    lane = lax.broadcasted_iota(jnp.int32, (half, HEAD_SIZE), 1)
    dgain = jnp.zeros((1, MODEL_WIDTH), f32)
    for part in range(2):
        band = slice(part * half, (part + 1) * half)
        nf_grad = parts[0][band, :].astype(f32)
        for other in parts[1:]:
            nf_grad += other[band, :].astype(f32)
        mid = mid_ref[band, :]
        r = lax.rsqrt(jnp.mean(mid * mid, axis=-1, keepdims=True) + epsilon)
        u = nf_grad * gain_ref[...]
        inner = jnp.mean(u * mid, axis=-1, keepdims=True)
        grad = g_ref[band, :].astype(f32) + r * u - mid * (r * r * r * inner)
        dgain += jnp.sum(nf_grad * mid * r, axis=0, keepdims=True)
        mg_ref[band, :] = grad
        low = grad.astype(bf16)
        mgl_ref[band, :] = low
        att_grad = dot_nt(low, wo_ref[...]).astype(bf16)
        ag_ref[band, :] = att_grad
        delta = jnp.zeros((half, HEAD_SIZE), f32)
        for head in range(QUERY_HEADS):
            span = slice(head * HEAD_SIZE, (head + 1) * HEAD_SIZE)
            one = jnp.sum(att_grad[:, span].astype(f32) * att_ref[band, span], axis=-1, keepdims=True)
            delta = jnp.where(lane == head, one, delta)
        delta_cols[band, :] = delta
    dgain_ref[...] = dgain
    delta_ref[...] = delta_cols[...].T[: delta_ref.shape[0], :]


def middle_backward(parts, mid, g, gain, wo, att):
    rows = mid.shape[0]
    return pl.pallas_call(
        middle_kernel,
        out_shape=(
            jax.ShapeDtypeStruct((rows, MODEL_WIDTH), f32),
            jax.ShapeDtypeStruct((rows, MODEL_WIDTH), bf16),
            jax.ShapeDtypeStruct((rows, MODEL_WIDTH), bf16),
            jax.ShapeDtypeStruct((HEAD_ROWS, rows), f32),
            jax.ShapeDtypeStruct((1, MODEL_WIDTH), f32),
        ),
        scratch_shapes=[pltpu.VMEM((rows, HEAD_SIZE), f32)],
        compiler_params=params(),
        cost_estimate=cost(2 * rows * MODEL_WIDTH * MODEL_WIDTH, 2e7),
        name="middle_backward",
    )(*parts, mid, g, gain, wo, att)


def attention_back_kernel(first, group, *refs):
    (q_ref, ag_ref, k_ref, v_ref, lse_ref, delta_ref, kpos_ref, qpos_ref) = refs[:8]
    rest = refs[8:]
    if not first:
        dq_in, dkv_in = rest[:2]
        rest = rest[2:]
    dq_ref, dkv_ref, dk_acc, dv_acc = rest
    member = pl.program_id(0)
    head = group * GROUP + member
    q, ag, keys, values = q_ref[...], ag_ref[...], k_ref[...], v_ref[...]
    scores = dot_nt(keys, q)
    weights = jnp.exp2(scores * score_to_log2 - lse_ref[pl.ds(head, 1), :])
    weights = jnp.where(kpos_ref[...] <= qpos_ref[...], weights, 0.0)
    weights_grad = dot_nt(values, ag)
    score_grad = (weights * (weights_grad - delta_ref[pl.ds(head, 1), :]) * score_scale).astype(bf16)
    dv = dot(weights.astype(bf16), ag)
    dk = dot(score_grad, q)
    dq = dot_tn(score_grad, keys)
    if not first:
        dq += dq_in[...]
    dq_ref[...] = dq

    @pl.when(member == 0)
    def _():
        dk_acc[...] = dk
        dv_acc[...] = dv

    @pl.when(member != 0)
    def _():
        dk_acc[...] += dk
        dv_acc[...] += dv

    @pl.when(member == GROUP - 1)
    def _():
        for place, total in enumerate((dk_acc, dv_acc)):
            columns = slice(place * HEAD_SIZE, (place + 1) * HEAD_SIZE)
            value = total[...]
            if not first:
                value += dkv_in[:, columns].astype(f32)
            dkv_ref[:, columns] = value.astype(bf16)


def attention_backward(group, q, ag, kv, lse, delta, kpos_col, qpos_row, dq, dkv):
    first = dq is None
    rows, keys = q.shape[0], kv.shape[0]
    by_head = pl.BlockSpec((rows, HEAD_SIZE), lambda m: (0, group * GROUP + m))
    by_member = pl.BlockSpec((rows, HEAD_SIZE), lambda m: (0, m))
    in_specs = [
        by_head,
        by_head,
        pl.BlockSpec((keys, HEAD_SIZE), lambda m: (0, group)),
        pl.BlockSpec((keys, HEAD_SIZE), lambda m: (0, KEY_VALUE_HEADS + group)),
        whole((HEAD_ROWS, rows)),
        whole((HEAD_ROWS, rows)),
        whole((keys, 1)),
        whole((1, rows)),
    ]
    args = [q, ag, kv, kv, lse, delta, kpos_col, qpos_row]
    if not first:
        in_specs += [by_member, whole((keys, 2 * HEAD_SIZE))]
        args += [dq, dkv]
    return pl.pallas_call(
        functools.partial(attention_back_kernel, first, group),
        grid=(GROUP,),
        in_specs=in_specs,
        out_specs=(by_member, whole((keys, 2 * HEAD_SIZE))),
        out_shape=(
            jax.ShapeDtypeStruct((rows, GROUP * HEAD_SIZE), f32),
            jax.ShapeDtypeStruct((keys, 2 * HEAD_SIZE), bf16),
        ),
        scratch_shapes=[pltpu.VMEM((keys, HEAD_SIZE), f32)] * 2,
        compiler_params=params(),
        cost_estimate=cost(5 * rows * keys * MODEL_WIDTH, 1e7, rows * keys * GROUP),
        name="attention_backward",
    )(*args)


def unrotate_kernel(*refs):
    *dq_refs, cos_ref, sin_ref, out_ref = refs
    cosine, sine = cos_ref[...], sin_ref[...]
    for head in range(QUERY_HEADS):
        span = slice(head * HEAD_SIZE, (head + 1) * HEAD_SIZE)
        member = head % GROUP
        source = slice(member * HEAD_SIZE, (member + 1) * HEAD_SIZE)
        out_ref[:, span] = rotate_back(dq_refs[head // GROUP][:, source], cosine, sine).astype(bf16)


def unrotate(dqs, cosine, sine):
    rows = dqs[0].shape[0]
    return pl.pallas_call(
        unrotate_kernel,
        out_shape=jax.ShapeDtypeStruct((rows, MODEL_WIDTH), bf16),
        compiler_params=params(),
        cost_estimate=cost(rows * MODEL_WIDTH * 4, rows * MODEL_WIDTH * 6),
        name="unrotate",
    )(*dqs, cosine, sine)


def input_kernel(
    dql_ref, dkv0_ref, dkv1_ref, wq_ref, wk_ref, wv_ref, cos_ref, sin_ref, x_ref, gain_ref, mg_ref,
    dkvl_ref, dx_ref, dgain_ref,
):
    cosine, sine = cos_ref[...], sin_ref[...]
    for head, dkv_ref in enumerate((dkv0_ref, dkv1_ref)):
        span = slice(head * HEAD_SIZE, (head + 1) * HEAD_SIZE)
        v_span = slice(KV_WIDTH + head * HEAD_SIZE, KV_WIDTH + (head + 1) * HEAD_SIZE)
        key_grad = dkv_ref[:, :HEAD_SIZE].astype(f32)
        dkvl_ref[:, span] = rotate_back(key_grad, cosine, sine).astype(bf16)
        dkvl_ref[:, v_span] = dkv_ref[:, HEAD_SIZE:]
    rows = x_ref.shape[0]
    half = rows // 2
    dgain = jnp.zeros((1, MODEL_WIDTH), f32)
    for part in range(2):
        band = slice(part * half, (part + 1) * half)
        grad = dot_nt(dql_ref[band, :], wq_ref[...])
        grad += dot_nt(dkvl_ref[band, :KV_WIDTH], wk_ref[...])
        grad += dot_nt(dkvl_ref[band, KV_WIDTH:], wv_ref[...])
        x = x_ref[band, :].astype(f32)
        r = lax.rsqrt(jnp.mean(x * x, axis=-1, keepdims=True) + epsilon)
        v = grad * gain_ref[...]
        inner = jnp.mean(v * x, axis=-1, keepdims=True)
        dgain += jnp.sum(grad * x * r, axis=0, keepdims=True)
        dx_ref[band, :] = (mg_ref[band, :] + r * v - x * (r * r * r * inner)).astype(bf16)
    dgain_ref[...] = dgain


def input_backward(dql, dkvs, wq, wk, wv, cosine, sine, x, gain, mg):
    rows = x.shape[0]
    return pl.pallas_call(
        input_kernel,
        out_shape=(
            jax.ShapeDtypeStruct((rows, 2 * KV_WIDTH), bf16),
            jax.ShapeDtypeStruct((rows, MODEL_WIDTH), bf16),
            jax.ShapeDtypeStruct((1, MODEL_WIDTH), f32),
        ),
        compiler_params=params(),
        cost_estimate=cost(2 * rows * MODEL_WIDTH * (MODEL_WIDTH + 2 * KV_WIDTH), 2e7),
        name="input_backward",
    )(dql, *dkvs, wq, wk, wv, cosine, sine, x, gain, mg)


def shifted(value, axis, steps):
    count = lax.axis_size(axis)
    return lax.ppermute(value, axis, [(i, (i + steps) % count) for i in range(count)])


def core_swap(value):
    return lax.ppermute(value, "exp", [(i, i ^ 1) for i in range(lax.axis_size("exp"))])


def chip_shift(value, steps):
    count = lax.axis_size("exp")
    return lax.ppermute(value, "exp", [(i, (i + 2 * steps) % count) for i in range(count)])


def gather_blocks(own):
    swapped = core_swap(own)
    out = [own, swapped]
    own, swapped = tie(own, swapped)
    for steps in range(1, lax.axis_size("exp") // 2):
        same = chip_shift(own, steps)
        out += [core_swap(same), same]
    return out


def return_blocks(parts):
    terms = [parts[0], core_swap(parts[1])]
    for steps in range(1, lax.axis_size("exp") // 2):
        crossed = core_swap(parts[2 * steps])
        both = (crossed.astype(f32) + parts[2 * steps + 1].astype(f32)).astype(bf16)
        terms.append(chip_shift(both, -steps))
    return terms


def ring_part(parts, index, count, step, axis=0):
    return lax.dynamic_index_in_dim(parts, (index - 1 - step) % count, axis, keepdims=False)


def add_low(a, b):
    return (a.astype(f32) + b.astype(f32)).astype(bf16)


def ring_scatter(parts, shift, index, count, axis=0):
    total = ring_part(parts, index, count, 0, axis)
    for step in range(1, count):
        total = add_low(shift(total), ring_part(parts, index, count, step, axis))
    return total


def sum_at_owner(parts, index, count):
    def part(place):
        return lax.dynamic_index_in_dim(parts, place % count, 0, keepdims=False)

    total = part(index).astype(f32)
    for step in range(1, count):
        total += shifted(part(index + step), "ctx", step).astype(f32)
    return total


def scatter_core(array):
    dp, ctx, exp = (lax.axis_size(a) for a in ("dp", "ctx", "exp"))
    rows, columns = array.shape
    parts = array.reshape(dp, ctx, exp // 2, 2, rows // (dp * ctx * exp), columns)
    parts = jnp.transpose(parts, (3, 2, 0, 1, 4, 5))
    return ring_scatter(parts, core_swap, lax.axis_index("exp") % 2, 2)


def scatter_chip(parts):
    return ring_scatter(
        parts, lambda v: chip_shift(v, 1), lax.axis_index("exp") // 2, lax.axis_size("exp") // 2
    )


def scatter_axis(parts, axis):
    return ring_scatter(
        parts, lambda v: shifted(v, axis, 1), lax.axis_index(axis), lax.axis_size(axis)
    )


def tie(*values):
    return lax.optimization_barrier(values)


def per_device(
    tokens, attn_gain, w_query, key_matrix, value_matrix, w_out, ffn_gain, expert_gate_up,
    expert_down, expert_ids, gate_weights, span_order, out_grad,
):
    ctx_size, exp_size = lax.axis_size("ctx"), lax.axis_size("exp")
    ctx_here, exp_here = lax.axis_index("ctx"), lax.axis_index("exp")
    experts = EXP_DEV * exp_size
    x, g = tokens[0], out_grad[0]
    rows = x.shape[0]
    capacity = rows * TOPK * 5 // (4 * experts)
    gain_one, gain_two = attn_gain[None, :], ffn_gain[None, :]
    offsets = jnp.arange(HALF, dtype=jnp.int32)

    def device_positions(device):
        pair = lax.dynamic_slice_in_dim(span_order[0], 2 * device, 2, 0)
        return (pair[:, None] * HALF + offsets[None, :]).reshape(-1)

    sources = [(ctx_here - s) % ctx_size for s in range(ctx_size)]
    key_positions = [device_positions(s) for s in sources]
    positions = key_positions[0]
    exponent = jnp.arange(HEAD_SIZE // 2, dtype=f32) * (-2.0 / HEAD_SIZE)
    frequency = jnp.power(f32(rope_base), exponent)
    angles = positions.astype(f32)[:, None] * frequency[None, :]
    cosine, sine = jnp.cos(angles), jnp.sin(angles)
    cosine = jnp.concatenate([cosine, cosine], axis=1)
    sine = jnp.concatenate([-sine, sine], axis=1)

    normed, kv_own = norm_kv(x, gain_one, key_matrix, value_matrix, cosine, sine)
    kv_blocks = [kv_own] + [shifted(kv_own, "ctx", s) for s in range(1, ctx_size)]
    q = query_projection(normed, w_query, cosine, sine)

    named = expert_ids[0][:, :, None] == jnp.arange(experts, dtype=jnp.int32)
    member = jnp.any(named, axis=1)
    count = member.astype(jnp.int32)
    place = jnp.where(member, jnp.cumsum(count, axis=0) - count, -1)
    route_gate = jnp.sum(jnp.where(named, gate_weights[0][:, :, None], 0.0), axis=1)
    routing = jnp.stack([place.astype(f32), route_gate]).transpose(0, 2, 1)
    routing = gather_blocks(routing)

    def local_routing(block):
        pair = lax.dynamic_slice_in_dim(block, EXP_DEV * exp_here, EXP_DEV, 1)
        return pair[0].astype(jnp.int32), pair[1]

    routing = [local_routing(block) for block in routing]
    pos = jnp.stack([r[0] for r in routing])
    gates = jnp.stack([r[1] for r in routing])
    g_blocks = gather_blocks(g)

    kv_all = jnp.concatenate(kv_blocks, axis=0)
    kv_all, pos, gates, g_blocks = tie(kv_all, pos, gates, g_blocks)
    kpos_row = jnp.concatenate(key_positions)[None, :]
    att, att_low, lse, mid, nf = attention_forward(
        q, kv_all, positions[:, None], kpos_row, w_out, x, gain_two
    )

    swapped = core_swap(nf)
    nf_blocks = [nf, swapped]
    nf, swapped = tie(nf, swapped)
    y_parts, dx_parts, kept = [], [], None
    for first in range(0, exp_size, 2):
        here = slice(first, first + 2)
        if first:
            same, dx_parts[-1] = tie(chip_shift(nf, first // 2), dx_parts[-1])
            nf_blocks += [core_swap(same), same]
        y_part, dx_part, kept = expert_blocks(
            first, exp_size, capacity, pos[here], gates[here], nf_blocks[here], g_blocks[here],
            expert_gate_up, expert_down, kept,
        )
        y_parts += y_part
        dx_parts += dx_part
    nf_grad_terms = return_blocks(dx_parts)
    slot_rows, hidden, slot_grad, projected_grad = (
        a.reshape(EXP_DEV, exp_size * capacity, a.shape[-1]) for a in kept
    )
    dp_size, dp_here = lax.axis_size("dp"), lax.axis_index("dp")
    gate_up_parts = [
        [
            weight_grad(
                e, 1, (dp_here - 1 - step) % dp_size, MODEL_WIDTH // dp_size, slot_rows,
                projected_grad,
            )
            for e in range(EXP_DEV)
        ]
        for step in range(dp_size)
    ]
    down_grad = weight_grad(0, EXP_DEV, jnp.int32(0), FF, hidden, slot_grad)

    def over_dp(expert):
        total = gate_up_parts[0][expert]
        for step in range(1, dp_size):
            total = shifted(total, "dp", 1).astype(f32) + gate_up_parts[step][expert].astype(f32)
            total = total.astype(bf16)
        return total[0].reshape(ctx_size, -1, 2 * FF)

    nf_grad_terms, down_grad, gate_up_parts, y_parts = tie(
        nf_grad_terms, down_grad, gate_up_parts, y_parts
    )

    mid_grad, mid_grad_low, att_grad, delta, ffn_gain_part = middle_backward(
        nf_grad_terms, mid, g, gain_two, w_out, att
    )
    w_out_grad = dot_tn(att_low, mid_grad_low).astype(bf16)
    att_grad, w_out_grad = tie(att_grad, w_out_grad)
    w_out_part = scatter_core(w_out_grad)
    y_terms = return_blocks(y_parts)
    down_parts = down_grad.reshape(EXP_DEV, dp_size, ctx_size, -1, MODEL_WIDTH)
    down_total = ring_part(down_parts, ctx_here, ctx_size, 0, 2)

    dqs, dkvs = [None] * KEY_VALUE_HEADS, [None] * KEY_VALUE_HEADS
    gate_up_totals = [None] * EXP_DEV
    for step in range(ctx_size):
        back = (step + 1) % ctx_size
        for group in range(KEY_VALUE_HEADS):
            dkv = shifted(dkvs[group], "ctx", 1) if step else None
            ag, other = tie(att_grad, dqs[group - 1]) if step + group else (att_grad, None)
            if other is not None:
                dqs[group - 1] = other
            dqs[group], dkvs[group] = attention_backward(
                group, q, ag, kv_blocks[back], lse, delta, key_positions[back][:, None],
                positions[None, :], dqs[group], dkv,
            )
        if step < ctx_size - 1:
            down_total = add_low(
                shifted(down_total, "ctx", 1), ring_part(down_parts, ctx_here, ctx_size, step + 1, 2)
            )
            att_grad, down_total = tie(att_grad, down_total)
        if step == 0:
            att_grad, w_out_part, gate_up_totals[0] = tie(att_grad, w_out_part, over_dp(0))
            w_out_part = scatter_chip(w_out_part)
        if step == 1:
            att_grad, y_terms = tie(att_grad, y_terms)
        if step == 2:
            att_grad, w_out_part = tie(att_grad, w_out_part)
    down_share = ring_scatter(
        down_total, lambda v: shifted(v, "dp", 1), dp_here, dp_size, 1
    )
    gate_up_totals[1] = over_dp(1)
    layer_output = mid
    for term in y_terms:
        layer_output = layer_output + term.astype(f32)
    layer_output = layer_output.astype(bf16)
    dql = unrotate(dqs, cosine, sine)
    w_query_grad = dot_tn(normed, dql).astype(bf16)
    dql, w_query_grad, gate_up_totals = tie(dql, w_query_grad, gate_up_totals)
    w_query_part = scatter_core(w_query_grad)
    dkvl, tokens_grad, attn_gain_part = input_backward(
        dql, dkvs, w_query, key_matrix, value_matrix, cosine, sine, x, gain_one, mid_grad
    )
    w_kv_grad = dot_tn(normed, dkvl)
    gains = jnp.concatenate([attn_gain_part, ffn_gain_part], axis=0).T
    gains = jnp.pad(gains, ((0, 0), (0, HEAD_SIZE - 2)))
    w_kv_grad = jnp.concatenate([w_kv_grad, gains], axis=1).astype(bf16)
    gate_up_share = jnp.stack(
        [sum_at_owner(total, ctx_here, ctx_size) for total in gate_up_totals]
    )
    w_out_share = scatter_axis(scatter_axis(w_out_part, "dp"), "ctx")
    w_query_share = scatter_axis(scatter_axis(scatter_chip(w_query_part), "dp"), "ctx")
    w_kv_share = scatter_axis(scatter_axis(scatter_chip(scatter_core(w_kv_grad)), "dp"), "ctx")
    w_kv_share = w_kv_share.astype(f32)
    return (
        layer_output[None],
        tokens_grad[None],
        w_kv_share[:, 2 * KV_WIDTH],
        w_query_share.astype(f32),
        w_kv_share[:, :KV_WIDTH],
        w_kv_share[:, KV_WIDTH : 2 * KV_WIDTH],
        w_out_share.astype(f32),
        w_kv_share[:, 2 * KV_WIDTH + 1],
        gate_up_share,
        down_share.astype(f32),
    )


def solution(mesh):
    by_row = P(("dp", "exp"), "ctx", None)
    share = P(("dp", "ctx", "exp"))
    share_rows = P(("dp", "ctx", "exp"), None)
    return jax.shard_map(
        per_device,
        mesh=mesh,
        in_specs=(
            by_row, P(), P(), P(), P(), P(), P(), P("exp", None, None), P("exp", None, None),
            by_row, by_row, P(("dp", "exp"), None), by_row,
        ),
        out_specs=(
            by_row, by_row, share, share_rows, share_rows, share_rows, share_rows, share,
            P("exp", ("dp", "ctx"), None), P("exp", ("dp", "ctx"), None),
        ),
        check_vma=False,
    )
```

```python
import functools
import math

import jax
import jax.numpy as jnp
from jax import lax
from jax.experimental import pallas as pl
from jax.experimental.pallas import tpu as pltpu
from jax.sharding import PartitionSpec as P

MODEL_WIDTH = 1536
QUERY_HEADS = 12
KEY_VALUE_HEADS = 2
GROUP = QUERY_HEADS // KEY_VALUE_HEADS
HEAD_SIZE = 128
KV_WIDTH = KEY_VALUE_HEADS * HEAD_SIZE
FF = 768
TOPK = 4
EXP_DEV = 2
TOK_DEV = 512
HALF = 256

epsilon = 1e-06
rope_base = 1000000.0
masked_score = -1e30
score_scale = HEAD_SIZE ** (-0.5)
score_to_log2 = score_scale * math.log2(math.e)
gelu_c = math.sqrt(2.0 / math.pi)

f32 = jnp.float32
bf16 = jnp.bfloat16
NT = (((1,), (1,)), ((), ()))
TN = (((0,), (0,)), ((), ()))
VMEM_BYTES = 60 * 1024 * 1024
MESH = pl.DeviceIdType.MESH


def dot(a, b):
    return jnp.dot(a, b, preferred_element_type=f32)


def dot_nt(a, b):
    return lax.dot_general(a, b, NT, preferred_element_type=f32)


def dot_tn(a, b):
    return lax.dot_general(a, b, TN, preferred_element_type=f32)


def params(**more):
    return pltpu.CompilerParams(vmem_limit_bytes=VMEM_BYTES, **more)


def cost(flops, size, exps=0):
    return pl.CostEstimate(flops=int(flops) // 32, bytes_accessed=int(size) // 32, transcendentals=int(exps) // 32)


def whole(shape):
    return pl.BlockSpec(shape, lambda *_: (0,) * len(shape))


def rotate(values, cosine, signed_sine):
    return values * cosine + pltpu.roll(values, HEAD_SIZE // 2, 1) * signed_sine


def rotate_back(values, cosine, signed_sine):
    return values * cosine - pltpu.roll(values, HEAD_SIZE // 2, 1) * signed_sine


def norm_kv_kernel(x_ref, gain_ref, wk_ref, wv_ref, cos_ref, sin_ref, normed_ref, kv_ref):
    x = x_ref[...].astype(f32)
    r = lax.rsqrt(jnp.mean(x * x, axis=-1, keepdims=True) + epsilon)
    normed = (x * r * gain_ref[...]).astype(bf16)
    normed_ref[...] = normed
    keys = dot(normed, wk_ref[...])
    cosine, sine = cos_ref[...], sin_ref[...]
    for head in range(KEY_VALUE_HEADS):
        span = slice(head * HEAD_SIZE, (head + 1) * HEAD_SIZE)
        kv_ref[:, span] = rotate(keys[:, span], cosine, sine).astype(bf16)
    kv_ref[:, KV_WIDTH:] = dot(normed, wv_ref[...]).astype(bf16)


def norm_kv(x, gain, wk, wv, cosine, sine):
    rows = x.shape[0]
    return pl.pallas_call(
        norm_kv_kernel,
        out_shape=(
            jax.ShapeDtypeStruct((rows, MODEL_WIDTH), bf16),
            jax.ShapeDtypeStruct((rows, 2 * KV_WIDTH), bf16),
        ),
        compiler_params=params(),
        cost_estimate=cost(4 * rows * MODEL_WIDTH * KV_WIDTH, 5e6),
        name="norm_kv",
    )(x, gain, wk, wv, cosine, sine)


Q_TILE = 512


def query_kernel(normed_ref, wq_ref, cos_ref, sin_ref, q_ref):
    lin = dot(normed_ref[...], wq_ref[...])
    cosine, sine = cos_ref[...], sin_ref[...]
    for head in range(Q_TILE // HEAD_SIZE):
        span = slice(head * HEAD_SIZE, (head + 1) * HEAD_SIZE)
        q_ref[:, span] = rotate(lin[:, span], cosine, sine).astype(bf16)


def query_projection(normed, wq, cosine, sine):
    rows = normed.shape[0]
    return pl.pallas_call(
        query_kernel,
        grid=(MODEL_WIDTH // Q_TILE,),
        in_specs=[
            whole((rows, MODEL_WIDTH)),
            pl.BlockSpec((MODEL_WIDTH, Q_TILE), lambda t: (0, t)),
            whole((rows, HEAD_SIZE)),
            whole((rows, HEAD_SIZE)),
        ],
        out_specs=pl.BlockSpec((rows, Q_TILE), lambda t: (0, t)),
        out_shape=jax.ShapeDtypeStruct((rows, MODEL_WIDTH), bf16),
        compiler_params=params(),
        cost_estimate=cost(2 * rows * MODEL_WIDTH * MODEL_WIDTH, 8e6),
        name="query_projection",
    )(normed, wq, cosine, sine)


def attention_kernel(
    q_ref, k_ref, v_ref, qpos_ref, kpos_ref, wo_ref, x_ref, gain_ref,
    att_ref, att_low_ref, lse_ref, mid_ref, nf_ref, lse_cols,
):
    head = pl.program_id(0)
    rows = q_ref.shape[0]
    half = rows // 2
    keys, values = k_ref[...], v_ref[...]
    lane = lax.broadcasted_iota(jnp.int32, (half, HEAD_SIZE), 1)
    for part in range(2):
        band = slice(part * half, (part + 1) * half)
        scores = dot_nt(q_ref[band, :], keys)
        scores = jnp.where(kpos_ref[...] <= qpos_ref[band, :], scores, masked_score)
        top = jnp.max(scores, axis=-1, keepdims=True) * score_to_log2
        weights = jnp.exp2(scores * score_to_log2 - top)
        total = jnp.sum(weights, axis=-1, keepdims=True)
        out = dot(weights.astype(bf16), values) / total
        columns = pl.ds(pl.multiple_of(head * HEAD_SIZE, HEAD_SIZE), HEAD_SIZE)
        att_ref[band, columns] = out
        att_low_ref[band, columns] = out.astype(bf16)
        lse = top + jnp.log2(total)
        lse_cols[band, :] = jnp.where(lane == head, lse, lse_cols[band, :])

    @pl.when(head == QUERY_HEADS - 1)
    def _():
        lse_ref[...] = lse_cols[...].T[: lse_ref.shape[0], :]
        for part in range(2):
            band = slice(part * half, (part + 1) * half)
            mid = x_ref[band, :].astype(f32) + dot(att_low_ref[band, :], wo_ref[...])
            mid_ref[band, :] = mid
            r = lax.rsqrt(jnp.mean(mid * mid, axis=-1, keepdims=True) + epsilon)
            nf_ref[band, :] = (mid * r * gain_ref[...]).astype(bf16)


HEAD_ROWS = 16


def attention_forward(q, kv_all, qpos_col, kpos_row, wo, x, gain):
    rows, keys = q.shape[0], kv_all.shape[0]
    return pl.pallas_call(
        attention_kernel,
        grid=(QUERY_HEADS,),
        in_specs=[
            pl.BlockSpec((rows, HEAD_SIZE), lambda h: (0, h)),
            pl.BlockSpec((keys, HEAD_SIZE), lambda h: (0, h // GROUP)),
            pl.BlockSpec((keys, HEAD_SIZE), lambda h: (0, KEY_VALUE_HEADS + h // GROUP)),
            whole((rows, 1)),
            whole((1, keys)),
            whole((MODEL_WIDTH, MODEL_WIDTH)),
            whole((rows, MODEL_WIDTH)),
            whole((1, MODEL_WIDTH)),
        ],
        out_specs=(
            whole((rows, MODEL_WIDTH)),
            whole((rows, MODEL_WIDTH)),
            whole((HEAD_ROWS, rows)),
            whole((rows, MODEL_WIDTH)),
            whole((rows, MODEL_WIDTH)),
        ),
        out_shape=(
            jax.ShapeDtypeStruct((rows, MODEL_WIDTH), f32),
            jax.ShapeDtypeStruct((rows, MODEL_WIDTH), bf16),
            jax.ShapeDtypeStruct((HEAD_ROWS, rows), f32),
            jax.ShapeDtypeStruct((rows, MODEL_WIDTH), f32),
            jax.ShapeDtypeStruct((rows, MODEL_WIDTH), bf16),
        ),
        scratch_shapes=[pltpu.VMEM((rows, HEAD_SIZE), f32)],
        compiler_params=params(),
        cost_estimate=cost(8 * rows * keys * MODEL_WIDTH, 2e7, rows * keys * QUERY_HEADS),
        name="attention_forward",
    )(q, kv_all, kv_all, qpos_col, kpos_row, wo, x, gain)


FF_TILE = 256
WIDTH_TILE = 512


def expert_kernel(count, pos_row_ref, pos_col_ref, gate_row_ref, *refs):
    x_refs, g_refs = refs[:count], refs[count : 2 * count]
    wgu_ref, wd_ref = refs[2 * count : 2 * count + 2]
    rows_ref, hidden_ref, slot_grad_ref, pg_ref, place, result, rows_grad = refs[-7:]
    y_refs, dx_refs = refs[-7 - 2 * count : -7 - count], refs[-7 - count : -7]
    block, expert = pl.program_id(0), pl.program_id(1)
    capacity = rows_ref.shape[-2]
    tokens = x_refs[0].shape[0]
    slot_r = lax.broadcasted_iota(jnp.int32, (capacity, tokens), 0)
    slot_c = lax.broadcasted_iota(jnp.int32, (tokens, capacity), 1)
    match = slot_r == pos_row_ref[0, 0]
    pick = match.astype(bf16)
    place[expert] = (slot_c == pos_col_ref[0, 0]).astype(bf16)
    gates = jnp.sum(jnp.where(match, gate_row_ref[0, 0], 0.0), axis=1, keepdims=True)
    for one in range(count):

        @pl.when(block == one)
        def _():
            for start in range(0, MODEL_WIDTH, WIDTH_TILE):
                span = slice(start, start + WIDTH_TILE)
                rows_ref[0, 0, :, span] = dot(pick, x_refs[one][:, span]).astype(bf16)
                slot_grad_ref[0, 0, :, span] = (dot(pick, g_refs[one][:, span]) * gates).astype(bf16)

    rows = rows_ref[0, 0]
    slot_grad = slot_grad_ref[0, 0]
    for start in range(0, FF, FF_TILE):
        span = slice(start, start + FF_TILE)
        up_span = slice(FF + start, FF + start + FF_TILE)
        gate = dot(rows, wgu_ref[0, :, span])
        up = dot(rows, wgu_ref[0, :, up_span])
        hidden_grad = dot_nt(slot_grad, wd_ref[0, span, :])
        square = gate * gate
        tangent = jnp.tanh(gate * (gelu_c + (gelu_c * 0.044715) * square))
        half_plus = 0.5 + 0.5 * tangent
        activated = gate * half_plus
        slope = half_plus + activated * (1.0 - tangent) * (
            gelu_c + (3.0 * 0.044715 * gelu_c) * square
        )
        hidden_ref[0, 0, :, span] = (activated * up).astype(bf16)
        pg_ref[0, 0, :, span] = (hidden_grad * up * slope).astype(bf16)
        pg_ref[0, 0, :, up_span] = (hidden_grad * activated).astype(bf16)
    hidden = hidden_ref[0, 0]
    projected_grad = pg_ref[0, 0]
    for start in range(0, MODEL_WIDTH, WIDTH_TILE):
        span = slice(start, start + WIDTH_TILE)
        result[expert, :, span] = (dot(hidden, wd_ref[0, :, span]) * gates).astype(bf16)
        rows_grad[expert, :, span] = dot_nt(projected_grad, wgu_ref[0, span, :]).astype(bf16)

    for one in range(count):

        @pl.when((expert == EXP_DEV - 1) & (block == one))
        def _():
            both = jnp.concatenate([place[e] for e in range(EXP_DEV)], axis=1)
            for start in range(0, MODEL_WIDTH, WIDTH_TILE):
                span = slice(start, start + WIDTH_TILE)
                for out_ref, terms in ((y_refs[one], result), (dx_refs[one], rows_grad)):
                    stacked = terms[:, :, span].reshape(EXP_DEV * capacity, WIDTH_TILE)
                    out_ref[:, span] = dot(both, stacked).astype(bf16)


def expert_blocks(first, blocks, capacity, pos, gates, xs, gs, wgu, wd, kept):
    count, tokens = len(xs), xs[0].shape[0]
    kept_shapes = tuple(
        jax.ShapeDtypeStruct((EXP_DEV, blocks, capacity, width), bf16)
        for width in (MODEL_WIDTH, FF, MODEL_WIDTH, 2 * FF)
    )
    kept_specs = tuple(
        pl.BlockSpec((1, 1, capacity, s.shape[-1]), lambda b, e: (e, first + b, 0, 0))
        for s in kept_shapes
    )
    args = [pos[:, :, None, :], pos[:, :, :, None], gates[:, :, None, :], *xs, *gs, wgu, wd]
    aliases = {} if kept is None else {len(args) + i: 2 * count + i for i in range(4)}
    flops = count * EXP_DEV * 2 * capacity * (4 * tokens * MODEL_WIDTH + 9 * MODEL_WIDTH * FF)
    result = jax.ShapeDtypeStruct((tokens, MODEL_WIDTH), bf16)
    once = pl.BlockSpec((tokens, MODEL_WIDTH), lambda b, e: (0, 0), pipeline_mode=pl.Buffered(1))
    out = pl.pallas_call(
        functools.partial(expert_kernel, count),
        grid=(count, EXP_DEV),
        in_specs=[
            pl.BlockSpec((1, 1, 1, tokens), lambda b, e: (b, e, 0, 0)),
            pl.BlockSpec((1, 1, tokens, 1), lambda b, e: (b, e, 0, 0)),
            pl.BlockSpec((1, 1, 1, tokens), lambda b, e: (b, e, 0, 0)),
        ]
        + [once] * (2 * count)
        + [
            pl.BlockSpec((1, MODEL_WIDTH, 2 * FF), lambda b, e: (e, 0, 0)),
            pl.BlockSpec((1, FF, MODEL_WIDTH), lambda b, e: (e, 0, 0)),
        ]
        + [pl.BlockSpec(memory_space=pl.ANY) for _ in aliases],
        out_specs=(once,) * (2 * count) + kept_specs,
        out_shape=(result,) * (2 * count) + kept_shapes,
        scratch_shapes=[
            pltpu.VMEM((EXP_DEV, tokens, capacity), bf16),
            pltpu.VMEM((EXP_DEV, capacity, MODEL_WIDTH), bf16),
            pltpu.VMEM((EXP_DEV, capacity, MODEL_WIDTH), bf16),
        ],
        input_output_aliases=aliases,
        compiler_params=params(),
        cost_estimate=cost(flops, 6e7),
        name="expert_blocks",
    )(*args, *(kept or ()))
    return out[:count], out[count : 2 * count], out[2 * count :]


GRAD_TILE = 384


def weight_grad_kernel(chunk_ref, a_ref, b_ref, out_ref):
    out_ref[0] = dot_tn(a_ref[0], b_ref[0]).astype(bf16)


def weight_grad(first, experts, chunk, size, a, b):
    slots, width = a.shape[1], b.shape[-1]
    tiles = size // GRAD_TILE
    return pl.pallas_call(
        weight_grad_kernel,
        grid_spec=pltpu.PrefetchScalarGridSpec(
            num_scalar_prefetch=1,
            grid=(experts, tiles),
            in_specs=[
                pl.BlockSpec((1, slots, GRAD_TILE), lambda e, t, c: (first + e, 0, c[0] * tiles + t)),
                pl.BlockSpec((1, slots, width), lambda e, t, c: (first + e, 0, 0)),
            ],
            out_specs=pl.BlockSpec((1, GRAD_TILE, width), lambda e, t, c: (e, t, 0)),
        ),
        out_shape=jax.ShapeDtypeStruct((experts, size, width), bf16),
        compiler_params=params(),
        cost_estimate=cost(2 * experts * slots * size * width, 2e7),
        name="weight_grad",
    )(chunk.reshape(1).astype(jnp.int32), a, b)


def middle_kernel(*refs):
    count = len(refs) - 11
    parts = refs[:count]
    mid_ref, g_ref, gain_ref, wo_ref, att_ref = refs[count : count + 5]
    mg_ref, mgl_ref, ag_ref, delta_ref, dgain_ref, delta_cols = refs[count + 5 :]
    rows = mid_ref.shape[0]
    half = rows // 2
    lane = lax.broadcasted_iota(jnp.int32, (half, HEAD_SIZE), 1)
    dgain = jnp.zeros((1, MODEL_WIDTH), f32)
    for part in range(2):
        band = slice(part * half, (part + 1) * half)
        nf_grad = parts[0][band, :].astype(f32)
        for other in parts[1:]:
            nf_grad += other[band, :].astype(f32)
        mid = mid_ref[band, :]
        r = lax.rsqrt(jnp.mean(mid * mid, axis=-1, keepdims=True) + epsilon)
        u = nf_grad * gain_ref[...]
        inner = jnp.mean(u * mid, axis=-1, keepdims=True)
        grad = g_ref[band, :].astype(f32) + r * u - mid * (r * r * r * inner)
        dgain += jnp.sum(nf_grad * mid * r, axis=0, keepdims=True)
        mg_ref[band, :] = grad
        low = grad.astype(bf16)
        mgl_ref[band, :] = low
        att_grad = dot_nt(low, wo_ref[...]).astype(bf16)
        ag_ref[band, :] = att_grad
        delta = jnp.zeros((half, HEAD_SIZE), f32)
        for head in range(QUERY_HEADS):
            span = slice(head * HEAD_SIZE, (head + 1) * HEAD_SIZE)
            one = jnp.sum(att_grad[:, span].astype(f32) * att_ref[band, span], axis=-1, keepdims=True)
            delta = jnp.where(lane == head, one, delta)
        delta_cols[band, :] = delta
    dgain_ref[...] = dgain
    delta_ref[...] = delta_cols[...].T[: delta_ref.shape[0], :]


def middle_backward(parts, mid, g, gain, wo, att):
    rows = mid.shape[0]
    return pl.pallas_call(
        middle_kernel,
        out_shape=(
            jax.ShapeDtypeStruct((rows, MODEL_WIDTH), f32),
            jax.ShapeDtypeStruct((rows, MODEL_WIDTH), bf16),
            jax.ShapeDtypeStruct((rows, MODEL_WIDTH), bf16),
            jax.ShapeDtypeStruct((HEAD_ROWS, rows), f32),
            jax.ShapeDtypeStruct((1, MODEL_WIDTH), f32),
        ),
        scratch_shapes=[pltpu.VMEM((rows, HEAD_SIZE), f32)],
        compiler_params=params(),
        cost_estimate=cost(2 * rows * MODEL_WIDTH * MODEL_WIDTH, 2e7),
        name="middle_backward",
    )(*parts, mid, g, gain, wo, att)


def signal_and_wait(neighbours):
    barrier = pltpu.get_barrier_semaphore()
    for neighbour in neighbours:
        pl.semaphore_signal(barrier, inc=1, device_id=neighbour, device_id_type=MESH)
    pl.semaphore_wait(barrier, len(neighbours))


def remote(source, target, send_sem, recv_sem, device):
    return pltpu.make_async_remote_copy(
        src_ref=source, dst_ref=target, send_sem=send_sem, recv_sem=recv_sem,
        device_id=device, device_id_type=MESH,
    )


class Axis:
    def __init__(self, name):
        if name in ("dp", "ctx"):
            self.count, self.me = lax.axis_size(name), lax.axis_index(name)
            place = lambda i: {name: i}
        else:
            exp = lax.axis_index("exp")
            core, chip = lax.rem(exp, 2), exp // 2
            if name == "core":
                self.count, self.me = 2, core
                place = lambda i: {"exp": chip * 2 + i}
            else:
                self.count, self.me = lax.axis_size("exp") // 2, chip
                place = lambda i: {"exp": i * 2 + core}
        self.next = place(lax.rem(self.me + 1, self.count))
        self.last = place(lax.rem(self.me + self.count - 1, self.count))

    def neighbours(self):
        return [self.next] if self.count == 2 else [self.next, self.last]


class Ring:
    def __init__(self, axis, terms, rows, send, recv, send_sem, recv_sem):
        self.axis, self.count, self.terms, self.rows = axis, axis.count, terms, rows
        self.send, self.recv, self.send_sem, self.recv_sem = send, recv, send_sem, recv_sem

    def here(self, hop):
        part = lax.rem(self.axis.me + self.count - 1 - hop, self.count)
        return pl.ds(pl.multiple_of(part * self.rows, self.rows), self.rows)

    def copy(self, hop):
        if len(self.terms) > 1:
            source = self.send.at[hop]
        elif hop == 0:
            source = self.terms[0].at[self.here(0), :]
        else:
            source = self.send.at[hop - 1]
        return remote(
            source, self.recv.at[hop], self.send_sem.at[hop], self.recv_sem.at[hop], self.axis.next
        )

    def hop(self, hop):
        if hop == 0 and len(self.terms) == 1:
            self.copy(0).start()
            return None
        here = self.here(hop)
        total = self.terms[0][here, :].astype(f32)
        for term in self.terms[1:]:
            total += term[here, :].astype(f32)
        if hop:
            self.copy(hop - 1).wait_recv()
            total += self.recv[hop - 1].astype(f32)
        if hop < self.count - 1:
            self.send[hop - (len(self.terms) == 1)] = total.astype(bf16)
            self.copy(hop).start()
        return total

    def finish(self):
        for hop in range(self.count - 1):
            self.copy(hop).wait_send()


def attention_back_kernel(
    n, q_ref, ag_ref, lse_ref, delta_ref, kpos_ref, qpos_ref, cos_ref, sin_ref, mine_ref, came_ref,
    next_ref, *refs,
):
    kv_refs = refs[:n]
    dql_ref, dkv_ref, share_ref, next_came_ref = refs[n : n + 4]
    (
        dq_acc, send, recv, ring_send, ring_recv,
        send_sem, recv_sem, ring_send_sem, ring_recv_sem, next_sem,
    ) = refs[n + 4 :]
    me = lax.axis_index("ctx")
    right, left = lax.rem(me + 1, n), lax.rem(me + n - 1, n)
    across = {"dp": 1 - lax.axis_index("dp")}
    signal_and_wait([{"ctx": right}, {"ctx": left}, across])
    exchange = remote(next_ref, next_came_ref, next_sem.at[0], next_sem.at[1], across)
    exchange.start()
    ring = Ring(
        Axis("ctx"), [mine_ref, came_ref], share_ref.shape[0], ring_send, ring_recv,
        ring_send_sem, ring_recv_sem,
    )
    ring.hop(0)

    def dkv_copy(step, group):
        return remote(
            send.at[group, step], recv.at[group, step], send_sem.at[group, step],
            recv_sem.at[group, step], {"ctx": right},
        )

    for step in range(n):
        kv_ref = kv_refs[(step + 1) % n]
        kpos = kpos_ref[(step + 1) % n]

        def one_group(group, carry):
            keys = kv_ref[:, pl.ds(pl.multiple_of(group * HEAD_SIZE, HEAD_SIZE), HEAD_SIZE)]
            start = pl.multiple_of(KV_WIDTH + group * HEAD_SIZE, HEAD_SIZE)
            values = kv_ref[:, pl.ds(start, HEAD_SIZE)]
            dk = dv = None
            for member in range(GROUP):
                head = group * GROUP + member
                columns = pl.ds(pl.multiple_of(head * HEAD_SIZE, HEAD_SIZE), HEAD_SIZE)
                q, ag = q_ref[:, columns], ag_ref[:, columns]
                scores = dot_nt(keys, q)
                weights = jnp.exp2(scores * score_to_log2 - lse_ref[pl.ds(head, 1), :])
                weights = jnp.where(kpos <= qpos_ref[...], weights, 0.0)
                weights_grad = dot_nt(values, ag)
                score_grad = weights * (weights_grad - delta_ref[pl.ds(head, 1), :]) * score_scale
                score_grad = score_grad.astype(bf16)
                dv_part = dot(weights.astype(bf16), ag)
                dk_part = dot(score_grad, q)
                dv = dv_part if dv is None else dv + dv_part
                dk = dk_part if dk is None else dk + dk_part
                dq = dot_tn(score_grad, keys)
                if step:
                    dq += dq_acc[:, columns]
                dq_acc[:, columns] = dq
            dkv = jnp.concatenate([dk, dv], axis=1)
            if step:
                dkv_copy(step - 1, group).wait_recv()
                dkv += recv[group, step - 1].astype(f32)
            if step < n - 1:
                send[group, step] = dkv.astype(bf16)
                dkv_copy(step, group).start()
            else:
                for place in range(2):
                    start = pl.multiple_of(place * KV_WIDTH + group * HEAD_SIZE, HEAD_SIZE)
                    part = dkv[:, place * HEAD_SIZE : (place + 1) * HEAD_SIZE]
                    dkv_ref[:, pl.ds(start, HEAD_SIZE)] = part.astype(bf16)
            return carry

        lax.fori_loop(0, KEY_VALUE_HEADS, one_group, 0)
        if step < n - 2:
            ring.hop(step + 1)
    cosine, sine = cos_ref[...], sin_ref[...]
    for head in range(QUERY_HEADS):
        span = slice(head * HEAD_SIZE, (head + 1) * HEAD_SIZE)
        dql_ref[:, span] = rotate_back(dq_acc[:, span], cosine, sine).astype(bf16)
    share_ref[...] = ring.hop(n - 1)
    for step in range(n - 1):
        for group in range(KEY_VALUE_HEADS):
            dkv_copy(step, group).wait_send()
    ring.finish()
    exchange.wait()


def attention_backward(q, ag, kvs, lse, delta, kpos, qpos_row, cosine, sine, mine, came, following):
    n = len(kvs)
    rows, keys = q.shape[0], kvs[0].shape[0]
    share = mine.shape[0] // n
    vmem = pl.BlockSpec(memory_space=pltpu.VMEM)
    hbm = pl.BlockSpec(memory_space=pl.ANY)
    return pl.pallas_call(
        functools.partial(attention_back_kernel, n),
        in_specs=[vmem] * 10 + [hbm] + [vmem] * n,
        out_specs=(vmem, vmem, vmem, hbm),
        out_shape=(
            jax.ShapeDtypeStruct((rows, MODEL_WIDTH), bf16),
            jax.ShapeDtypeStruct((keys, 2 * KV_WIDTH), bf16),
            jax.ShapeDtypeStruct((share, mine.shape[1]), f32),
            jax.ShapeDtypeStruct(following.shape, bf16),
        ),
        scratch_shapes=[
            pltpu.VMEM((rows, MODEL_WIDTH), f32),
            pltpu.VMEM((KEY_VALUE_HEADS, n - 1, keys, 2 * HEAD_SIZE), bf16),
            pltpu.VMEM((KEY_VALUE_HEADS, n - 1, keys, 2 * HEAD_SIZE), bf16),
            pltpu.VMEM((n - 1, share, mine.shape[1]), bf16),
            pltpu.VMEM((n - 1, share, mine.shape[1]), bf16),
            pltpu.SemaphoreType.DMA((KEY_VALUE_HEADS, n - 1)),
            pltpu.SemaphoreType.DMA((KEY_VALUE_HEADS, n - 1)),
            pltpu.SemaphoreType.DMA((n - 1,)),
            pltpu.SemaphoreType.DMA((n - 1,)),
            pltpu.SemaphoreType.DMA((2,)),
        ],
        compiler_params=params(collective_id=1, has_side_effects=True),
        cost_estimate=cost(10 * n * rows * keys * MODEL_WIDTH, 4e7, n * rows * keys * QUERY_HEADS),
        name="attention_backward",
    )(q, ag, lse, delta, kpos, qpos_row, cosine, sine, mine, came, following, *kvs)


def input_kernel(
    dql_ref, dkv_ref, wq_ref, wk_ref, wv_ref, cos_ref, sin_ref, x_ref, gain_ref, mg_ref,
    dkvl_ref, dx_ref, dgain_ref,
):
    cosine, sine = cos_ref[...], sin_ref[...]
    for head in range(KEY_VALUE_HEADS):
        span = slice(head * HEAD_SIZE, (head + 1) * HEAD_SIZE)
        dkvl_ref[:, span] = rotate_back(dkv_ref[:, span].astype(f32), cosine, sine).astype(bf16)
    dkvl_ref[:, KV_WIDTH:] = dkv_ref[:, KV_WIDTH:]
    rows = x_ref.shape[0]
    half = rows // 2
    dgain = jnp.zeros((1, MODEL_WIDTH), f32)
    for part in range(2):
        band = slice(part * half, (part + 1) * half)
        grad = dot_nt(dql_ref[band, :], wq_ref[...])
        grad += dot_nt(dkvl_ref[band, :KV_WIDTH], wk_ref[...])
        grad += dot_nt(dkvl_ref[band, KV_WIDTH:], wv_ref[...])
        x = x_ref[band, :].astype(f32)
        r = lax.rsqrt(jnp.mean(x * x, axis=-1, keepdims=True) + epsilon)
        v = grad * gain_ref[...]
        inner = jnp.mean(v * x, axis=-1, keepdims=True)
        dgain += jnp.sum(grad * x * r, axis=0, keepdims=True)
        dx_ref[band, :] = (mg_ref[band, :] + r * v - x * (r * r * r * inner)).astype(bf16)
    dgain_ref[...] = dgain


def input_backward(dql, dkv, wq, wk, wv, cosine, sine, x, gain, mg):
    rows = x.shape[0]
    return pl.pallas_call(
        input_kernel,
        out_shape=(
            jax.ShapeDtypeStruct((rows, 2 * KV_WIDTH), bf16),
            jax.ShapeDtypeStruct((rows, MODEL_WIDTH), bf16),
            jax.ShapeDtypeStruct((1, MODEL_WIDTH), f32),
        ),
        compiler_params=params(),
        cost_estimate=cost(2 * rows * MODEL_WIDTH * (MODEL_WIDTH + 2 * KV_WIDTH), 2e7),
        name="input_backward",
    )(dql, dkv, wq, wk, wv, cosine, sine, x, gain, mg)


def ring_buffers(count, terms, rows, width):
    sends = count - 1 if terms > 1 else max(count - 2, 1)
    return [
        pltpu.VMEM((sends, rows, width), bf16),
        pltpu.VMEM((count - 1, rows, width), bf16),
        pltpu.SemaphoreType.DMA((count - 1,)),
        pltpu.SemaphoreType.DMA((count - 1,)),
    ]


class Chain:
    def __init__(self, rings, stores):
        self.hops = [(r, h) for r in range(len(rings)) for h in range(rings[r].count)]
        self.rings, self.stores, self.done = rings, stores, 0

    def step(self, times=1):
        for _ in range(times):
            if self.done == len(self.hops):
                return
            index, hop = self.hops[self.done]
            self.done += 1
            ring = self.rings[index]
            total = ring.hop(hop)
            if hop == ring.count - 1:
                store = self.stores[index]
                store[...] = total.astype(store.dtype)

    def finish(self):
        assert self.done == len(self.hops)
        for ring in self.rings:
            ring.finish()


FULL_AXES = ("core", "chip", "dp", "ctx")


def sizes():
    exp = lax.axis_size("exp")
    return {"core": 2, "chip": exp // 2, "dp": lax.axis_size("dp"), "ctx": lax.axis_size("ctx")}


def last_kernel(plan, *refs):
    mine_ref, came_ref, mine_down_ref, other_down_ref = refs[:4]
    arrays = refs[4 : 4 + len(plan)]
    share_ref, down_ref = refs[4 + len(plan) : 6 + len(plan)]
    outs = refs[6 + len(plan) : 6 + 2 * len(plan)]
    scratch = list(refs[6 + 2 * len(plan) :])

    def take(number):
        taken = scratch[:number]
        del scratch[:number]
        return taken

    axes = {name: Axis(name) for name in FULL_AXES}
    across = axes["dp"].next
    piece = Chain(
        [Ring(axes["ctx"], [mine_ref, came_ref], share_ref.shape[0], *take(4))], [share_ref]
    )
    came_down, down_sem = take(2)
    downs, exchanges = [], []
    for expert in range(EXP_DEV):
        exchanges.append(
            remote(
                other_down_ref.at[expert], came_down.at[expert], down_sem.at[expert, 0],
                down_sem.at[expert, 1], across,
            )
        )
        terms = [mine_down_ref.at[expert], came_down.at[expert]]
        downs.append(
            Chain(
                [Ring(axes["ctx"], terms, down_ref.shape[1], *take(4))], [down_ref.at[expert]]
            )
        )
    chains = []
    for (names, rows), array, out in zip(plan, arrays, outs):
        rings, stores, source = [], [], array
        for name in names:
            rows //= axes[name].count
            rings.append(Ring(axes[name], [source], rows, *take(4)))
            source = out if name == names[-1] else take(1)[0]
            stores.append(source)
        chains.append(Chain(rings, stores))
    query, kv, out_chain = chains
    signal_and_wait([device for axis in axes.values() for device in axis.neighbours()])

    query.step()
    kv.step()
    piece.step()
    out_chain.step()
    exchanges[0].start()
    query.step(2)
    kv.step(2)
    piece.step()
    out_chain.step(2)
    exchanges[1].start()
    piece.step()
    out_chain.step()
    exchanges[0].wait_recv()
    downs[0].step()
    query.step(2)
    kv.step(2)
    piece.step()
    out_chain.step()
    downs[0].step()
    out_chain.step()
    exchanges[1].wait_recv()
    downs[1].step()
    downs[0].step()
    query.step(2)
    kv.step(2)
    everything = [downs[0], downs[1], query, kv, piece, out_chain]
    while any(chain.done < len(chain.hops) for chain in everything):
        for chain in everything:
            chain.step()
    for chain in everything:
        chain.finish()
    for exchange in exchanges:
        exchange.wait_send()


def last_transfers(mine, came, mine_down, other_down, w_query, w_kv, w_out):
    counts = sizes()
    n = counts["ctx"]
    full = FULL_AXES if (MODEL_WIDTH // (2 * counts["chip"] * counts["dp"] * n)) % 16 == 0 else FULL_AXES[:3]
    plan = [(full, w_query.shape[0]), (full, w_kv.shape[0]), (full[2:], w_out.shape[0])]
    share, down_share = mine.shape[0] // n, mine_down.shape[1] // n
    scratch = ring_buffers(n, 2, share, mine.shape[1])
    scratch += [pltpu.VMEM(mine_down.shape, bf16), pltpu.SemaphoreType.DMA((EXP_DEV, 2))]
    for _ in range(EXP_DEV):
        scratch += ring_buffers(n, 2, down_share, mine_down.shape[2])
    shapes = [
        jax.ShapeDtypeStruct((share, mine.shape[1]), f32),
        jax.ShapeDtypeStruct((EXP_DEV, down_share, mine_down.shape[2]), f32),
    ]
    for (names, rows), array in zip(plan, (w_query, w_kv, w_out)):
        width = array.shape[1]
        for name in names:
            rows //= counts[name]
            scratch += ring_buffers(counts[name], 1, rows, width)
            if name != names[-1]:
                scratch.append(pltpu.VMEM((rows, width), bf16))
        shapes.append(jax.ShapeDtypeStruct((rows, width), f32 if "ctx" in names else bf16))
    vmem = pl.BlockSpec(memory_space=pltpu.VMEM)
    out = pl.pallas_call(
        functools.partial(last_kernel, plan),
        in_specs=[vmem] * 3 + [pl.BlockSpec(memory_space=pl.ANY)] + [vmem] * 3,
        out_specs=(vmem,) * 5,
        out_shape=tuple(shapes),
        scratch_shapes=scratch,
        compiler_params=params(collective_id=2, has_side_effects=True),
        cost_estimate=cost(1e6, 4e7),
        name="last_transfers",
    )(mine, came, mine_down, other_down, w_query, w_kv, w_out)
    attention = out[2:]
    if "ctx" not in full:
        attention = [
            scatter_axis(a.reshape(n, a.shape[0] // n, a.shape[1]), "ctx").astype(f32)
            for a in attention
        ]
    return out[0], out[1], attention


def shifted(value, axis, steps):
    count = lax.axis_size(axis)
    return lax.ppermute(value, axis, [(i, (i + steps) % count) for i in range(count)])


def core_swap(value):
    return lax.ppermute(value, "exp", [(i, i ^ 1) for i in range(lax.axis_size("exp"))])


def chip_shift(value, steps):
    count = lax.axis_size("exp")
    return lax.ppermute(value, "exp", [(i, (i + 2 * steps) % count) for i in range(count)])


def gather_blocks(own):
    swapped = core_swap(own)
    out = [own, swapped]
    own, swapped = tie(own, swapped)
    for steps in range(1, lax.axis_size("exp") // 2):
        same = chip_shift(own, steps)
        out += [core_swap(same), same]
    return out


def return_blocks(parts):
    terms = [parts[0], core_swap(parts[1])]
    for steps in range(1, lax.axis_size("exp") // 2):
        crossed = core_swap(parts[2 * steps])
        both = (crossed.astype(f32) + parts[2 * steps + 1].astype(f32)).astype(bf16)
        terms.append(chip_shift(both, -steps))
    return terms


def ring_part(parts, index, count, step, axis=0):
    return lax.dynamic_index_in_dim(parts, (index - 1 - step) % count, axis, keepdims=False)


def add_low(a, b):
    return (a.astype(f32) + b.astype(f32)).astype(bf16)


def ring_scatter(parts, shift, index, count, axis=0):
    total = ring_part(parts, index, count, 0, axis)
    for step in range(1, count):
        total = add_low(shift(total), ring_part(parts, index, count, step, axis))
    return total


def by_owner(array):
    dp, ctx, exp = (lax.axis_size(a) for a in ("dp", "ctx", "exp"))
    rows, columns = array.shape
    parts = array.reshape(dp, ctx, exp // 2, 2, rows // (dp * ctx * exp), columns)
    return jnp.transpose(parts, (3, 2, 0, 1, 4, 5)).reshape(rows, columns)


def scatter_core(array):
    parts = array.reshape(2, lax.axis_size("exp") // 2, -1, array.shape[1])
    return ring_scatter(parts, core_swap, lax.axis_index("exp") % 2, 2)


def scatter_chip(parts):
    return ring_scatter(
        parts, lambda v: chip_shift(v, 1), lax.axis_index("exp") // 2, lax.axis_size("exp") // 2
    )


def scatter_axis(parts, axis):
    return ring_scatter(
        parts, lambda v: shifted(v, axis, 1), lax.axis_index(axis), lax.axis_size(axis)
    )


def tie(*values):
    return lax.optimization_barrier(values)


def per_device(
    tokens, attn_gain, w_query, key_matrix, value_matrix, w_out, ffn_gain, expert_gate_up,
    expert_down, expert_ids, gate_weights, span_order, out_grad,
):
    ctx_size, exp_size = lax.axis_size("ctx"), lax.axis_size("exp")
    ctx_here, exp_here = lax.axis_index("ctx"), lax.axis_index("exp")
    experts = EXP_DEV * exp_size
    x, g = tokens[0], out_grad[0]
    rows = x.shape[0]
    capacity = rows * TOPK * 5 // (4 * experts)
    gain_one, gain_two = attn_gain[None, :], ffn_gain[None, :]
    offsets = jnp.arange(HALF, dtype=jnp.int32)

    def device_positions(device):
        pair = lax.dynamic_slice_in_dim(span_order[0], 2 * device, 2, 0)
        return (pair[:, None] * HALF + offsets[None, :]).reshape(-1)

    sources = [(ctx_here - s) % ctx_size for s in range(ctx_size)]
    key_positions = [device_positions(s) for s in sources]
    positions = key_positions[0]
    exponent = jnp.arange(HEAD_SIZE // 2, dtype=f32) * (-2.0 / HEAD_SIZE)
    frequency = jnp.power(f32(rope_base), exponent)
    angles = positions.astype(f32)[:, None] * frequency[None, :]
    cosine, sine = jnp.cos(angles), jnp.sin(angles)
    cosine = jnp.concatenate([cosine, cosine], axis=1)
    sine = jnp.concatenate([-sine, sine], axis=1)

    normed, kv_own = norm_kv(x, gain_one, key_matrix, value_matrix, cosine, sine)
    kv_blocks = [kv_own] + [shifted(kv_own, "ctx", s) for s in range(1, ctx_size)]
    q = query_projection(normed, w_query, cosine, sine)

    named = expert_ids[0][:, :, None] == jnp.arange(experts, dtype=jnp.int32)
    member = jnp.any(named, axis=1)
    count = member.astype(jnp.int32)
    place = jnp.where(member, jnp.cumsum(count, axis=0) - count, -1)
    route_gate = jnp.sum(jnp.where(named, gate_weights[0][:, :, None], 0.0), axis=1)
    routing = jnp.stack([place.astype(f32), route_gate]).transpose(0, 2, 1)
    routing = gather_blocks(routing)

    def local_routing(block):
        pair = lax.dynamic_slice_in_dim(block, EXP_DEV * exp_here, EXP_DEV, 1)
        return pair[0].astype(jnp.int32), pair[1]

    routing = [local_routing(block) for block in routing]
    pos = jnp.stack([r[0] for r in routing])
    gates = jnp.stack([r[1] for r in routing])
    g_blocks = gather_blocks(g)

    kv_all = jnp.concatenate(kv_blocks, axis=0)
    kv_all, pos, gates, g_blocks = tie(kv_all, pos, gates, g_blocks)
    kpos_row = jnp.concatenate(key_positions)[None, :]
    att, att_low, lse, mid, nf = attention_forward(
        q, kv_all, positions[:, None], kpos_row, w_out, x, gain_two
    )

    swapped = core_swap(nf)
    nf_blocks = [nf, swapped]
    nf, swapped = tie(nf, swapped)
    y_parts, dx_parts, kept = [], [], None
    for first in range(0, exp_size, 2):
        here = slice(first, first + 2)
        if first:
            same, dx_parts[-1] = tie(chip_shift(nf, first // 2), dx_parts[-1])
            nf_blocks += [core_swap(same), same]
        y_part, dx_part, kept = expert_blocks(
            first, exp_size, capacity, pos[here], gates[here], nf_blocks[here], g_blocks[here],
            expert_gate_up, expert_down, kept,
        )
        y_parts += y_part
        dx_parts += dx_part
    nf_grad_terms = return_blocks(dx_parts)
    slot_rows, hidden, slot_grad, projected_grad = (
        a.reshape(EXP_DEV, exp_size * capacity, a.shape[-1]) for a in kept
    )
    dp_size, dp_here = lax.axis_size("dp"), lax.axis_index("dp")
    half, down_half = MODEL_WIDTH // dp_size, FF // dp_size
    theirs = [
        weight_grad(e, 1, (dp_here - 1) % dp_size, half, slot_rows, projected_grad)[0]
        for e in range(EXP_DEV)
    ]
    came_first = shifted(theirs[0][: half // 2], "dp", 1)
    mine = [weight_grad(0, 1, dp_here, half, slot_rows, projected_grad)[0]]
    slot_rows, theirs, mine, came_first = tie(slot_rows, theirs, mine, came_first)
    came_second = shifted(theirs[0][half // 2 :], "dp", 1)
    mine.append(weight_grad(1, 1, dp_here, half, slot_rows, projected_grad)[0])
    other_down = weight_grad(0, EXP_DEV, (dp_here - 1) % dp_size, down_half, hidden, slot_grad)
    mine_down = weight_grad(0, EXP_DEV, dp_here, down_half, hidden, slot_grad)
    nf_grad_terms, mine, mine_down, other_down, y_parts = tie(
        nf_grad_terms, mine, mine_down, other_down, y_parts
    )

    mid_grad, mid_grad_low, att_grad, delta, ffn_gain_part = middle_backward(
        nf_grad_terms, mid, g, gain_two, w_out, att
    )
    mid_grad_low, came_second = tie(mid_grad_low, came_second)
    w_out_grad = dot_tn(att_low, mid_grad_low).astype(bf16)
    w_out_part = scatter_core(by_owner(w_out_grad))
    w_out_part, att_grad = tie(w_out_part, att_grad)
    w_out_part = scatter_chip(w_out_part)
    y_terms = return_blocks(y_parts)

    came = jnp.concatenate([came_first, came_second], axis=0)
    dql, dkv, gate_up_first, came = attention_backward(
        q, att_grad, kv_blocks, lse, delta, jnp.stack(key_positions)[:, :, None],
        positions[None, :], cosine, sine, mine[0], came, theirs[1],
    )
    layer_output = mid
    for term in y_terms:
        layer_output = layer_output + term.astype(f32)
    layer_output = layer_output.astype(bf16)
    w_query_grad = by_owner(dot_tn(normed, dql).astype(bf16))
    dkvl, tokens_grad, attn_gain_part = input_backward(
        dql, dkv, w_query, key_matrix, value_matrix, cosine, sine, x, gain_one, mid_grad
    )
    w_kv_grad = dot_tn(normed, dkvl)
    gains = jnp.concatenate([attn_gain_part, ffn_gain_part], axis=0).T
    gains = jnp.pad(gains, ((0, 0), (0, HEAD_SIZE - 2)))
    w_kv_grad = by_owner(jnp.concatenate([w_kv_grad, gains], axis=1).astype(bf16))
    gate_up_second, down_share, (w_query_share, w_kv_share, w_out_share) = last_transfers(
        mine[1], came, mine_down, other_down, w_query_grad, w_kv_grad, w_out_part
    )
    return (
        layer_output[None],
        tokens_grad[None],
        w_kv_share[:, 2 * KV_WIDTH],
        w_query_share,
        w_kv_share[:, :KV_WIDTH],
        w_kv_share[:, KV_WIDTH : 2 * KV_WIDTH],
        w_out_share,
        w_kv_share[:, 2 * KV_WIDTH + 1],
        jnp.stack([gate_up_first, gate_up_second]),
        down_share,
    )


def solution(mesh):
    by_row = P(("dp", "exp"), "ctx", None)
    share = P(("dp", "ctx", "exp"))
    share_rows = P(("dp", "ctx", "exp"), None)
    return jax.shard_map(
        per_device,
        mesh=mesh,
        in_specs=(
            by_row, P(), P(), P(), P(), P(), P(), P("exp", None, None), P("exp", None, None),
            by_row, by_row, P(("dp", "exp"), None), by_row,
        ),
        out_specs=(
            by_row, by_row, share, share_rows, share_rows, share_rows, share_rows, share,
            P("exp", ("dp", "ctx"), None), P("exp", ("dp", "ctx"), None),
        ),
        check_vma=False,
    )
```

```python
import functools
import math

import jax
import jax.numpy as jnp
from jax import lax
from jax.experimental import pallas as pl
from jax.experimental.pallas import tpu as pltpu
from jax.sharding import PartitionSpec as P

MODEL_WIDTH = 1536
QUERY_HEADS = 12
KEY_VALUE_HEADS = 2
GROUP = QUERY_HEADS // KEY_VALUE_HEADS
HEAD_SIZE = 128
KV_WIDTH = KEY_VALUE_HEADS * HEAD_SIZE
FF = 768
TOPK = 4
EXP_DEV = 2
TOK_DEV = 512
HALF = 256

epsilon = 1e-06
rope_base = 1000000.0
masked_score = -1e30
score_scale = HEAD_SIZE ** (-0.5)
score_to_log2 = score_scale * math.log2(math.e)
gelu_c = math.sqrt(2.0 / math.pi)

f32 = jnp.float32
bf16 = jnp.bfloat16
NT = (((1,), (1,)), ((), ()))
TN = (((0,), (0,)), ((), ()))
VMEM_BYTES = 63 * 1024 * 1024
MESH = pl.DeviceIdType.MESH


def dot(a, b):
    return jnp.dot(a, b, preferred_element_type=f32)


def dot_nt(a, b):
    return lax.dot_general(a, b, NT, preferred_element_type=f32)


def dot_tn(a, b):
    return lax.dot_general(a, b, TN, preferred_element_type=f32)


def params(**more):
    return pltpu.CompilerParams(vmem_limit_bytes=VMEM_BYTES, **more)


def cost(flops, size, exps=0):
    return pl.CostEstimate(flops=int(flops) // 32, bytes_accessed=int(size) // 32, transcendentals=int(exps) // 32)


def whole(shape):
    return pl.BlockSpec(shape, lambda *_: (0,) * len(shape))


def rotate(values, cosine, signed_sine):
    return values * cosine + pltpu.roll(values, HEAD_SIZE // 2, 1) * signed_sine


def rotate_back(values, cosine, signed_sine):
    return values * cosine - pltpu.roll(values, HEAD_SIZE // 2, 1) * signed_sine


HEAD_ROWS = 16


class Gather:
    def __init__(self, own, slots, send_sem, recv_sem):
        self.own, self.slots, self.send_sem, self.recv_sem = own, slots, send_sem, recv_sem
        self.chips = lax.axis_size("exp") // 2
        exp = lax.axis_index("exp")
        core, chip = lax.rem(exp, 2), exp // 2
        self.other = {"exp": chip * 2 + 1 - core}
        self.ahead = [
            {"exp": lax.rem(chip + s, self.chips) * 2 + core} for s in range(self.chips)
        ]
        self.behind = [
            {"exp": lax.rem(chip + self.chips - s, self.chips) * 2 + core}
            for s in range(self.chips)
        ]

    def neighbours(self):
        if self.chips == 2:
            return [self.other, self.ahead[1]]
        return [self.other] + self.ahead[1:]

    def copy(self, slot):
        source, device = self.own, self.other
        if slot > 1 and slot % 2 == 0:
            source = self.slots.at[slot + 1]
        elif slot > 1:
            device = self.ahead[slot // 2]
        return remote(
            source, self.slots.at[slot], self.send_sem.at[slot], self.recv_sem.at[slot], device
        )

    def start(self):
        self.copy(1).start()
        for s in range(1, self.chips):
            self.copy(2 * s + 1).start()

    def cross(self):
        for s in range(1, self.chips):
            self.copy(2 * s + 1).wait_recv()
            self.copy(2 * s).start()

    def finish(self):
        self.copy(1).wait_recv()
        for s in range(1, self.chips):
            self.copy(2 * s).wait_recv()
        for slot in range(1, 2 * self.chips):
            self.copy(slot).wait_send()


def forward_kernel(
    n, x_ref, gain_ref, wk_ref, wv_ref, cos_ref, sin_ref, qpos_ref, kpos_ref, ffn_gain_ref, wq_hbm,
    wo_hbm, g_hbm, routing_hbm, normed_ref, q_ref, kv_ref, att_ref, att_low_ref, lse_ref, mid_ref,
    nf_ref, g_all, routing_all, wq_ref, wo_ref, tops, totals, load_sem, send_sem, recv_sem,
    g_send_sem, g_recv_sem, routing_send_sem, routing_recv_sem,
):
    load_q = pltpu.make_async_copy(wq_hbm, wq_ref, load_sem.at[0])
    load_o = pltpu.make_async_copy(wo_hbm, wo_ref, load_sem.at[1])
    load_q.start()
    load_o.start()
    ctx = Axis("ctx")
    gathers = [
        Gather(routing_hbm, routing_all, routing_send_sem, routing_recv_sem),
        Gather(g_hbm, g_all, g_send_sem, g_recv_sem),
    ]
    signal_and_wait(ctx.neighbours() + gathers[0].neighbours())
    for gather in gathers:
        gather.start()

    def pass_on(step):
        return remote(
            kv_ref.at[step], kv_ref.at[step + 1], send_sem.at[step], recv_sem.at[step], ctx.next
        )

    rows = x_ref.shape[0]
    x = x_ref[...].astype(f32)
    r = lax.rsqrt(jnp.mean(x * x, axis=-1, keepdims=True) + epsilon)
    normed_ref[...] = (x * r * gain_ref[...]).astype(bf16)
    normed = normed_ref[...]
    cosine, sine = cos_ref[...], sin_ref[...]
    keys = dot(normed, wk_ref[...])
    for head in range(KEY_VALUE_HEADS):
        span = slice(head * HEAD_SIZE, (head + 1) * HEAD_SIZE)
        kv_ref[0, :, span] = rotate(keys[:, span], cosine, sine).astype(bf16)
    kv_ref[0, :, KV_WIDTH:] = dot(normed, wv_ref[...]).astype(bf16)
    pass_on(0).start()
    load_q.wait()
    for start in range(0, MODEL_WIDTH, WIDTH_TILE):
        queries = dot(normed, wq_ref[:, start : start + WIDTH_TILE])
        for offset in range(0, WIDTH_TILE, HEAD_SIZE):
            span = slice(start + offset, start + offset + HEAD_SIZE)
            part = queries[:, offset : offset + HEAD_SIZE]
            q_ref[:, span] = rotate(part, cosine, sine).astype(bf16)

    for step in range(n):
        if step:
            pass_on(step - 1).wait_recv()
            if step < n - 1:
                pass_on(step).start()
        allowed = kpos_ref[step] <= qpos_ref[...]

        def one_group(group, carry):
            keys = kv_ref[step, :, pl.ds(pl.multiple_of(group * HEAD_SIZE, HEAD_SIZE), HEAD_SIZE)]
            start = pl.multiple_of(KV_WIDTH + group * HEAD_SIZE, HEAD_SIZE)
            values = kv_ref[step, :, pl.ds(start, HEAD_SIZE)]
            for member in range(GROUP):
                head = group * GROUP + member
                columns = pl.ds(pl.multiple_of(head * HEAD_SIZE, HEAD_SIZE), HEAD_SIZE)
                lane = slice(member, member + 1)
                scores = jnp.where(allowed, dot_nt(q_ref[:, columns], keys), masked_score)
                top = jnp.max(scores, axis=-1, keepdims=True) * score_to_log2
                if step:
                    before = tops[group, :, lane]
                    top = jnp.maximum(before, top)
                    rescale = jnp.exp2(before - top)
                weights = jnp.exp2(scores * score_to_log2 - top)
                total = jnp.sum(weights, axis=-1, keepdims=True)
                out = dot(weights.astype(bf16), values)
                if step:
                    total += totals[group, :, lane] * rescale
                    out += att_ref[:, columns] * rescale
                if step < n - 1:
                    tops[group, :, lane] = top
                    totals[group, :, lane] = total
                else:
                    out /= total
                    att_low_ref[:, columns] = out.astype(bf16)
                    tops[group, :, lane] = top + jnp.log2(total)
                att_ref[:, columns] = out
            return carry

        lax.fori_loop(0, KEY_VALUE_HEADS, one_group, 0)
    for group in range(KEY_VALUE_HEADS):
        lse_ref[group * GROUP : (group + 1) * GROUP, :] = tops[group].T[:GROUP, :]
    lse_ref[QUERY_HEADS:, :] = jnp.zeros((HEAD_ROWS - QUERY_HEADS, rows), f32)
    for gather in gathers:
        gather.cross()
    load_o.wait()
    half = rows // 2
    for part in range(2):
        band = slice(part * half, (part + 1) * half)
        mid = x_ref[band, :].astype(f32) + dot(att_low_ref[band, :], wo_ref[...])
        mid_ref[band, :] = mid
        r = lax.rsqrt(jnp.mean(mid * mid, axis=-1, keepdims=True) + epsilon)
        nf_ref[band, :] = (mid * r * ffn_gain_ref[...]).astype(bf16)
    for step in range(n - 1):
        pass_on(step).wait_send()
    for gather in gathers:
        gather.finish()


def forward_to_experts(
    x, gain, wk, wv, cosine, sine, qpos_col, kpos_rows, ffn_gain, wq, wo, g, routing
):
    exp_size = lax.axis_size("exp")
    rows, n = x.shape[0], kpos_rows.shape[0]
    vmem = pl.BlockSpec(memory_space=pltpu.VMEM)
    hbm = pl.BlockSpec(memory_space=pl.ANY)
    wide = (rows, MODEL_WIDTH)
    return pl.pallas_call(
        functools.partial(forward_kernel, n),
        in_specs=[vmem] * 9 + [hbm] * 4,
        out_specs=(vmem,) * 8 + (hbm,) * 2,
        out_shape=(
            jax.ShapeDtypeStruct(wide, bf16),
            jax.ShapeDtypeStruct(wide, bf16),
            jax.ShapeDtypeStruct((n, rows, 2 * KV_WIDTH), bf16),
            jax.ShapeDtypeStruct(wide, f32),
            jax.ShapeDtypeStruct(wide, bf16),
            jax.ShapeDtypeStruct((HEAD_ROWS, rows), f32),
            jax.ShapeDtypeStruct(wide, f32),
            jax.ShapeDtypeStruct(wide, bf16),
            jax.ShapeDtypeStruct((exp_size, *g.shape), bf16),
            jax.ShapeDtypeStruct((exp_size, *routing.shape), f32),
        ),
        scratch_shapes=[
            pltpu.VMEM((MODEL_WIDTH, MODEL_WIDTH), bf16),
            pltpu.VMEM((MODEL_WIDTH, MODEL_WIDTH), bf16),
            pltpu.VMEM((KEY_VALUE_HEADS, rows, HEAD_SIZE), f32),
            pltpu.VMEM((KEY_VALUE_HEADS, rows, HEAD_SIZE), f32),
            pltpu.SemaphoreType.DMA((2,)),
            pltpu.SemaphoreType.DMA((n - 1,)),
            pltpu.SemaphoreType.DMA((n - 1,)),
        ]
        + [pltpu.SemaphoreType.DMA((exp_size,))] * 4,
        compiler_params=params(collective_id=3, has_side_effects=True),
        cost_estimate=cost(
            4 * n * rows * rows * MODEL_WIDTH + 5 * rows * MODEL_WIDTH * MODEL_WIDTH, 4e7,
            n * rows * rows * QUERY_HEADS,
        ),
        name="forward_to_experts",
    )(x, gain, wk, wv, cosine, sine, qpos_col, kpos_rows, ffn_gain, wq, wo, g, routing)


FF_TILE = 256
WIDTH_TILE = 512


def expert_kernel(first, count, pos_row_ref, pos_col_ref, gate_row_ref, *refs):
    x_refs = refs[:count]
    g_own_ref, g_ref, wgu_ref, wd_ref = refs[count : count + 4]
    rows_ref, hidden_ref, slot_grad_ref, pg_ref, place, result, rows_grad = refs[-7:]
    y_refs, dx_refs = refs[-7 - 2 * count : -7 - count], refs[-7 - count : -7]
    block, expert = pl.program_id(0), pl.program_id(1)
    capacity = rows_ref.shape[-2]
    tokens = x_refs[0].shape[0]
    slot_r = lax.broadcasted_iota(jnp.int32, (capacity, tokens), 0)
    slot_c = lax.broadcasted_iota(jnp.int32, (tokens, capacity), 1)
    match = slot_r == pos_row_ref[0, 0]
    pick = match.astype(bf16)
    place[expert] = (slot_c == pos_col_ref[0, 0]).astype(bf16)
    gates = jnp.sum(jnp.where(match, gate_row_ref[0, 0], 0.0), axis=1, keepdims=True)
    for one in range(count):

        @pl.when(block == one)
        def _():
            for start in range(0, MODEL_WIDTH, WIDTH_TILE):
                span = slice(start, start + WIDTH_TILE)
                rows_ref[0, 0, :, span] = dot(pick, x_refs[one][:, span]).astype(bf16)
                g_here = g_own_ref[:, span] if first + one == 0 else g_ref[0, :, span]
                slot_grad_ref[0, 0, :, span] = (dot(pick, g_here) * gates).astype(bf16)

    rows = rows_ref[0, 0]
    slot_grad = slot_grad_ref[0, 0]
    for start in range(0, FF, FF_TILE):
        span = slice(start, start + FF_TILE)
        up_span = slice(FF + start, FF + start + FF_TILE)
        gate = dot(rows, wgu_ref[0, :, span])
        up = dot(rows, wgu_ref[0, :, up_span])
        hidden_grad = dot_nt(slot_grad, wd_ref[0, span, :])
        square = gate * gate
        tangent = jnp.tanh(gate * (gelu_c + (gelu_c * 0.044715) * square))
        half_plus = 0.5 + 0.5 * tangent
        activated = gate * half_plus
        slope = half_plus + activated * (1.0 - tangent) * (
            gelu_c + (3.0 * 0.044715 * gelu_c) * square
        )
        hidden_ref[0, 0, :, span] = (activated * up).astype(bf16)
        pg_ref[0, 0, :, span] = (hidden_grad * up * slope).astype(bf16)
        pg_ref[0, 0, :, up_span] = (hidden_grad * activated).astype(bf16)
    hidden = hidden_ref[0, 0]
    projected_grad = pg_ref[0, 0]
    for start in range(0, MODEL_WIDTH, WIDTH_TILE):
        span = slice(start, start + WIDTH_TILE)
        result[expert, :, span] = (dot(hidden, wd_ref[0, :, span]) * gates).astype(bf16)
        rows_grad[expert, :, span] = dot_nt(projected_grad, wgu_ref[0, span, :]).astype(bf16)

    for one in range(count):

        @pl.when((expert == EXP_DEV - 1) & (block == one))
        def _():
            both = jnp.concatenate([place[e] for e in range(EXP_DEV)], axis=1)
            for start in range(0, MODEL_WIDTH, WIDTH_TILE):
                span = slice(start, start + WIDTH_TILE)
                for out_ref, terms in ((y_refs[one], result), (dx_refs[one], rows_grad)):
                    stacked = terms[:, :, span].reshape(EXP_DEV * capacity, WIDTH_TILE)
                    out_ref[:, span] = dot(both, stacked).astype(bf16)


def expert_blocks(first, blocks, capacity, pos, gates, xs, g, g_all, wgu, wd, kept):
    count, tokens = len(xs), xs[0].shape[0]
    kept_shapes = tuple(
        jax.ShapeDtypeStruct((EXP_DEV, blocks, capacity, width), bf16)
        for width in (MODEL_WIDTH, FF, MODEL_WIDTH, 2 * FF)
    )
    kept_specs = tuple(
        pl.BlockSpec((1, 1, capacity, s.shape[-1]), lambda b, e: (e, first + b, 0, 0))
        for s in kept_shapes
    )
    args = [pos[:, :, None, :], pos[:, :, :, None], gates[:, :, None, :], *xs, g, g_all, wgu, wd]
    aliases = {} if kept is None else {len(args) + i: 2 * count + i for i in range(4)}
    flops = count * EXP_DEV * 2 * capacity * (4 * tokens * MODEL_WIDTH + 9 * MODEL_WIDTH * FF)
    result = jax.ShapeDtypeStruct((tokens, MODEL_WIDTH), bf16)
    once = pl.BlockSpec((tokens, MODEL_WIDTH), lambda b, e: (0, 0), pipeline_mode=pl.Buffered(1))
    out = pl.pallas_call(
        functools.partial(expert_kernel, first, count),
        grid=(count, EXP_DEV),
        in_specs=[
            pl.BlockSpec((1, 1, 1, tokens), lambda b, e: (b, e, 0, 0)),
            pl.BlockSpec((1, 1, tokens, 1), lambda b, e: (b, e, 0, 0)),
            pl.BlockSpec((1, 1, 1, tokens), lambda b, e: (b, e, 0, 0)),
        ]
        + [once] * (count + 1)
        + [
            pl.BlockSpec((1, tokens, MODEL_WIDTH), lambda b, e: (jnp.maximum(first + b, 1), 0, 0)),
            pl.BlockSpec((1, MODEL_WIDTH, 2 * FF), lambda b, e: (e, 0, 0)),
            pl.BlockSpec((1, FF, MODEL_WIDTH), lambda b, e: (e, 0, 0)),
        ]
        + [pl.BlockSpec(memory_space=pl.ANY) for _ in aliases],
        out_specs=(once,) * (2 * count) + kept_specs,
        out_shape=(result,) * (2 * count) + kept_shapes,
        scratch_shapes=[
            pltpu.VMEM((EXP_DEV, tokens, capacity), bf16),
            pltpu.VMEM((EXP_DEV, capacity, MODEL_WIDTH), bf16),
            pltpu.VMEM((EXP_DEV, capacity, MODEL_WIDTH), bf16),
        ],
        input_output_aliases=aliases,
        compiler_params=params(),
        cost_estimate=cost(flops, 6e7),
        name="expert_blocks",
    )(*args, *(kept or ()))
    return out[:count], out[count : 2 * count], out[2 * count :]


GRAD_TILE = 384


def weight_grad_kernel(chunk_ref, a_ref, b_ref, out_ref):
    out_ref[0] = dot_tn(a_ref[0], b_ref[0]).astype(bf16)


def weight_grad(first, experts, chunk, size, a, b):
    slots, width = a.shape[1], b.shape[-1]
    tiles = size // GRAD_TILE
    return pl.pallas_call(
        weight_grad_kernel,
        grid_spec=pltpu.PrefetchScalarGridSpec(
            num_scalar_prefetch=1,
            grid=(experts, tiles),
            in_specs=[
                pl.BlockSpec((1, slots, GRAD_TILE), lambda e, t, c: (first + e, 0, c[0] * tiles + t)),
                pl.BlockSpec((1, slots, width), lambda e, t, c: (first + e, 0, 0)),
            ],
            out_specs=pl.BlockSpec((1, GRAD_TILE, width), lambda e, t, c: (e, t, 0)),
        ),
        out_shape=jax.ShapeDtypeStruct((experts, size, width), bf16),
        compiler_params=params(),
        cost_estimate=cost(2 * experts * slots * size * width, 2e7),
        name="weight_grad",
    )(chunk.reshape(1).astype(jnp.int32), a, b)


def middle_kernel(*refs):
    count = len(refs) - 11
    parts = refs[:count]
    mid_ref, g_ref, gain_ref, wo_ref, att_ref = refs[count : count + 5]
    mg_ref, mgl_ref, ag_ref, delta_ref, dgain_ref, delta_cols = refs[count + 5 :]
    rows = mid_ref.shape[0]
    half = rows // 2
    lane = lax.broadcasted_iota(jnp.int32, (half, HEAD_SIZE), 1)
    dgain = jnp.zeros((1, MODEL_WIDTH), f32)
    for part in range(2):
        band = slice(part * half, (part + 1) * half)
        nf_grad = parts[0][band, :].astype(f32)
        for other in parts[1:]:
            nf_grad += other[band, :].astype(f32)
        mid = mid_ref[band, :]
        r = lax.rsqrt(jnp.mean(mid * mid, axis=-1, keepdims=True) + epsilon)
        u = nf_grad * gain_ref[...]
        inner = jnp.mean(u * mid, axis=-1, keepdims=True)
        grad = g_ref[band, :].astype(f32) + r * u - mid * (r * r * r * inner)
        dgain += jnp.sum(nf_grad * mid * r, axis=0, keepdims=True)
        mg_ref[band, :] = grad
        low = grad.astype(bf16)
        mgl_ref[band, :] = low
        att_grad = dot_nt(low, wo_ref[...]).astype(bf16)
        ag_ref[band, :] = att_grad
        delta = jnp.zeros((half, HEAD_SIZE), f32)
        for head in range(QUERY_HEADS):
            span = slice(head * HEAD_SIZE, (head + 1) * HEAD_SIZE)
            one = jnp.sum(att_grad[:, span].astype(f32) * att_ref[band, span], axis=-1, keepdims=True)
            delta = jnp.where(lane == head, one, delta)
        delta_cols[band, :] = delta
    dgain_ref[...] = dgain
    delta_ref[...] = delta_cols[...].T[: delta_ref.shape[0], :]


def middle_backward(parts, mid, g, gain, wo, att):
    rows = mid.shape[0]
    return pl.pallas_call(
        middle_kernel,
        out_shape=(
            jax.ShapeDtypeStruct((rows, MODEL_WIDTH), f32),
            jax.ShapeDtypeStruct((rows, MODEL_WIDTH), bf16),
            jax.ShapeDtypeStruct((rows, MODEL_WIDTH), bf16),
            jax.ShapeDtypeStruct((HEAD_ROWS, rows), f32),
            jax.ShapeDtypeStruct((1, MODEL_WIDTH), f32),
        ),
        scratch_shapes=[pltpu.VMEM((rows, HEAD_SIZE), f32)],
        compiler_params=params(),
        cost_estimate=cost(2 * rows * MODEL_WIDTH * MODEL_WIDTH, 2e7),
        name="middle_backward",
    )(*parts, mid, g, gain, wo, att)


def signal_and_wait(neighbours):
    barrier = pltpu.get_barrier_semaphore()
    for neighbour in neighbours:
        pl.semaphore_signal(barrier, inc=1, device_id=neighbour, device_id_type=MESH)
    pl.semaphore_wait(barrier, len(neighbours))


def remote(source, target, send_sem, recv_sem, device):
    return pltpu.make_async_remote_copy(
        src_ref=source, dst_ref=target, send_sem=send_sem, recv_sem=recv_sem,
        device_id=device, device_id_type=MESH,
    )


class Axis:
    def __init__(self, name):
        if name in ("dp", "ctx"):
            self.count, self.me = lax.axis_size(name), lax.axis_index(name)
            place = lambda i: {name: i}
        else:
            exp = lax.axis_index("exp")
            core, chip = lax.rem(exp, 2), exp // 2
            if name == "core":
                self.count, self.me = 2, core
                place = lambda i: {"exp": chip * 2 + i}
            else:
                self.count, self.me = lax.axis_size("exp") // 2, chip
                place = lambda i: {"exp": i * 2 + core}
        self.next = place(lax.rem(self.me + 1, self.count))
        self.last = place(lax.rem(self.me + self.count - 1, self.count))

    def neighbours(self):
        return [self.next] if self.count == 2 else [self.next, self.last]


class Ring:
    def __init__(self, axis, terms, rows, send, recv, send_sem, recv_sem):
        self.axis, self.count, self.terms, self.rows = axis, axis.count, terms, rows
        self.send, self.recv, self.send_sem, self.recv_sem = send, recv, send_sem, recv_sem

    def here(self, hop):
        part = lax.rem(self.axis.me + self.count - 1 - hop, self.count)
        return pl.ds(pl.multiple_of(part * self.rows, self.rows), self.rows)

    def copy(self, hop):
        if len(self.terms) > 1:
            source = self.send.at[hop]
        elif hop == 0:
            source = self.terms[0].at[self.here(0), :]
        else:
            source = self.send.at[hop - 1]
        return remote(
            source, self.recv.at[hop], self.send_sem.at[hop], self.recv_sem.at[hop], self.axis.next
        )

    def hop(self, hop):
        if hop == 0 and len(self.terms) == 1:
            self.copy(0).start()
            return None
        here = self.here(hop)
        total = self.terms[0][here, :].astype(f32)
        for term in self.terms[1:]:
            total += term[here, :].astype(f32)
        if hop:
            self.copy(hop - 1).wait_recv()
            total += self.recv[hop - 1].astype(f32)
        if hop < self.count - 1:
            self.send[hop - (len(self.terms) == 1)] = total.astype(bf16)
            self.copy(hop).start()
        return total

    def finish(self):
        for hop in range(self.count - 1):
            self.copy(hop).wait_send()


def attention_back_kernel(
    n, q_ref, ag_ref, kv_ref, lse_ref, delta_ref, kpos_ref, qpos_ref, cos_ref, sin_ref, mine_ref,
    came_ref, wo_grad_ref, next_ref, next_mine_ref, down_ref, down_mine_ref, dql_ref, dkv_ref,
    share_ref, next_sum_ref, down_sum_ref, wo_sum_ref, next_came, down_came, next_mine, down_mine,
    dq_acc, held, send, recv, send_sem, recv_sem, next_sem, *scratch,
):
    ctx, core, chip = Axis("ctx"), Axis("core"), Axis("chip")
    right, across = ctx.next, Axis("dp").next
    signal_and_wait(ctx.neighbours() + core.neighbours() + chip.neighbours() + [across])
    core_rows = wo_grad_ref.shape[0] // 2
    wo_chain = Chain(
        [
            Ring(core, [wo_grad_ref], core_rows, *scratch[:4]),
            Ring(chip, [scratch[4]], core_rows // chip.count, *scratch[5:9]),
        ],
        [scratch[4], wo_sum_ref],
    )
    ring = Ring(ctx, [mine_ref, came_ref], share_ref.shape[0], *scratch[9:])
    ring.hop(0)
    wo_chain.step()
    exchanges, loads = [], []
    for i, (source, target, mine_hbm, mine) in enumerate(
        (
            (next_ref, next_came, next_mine_ref, next_mine),
            (down_ref.at[0], down_came, down_mine_ref.at[0], down_mine),
        )
    ):
        exchanges.append(remote(source, target, next_sem.at[i, 0], next_sem.at[i, 1], across))
        loads.append(pltpu.make_async_copy(mine_hbm, mine, next_sem.at[i, 2]))
        exchanges[i].start()
        loads[i].start()
    def dkv_copy(step, group):
        return remote(
            send.at[group, step], recv.at[group, step], send_sem.at[group, step],
            recv_sem.at[group, step], right,
        )

    for step in range(n):
        back = (step + 1) % n
        kpos = kpos_ref[back]

        def one_group(group, carry):
            keys = kv_ref[back, :, pl.ds(pl.multiple_of(group * HEAD_SIZE, HEAD_SIZE), HEAD_SIZE)]
            start = pl.multiple_of(KV_WIDTH + group * HEAD_SIZE, HEAD_SIZE)
            values = kv_ref[back, :, pl.ds(start, HEAD_SIZE)]
            dk = dv = None
            for member in range(GROUP):
                head = group * GROUP + member
                columns = pl.ds(pl.multiple_of(head * HEAD_SIZE, HEAD_SIZE), HEAD_SIZE)
                q, ag = q_ref[:, columns], ag_ref[:, columns]
                scores = dot_nt(keys, q)
                weights = jnp.exp2(scores * score_to_log2 - lse_ref[pl.ds(head, 1), :])
                weights = jnp.where(kpos <= qpos_ref[...], weights, 0.0)
                weights_grad = dot_nt(values, ag)
                score_grad = weights * (weights_grad - delta_ref[pl.ds(head, 1), :]) * score_scale
                score_grad = score_grad.astype(bf16)
                dv_part = dot(weights.astype(bf16), ag)
                dk_part = dot(score_grad, q)
                dv = dv_part if dv is None else dv + dv_part
                dk = dk_part if dk is None else dk + dk_part
                dq = dot_tn(score_grad, keys)
                if step:
                    dq += dq_acc[:, columns]
                dq_acc[:, columns] = dq
            held[group] = jnp.concatenate([dk, dv], axis=1)
            return carry

        lax.fori_loop(0, KEY_VALUE_HEADS, one_group, 0)
        for group in range(KEY_VALUE_HEADS):
            dkv = held[group]
            if step:
                dkv_copy(step - 1, group).wait_recv()
                dkv += recv[group, step - 1].astype(f32)
            if step < n - 1:
                send[group, step] = dkv.astype(bf16)
                dkv_copy(step, group).start()
            else:
                for place in range(2):
                    start = place * KV_WIDTH + group * HEAD_SIZE
                    part = dkv[:, place * HEAD_SIZE : (place + 1) * HEAD_SIZE]
                    dkv_ref[:, start : start + HEAD_SIZE] = part.astype(bf16)
        if step < n - 2:
            ring.hop(step + 1)
        wo_chain.step(2 if step == 0 else 1)
    cosine, sine = cos_ref[...], sin_ref[...]
    for head in range(QUERY_HEADS):
        span = slice(head * HEAD_SIZE, (head + 1) * HEAD_SIZE)
        dql_ref[:, span] = rotate_back(dq_acc[:, span], cosine, sine).astype(bf16)
    share_ref[...] = ring.hop(n - 1)
    ring.finish()
    for step in range(n - 1):
        for group in range(KEY_VALUE_HEADS):
            dkv_copy(step, group).wait_send()
    wo_chain.step(len(wo_chain.hops))
    wo_chain.finish()
    for i, (sum_ref, mine, came) in enumerate(
        ((next_sum_ref, next_mine, next_came), (down_sum_ref, down_mine, down_came))
    ):
        loads[i].wait()
        exchanges[i].wait()
        for start in range(0, sum_ref.shape[0], HEAD_SIZE):
            band = slice(start, start + HEAD_SIZE)
            total = mine[band, :].astype(f32) + came[band, :].astype(f32)
            sum_ref[band, :] = total.astype(bf16)


def attention_backward(
    q, ag, kv, lse, delta, kpos, qpos_row, cosine, sine, mine, came, w_out_grad, following,
    following_mine, other_down, mine_down,
):
    n, keys, _ = kv.shape
    rows = q.shape[0]
    chips = sizes()["chip"]
    wo_rows = w_out_grad.shape[0] // 2
    vmem = pl.BlockSpec(memory_space=pltpu.VMEM)
    hbm = pl.BlockSpec(memory_space=pl.ANY)
    return pl.pallas_call(
        functools.partial(attention_back_kernel, n),
        in_specs=[vmem] * 12 + [hbm] * 4,
        out_specs=(vmem,) * 6,
        out_shape=(
            jax.ShapeDtypeStruct((rows, MODEL_WIDTH), bf16),
            jax.ShapeDtypeStruct((keys, 2 * KV_WIDTH), bf16),
            jax.ShapeDtypeStruct((mine.shape[0] // n, mine.shape[1]), f32),
            jax.ShapeDtypeStruct(following.shape, bf16),
            jax.ShapeDtypeStruct(other_down.shape[1:], bf16),
            jax.ShapeDtypeStruct((wo_rows // chips, MODEL_WIDTH), bf16),
        ),
        scratch_shapes=[
            pltpu.VMEM(following.shape, bf16),
            pltpu.VMEM(other_down.shape[1:], bf16),
            pltpu.VMEM(following.shape, bf16),
            pltpu.VMEM(other_down.shape[1:], bf16),
            pltpu.VMEM((rows, MODEL_WIDTH), f32),
            pltpu.VMEM((KEY_VALUE_HEADS, keys, 2 * HEAD_SIZE), f32),
            pltpu.VMEM((KEY_VALUE_HEADS, n - 1, keys, 2 * HEAD_SIZE), bf16),
            pltpu.VMEM((KEY_VALUE_HEADS, n - 1, keys, 2 * HEAD_SIZE), bf16),
            pltpu.SemaphoreType.DMA((KEY_VALUE_HEADS, n - 1)),
            pltpu.SemaphoreType.DMA((KEY_VALUE_HEADS, n - 1)),
            pltpu.SemaphoreType.DMA((2, 3)),
        ]
        + ring_buffers(2, 1, wo_rows, MODEL_WIDTH)
        + [pltpu.VMEM((wo_rows, MODEL_WIDTH), bf16)]
        + ring_buffers(chips, 1, wo_rows // chips, MODEL_WIDTH)
        + ring_buffers(n, 2, mine.shape[0] // n, mine.shape[1]),
        compiler_params=params(collective_id=1, has_side_effects=True),
        cost_estimate=cost(10 * n * rows * keys * MODEL_WIDTH, 4e7, n * rows * keys * QUERY_HEADS),
        name="attention_backward",
    )(
        q, ag, kv, lse, delta, kpos, qpos_row, cosine, sine, mine, came, w_out_grad, following,
        following_mine, other_down, mine_down,
    )


def ring_buffers(count, terms, rows, width):
    sends = count - 1 if terms > 1 else count - 2
    return [
        pltpu.VMEM((sends, rows, width) if sends else (16, HEAD_SIZE), bf16),
        pltpu.VMEM((count - 1, rows, width), bf16),
        pltpu.SemaphoreType.DMA((count - 1,)),
        pltpu.SemaphoreType.DMA((count - 1,)),
    ]


class Chain:
    def __init__(self, rings, stores):
        self.hops = [(r, h) for r in range(len(rings)) for h in range(rings[r].count)]
        self.rings, self.stores, self.done = rings, stores, 0

    def step(self, times=1):
        for _ in range(times):
            if self.done == len(self.hops):
                return
            index, hop = self.hops[self.done]
            self.done += 1
            ring = self.rings[index]
            total = ring.hop(hop)
            if hop == ring.count - 1:
                store = self.stores[index]
                store[...] = total.astype(store.dtype)

    def finish(self):
        assert self.done == len(self.hops)
        for ring in self.rings:
            ring.finish()


FULL_AXES = ("core", "chip", "dp", "ctx")


def sizes():
    exp = lax.axis_size("exp")
    return {"core": 2, "chip": exp // 2, "dp": lax.axis_size("dp"), "ctx": lax.axis_size("ctx")}


class Total:
    def __init__(self, axis, value, recv, send_sem, recv_sem):
        self.axis, self.value, self.recv = axis, value, recv
        self.send_sem, self.recv_sem = send_sem, recv_sem

    def copy(self, hop):
        source = self.recv.at[hop - 1] if hop else self.value
        return remote(
            source, self.recv.at[hop], self.send_sem.at[hop], self.recv_sem.at[hop], self.axis.next
        )

    def run(self):
        count = self.axis.count
        self.copy(0).start()
        total = self.value[...]
        for hop in range(1, count):
            self.copy(hop - 1).wait_recv()
            total += self.recv[hop - 1]
            if hop < count - 1:
                self.copy(hop).start()
        for hop in range(count - 1):
            self.copy(hop).wait_send()
        self.value[...] = total


GAIN_ROWS = 8


def last_kernel(
    plan, piece_ref, down_sum_ref, mine_down_ref, other_down_ref, dql_ref, dkv_ref, normed_ref, wq_ref,
    wk_ref, wv_ref, cos_ref, sin_ref, x_ref, gain_ref, mg_hbm, ffn_gain_ref, wo_sum_ref,
    gate_up_ref, down_ref, dx_ref, gains_ref, wq_out, wkv_out, wo_out, wq_grad, wkv_grad, dkvl,
    mg_band, mg_sem, *scratch,
):
    scratch = list(scratch)

    def take(number):
        taken = scratch[:number]
        del scratch[:number]
        return taken

    axes = {name: Axis(name) for name in FULL_AXES}
    across = axes["dp"].next
    piece = Chain(
        [Ring(axes["ctx"], [piece_ref], gate_up_ref.shape[0], *take(4))], [gate_up_ref]
    )
    came_down, mine_down, down_sem = take(3)
    exchange = remote(
        other_down_ref.at[1], came_down, down_sem.at[0], down_sem.at[1], across
    )
    load_down = pltpu.make_async_copy(mine_down_ref.at[1], mine_down, down_sem.at[2])
    downs = [
        Chain([Ring(axes["ctx"], terms, down_ref.shape[1], *take(4))], [down_ref.at[expert]])
        for expert, terms in enumerate(([down_sum_ref], [mine_down, came_down]))
    ]
    chains = []
    for (names, rows), array, out in zip(
        plan, (wq_grad, wkv_grad, wo_sum_ref), (wq_out, wkv_out, wo_out)
    ):
        rings, stores, source = [], [], array
        for name in names:
            rows //= axes[name].count
            rings.append(Ring(axes[name], [source], rows, *take(4)))
            source = out if name == names[-1] else take(1)[0]
            stores.append(source)
        chains.append(Chain(rings, stores))
    query, kv, out_chain = chains
    totals = [Total(axes[name], gains_ref, *take(3)) for name in FULL_AXES]
    signal_and_wait([device for axis in axes.values() for device in axis.neighbours()])

    quarter = x_ref.shape[0] // 4

    def load_mid_grad(part):
        band = slice(part * quarter, (part + 1) * quarter)
        return pltpu.make_async_copy(mg_hbm.at[band, :], mg_band.at[part % 2], mg_sem.at[part])

    load_mid_grad(0).start()
    load_mid_grad(1).start()
    load_down.start()
    piece.step()
    exchange.start()
    out_chain.step()
    downs[0].step()
    for start in range(0, MODEL_WIDTH, HALF):
        span = slice(start, start + HALF)
        wq_grad[span, :] = dot_tn(normed_ref[:, span], dql_ref[...]).astype(bf16)
    query.step()
    cosine, sine = cos_ref[...], sin_ref[...]
    for head in range(KEY_VALUE_HEADS):
        span = slice(head * HEAD_SIZE, (head + 1) * HEAD_SIZE)
        dkvl[:, span] = rotate_back(dkv_ref[:, span].astype(f32), cosine, sine).astype(bf16)
    dkvl[:, KV_WIDTH:] = dkv_ref[:, KV_WIDTH:]
    for start in range(0, MODEL_WIDTH, WIDTH_TILE):
        span = slice(start, start + WIDTH_TILE)
        wkv_grad[span, :] = dot_tn(normed_ref[:, span], dkvl[...]).astype(bf16)
    query.step(2)
    kv.step()
    piece.step()
    downs[0].step()
    dgain = jnp.zeros((1, MODEL_WIDTH), f32)
    for part in range(4):
        band = slice(part * quarter, (part + 1) * quarter)
        grad = dot_nt(dql_ref[band, :], wq_ref[...])
        grad += dot_nt(dkvl[band, :KV_WIDTH], wk_ref[...])
        grad += dot_nt(dkvl[band, KV_WIDTH:], wv_ref[...])
        x = x_ref[band, :].astype(f32)
        r = lax.rsqrt(jnp.mean(x * x, axis=-1, keepdims=True) + epsilon)
        v = grad * gain_ref[...]
        inner = jnp.mean(v * x, axis=-1, keepdims=True)
        dgain += jnp.sum(grad * x * r, axis=0, keepdims=True)
        load_mid_grad(part).wait()
        mid_grad = mg_band[part % 2]
        dx_ref[band, :] = (mid_grad + r * v - x * (r * r * r * inner)).astype(bf16)
        if part < 2:
            load_mid_grad(part + 2).start()
        if part == 1:
            kv.step()
    gains_ref[0:1, :] = dgain
    gains_ref[1:2, :] = ffn_gain_ref[...]
    gains_ref[2:, :] = jnp.zeros((GAIN_ROWS - 2, MODEL_WIDTH), f32)
    out_chain.step(2)
    piece.step()
    downs[0].step()
    totals[0].run()
    totals[1].run()
    query.step(2)
    kv.step()
    load_down.wait()
    exchange.wait_recv()
    downs[1].step()
    out_chain.step()
    piece.step()
    downs[0].step()
    totals[2].run()
    downs[1].step()
    out_chain.step()
    kv.step(2)
    query.step(2)
    downs[1].step()
    kv.step(2)
    totals[3].run()
    everything = [query, kv, downs[1], downs[0], out_chain, piece]
    while any(chain.done < len(chain.hops) for chain in everything):
        for chain in everything:
            chain.step()
    for chain in everything:
        chain.finish()
    exchange.wait_send()


def last_part(
    piece, down_sum, mine_down, other_down, dql, dkv, normed, wq, wk, wv, cosine, sine, x, gain,
    mg, ffn_gain_part, wo_sum,
):
    counts = sizes()
    n = counts["ctx"]
    share = MODEL_WIDTH // (2 * counts["chip"] * counts["dp"] * n)
    full = FULL_AXES if share % 16 == 0 else FULL_AXES[:3]
    widths = (MODEL_WIDTH, 2 * KV_WIDTH, MODEL_WIDTH)
    plan = [(full, MODEL_WIDTH), (full, MODEL_WIDTH), (full[2:], wo_sum.shape[0])]
    share, down_share = piece.shape[0] // n, mine_down.shape[1] // n
    shapes = [
        jax.ShapeDtypeStruct((share, 2 * FF), f32),
        jax.ShapeDtypeStruct((EXP_DEV, down_share, mine_down.shape[2]), f32),
        jax.ShapeDtypeStruct(x.shape, bf16),
        jax.ShapeDtypeStruct((GAIN_ROWS, MODEL_WIDTH), f32),
    ]
    scratch = [
        pltpu.VMEM((MODEL_WIDTH, MODEL_WIDTH), bf16),
        pltpu.VMEM((MODEL_WIDTH, 2 * KV_WIDTH), bf16),
        pltpu.VMEM((x.shape[0], 2 * KV_WIDTH), bf16),
        pltpu.VMEM((2, x.shape[0] // 4, MODEL_WIDTH), f32),
        pltpu.SemaphoreType.DMA((4,)),
    ]
    scratch += ring_buffers(n, 1, share, 2 * FF)
    scratch += [pltpu.VMEM(mine_down.shape[1:], bf16)] * 2 + [pltpu.SemaphoreType.DMA((3,))]
    for terms in (1, 2):
        scratch += ring_buffers(n, terms, down_share, mine_down.shape[2])
    for (names, rows), width in zip(plan, widths):
        for name in names:
            rows //= counts[name]
            scratch += ring_buffers(counts[name], 1, rows, width)
            if name != names[-1]:
                scratch.append(pltpu.VMEM((rows, width), bf16))
        shapes.append(jax.ShapeDtypeStruct((rows, width), f32 if "ctx" in names else bf16))
    for name in FULL_AXES:
        hops = counts[name] - 1
        scratch += [
            pltpu.VMEM((hops, GAIN_ROWS, MODEL_WIDTH), f32),
            pltpu.SemaphoreType.DMA((hops,)),
            pltpu.SemaphoreType.DMA((hops,)),
        ]
    vmem, hbm = pl.BlockSpec(memory_space=pltpu.VMEM), pl.BlockSpec(memory_space=pl.ANY)
    gate_up, down, dx, gains, *attention = pl.pallas_call(
        functools.partial(last_kernel, plan),
        in_specs=[vmem] * 2 + [hbm] * 2 + [vmem] * 10 + [hbm] + [vmem] * 2,
        out_specs=(vmem,) * 7,
        out_shape=tuple(shapes),
        scratch_shapes=scratch,
        compiler_params=params(collective_id=2, has_side_effects=True),
        cost_estimate=cost(1e10, 4e7),
        name="last_part",
    )(
        piece, down_sum, mine_down, other_down, dql, dkv, normed, wq, wk, wv, cosine, sine, x, gain,
        mg, ffn_gain_part, wo_sum,
    )
    if "ctx" not in full:
        attention = [
            scatter_axis(a.reshape(n, a.shape[0] // n, a.shape[1]), "ctx").astype(f32)
            for a in attention
        ]
    return gate_up, down, dx, gains, attention


def shifted(value, axis, steps):
    count = lax.axis_size(axis)
    return lax.ppermute(value, axis, [(i, (i + steps) % count) for i in range(count)])


def core_swap(value):
    return lax.ppermute(value, "exp", [(i, i ^ 1) for i in range(lax.axis_size("exp"))])


def chip_shift(value, steps):
    count = lax.axis_size("exp")
    return lax.ppermute(value, "exp", [(i, (i + 2 * steps) % count) for i in range(count)])


def return_blocks(parts):
    terms = [parts[0], core_swap(parts[1])]
    for steps in range(1, lax.axis_size("exp") // 2):
        crossed = core_swap(parts[2 * steps])
        both = (crossed.astype(f32) + parts[2 * steps + 1].astype(f32)).astype(bf16)
        terms.append(chip_shift(both, -steps))
    return terms


def ring_part(parts, index, count, step, axis=0):
    return lax.dynamic_index_in_dim(parts, (index - 1 - step) % count, axis, keepdims=False)


def add_low(a, b):
    return (a.astype(f32) + b.astype(f32)).astype(bf16)


def ring_scatter(parts, shift, index, count, axis=0):
    total = ring_part(parts, index, count, 0, axis)
    for step in range(1, count):
        total = add_low(shift(total), ring_part(parts, index, count, step, axis))
    return total


def by_owner(array, axis):
    dp, ctx, exp = (lax.axis_size(a) for a in ("dp", "ctx", "exp"))
    size = array.shape[axis]
    before, after = array.shape[:axis], array.shape[axis + 1 :]
    parts = array.reshape(*before, dp, ctx, exp // 2, 2, size // (dp * ctx * exp), *after)
    order = list(range(axis)) + [axis + i for i in (3, 2, 0, 1, 4)]
    order += list(range(axis + 5, parts.ndim))
    return jnp.transpose(parts, order).reshape(array.shape)


def scatter_axis(parts, axis):
    return ring_scatter(
        parts, lambda v: shifted(v, axis, 1), lax.axis_index(axis), lax.axis_size(axis)
    )


def tie(*values):
    return lax.optimization_barrier(values)


def per_device(
    tokens, attn_gain, w_query, key_matrix, value_matrix, w_out, ffn_gain, expert_gate_up,
    expert_down, expert_ids, gate_weights, span_order, out_grad,
):
    ctx_size, exp_size = lax.axis_size("ctx"), lax.axis_size("exp")
    ctx_here, exp_here = lax.axis_index("ctx"), lax.axis_index("exp")
    experts = EXP_DEV * exp_size
    x, g = tokens[0], out_grad[0]
    rows = x.shape[0]
    capacity = rows * TOPK * 5 // (4 * experts)
    gain_one, gain_two = attn_gain[None, :], ffn_gain[None, :]
    offsets = jnp.arange(HALF, dtype=jnp.int32)

    def device_positions(device):
        pair = lax.dynamic_slice_in_dim(span_order[0], 2 * device, 2, 0)
        return (pair[:, None] * HALF + offsets[None, :]).reshape(-1)

    sources = [(ctx_here - s) % ctx_size for s in range(ctx_size)]
    key_positions = [device_positions(s) for s in sources]
    positions = key_positions[0]
    exponent = jnp.arange(HEAD_SIZE // 2, dtype=f32) * (-2.0 / HEAD_SIZE)
    frequency = jnp.power(f32(rope_base), exponent)
    angles = positions.astype(f32)[:, None] * frequency[None, :]
    cosine, sine = jnp.cos(angles), jnp.sin(angles)
    cosine = jnp.concatenate([cosine, cosine], axis=1)
    sine = jnp.concatenate([-sine, sine], axis=1)

    named = expert_ids[0][:, :, None] == jnp.arange(experts, dtype=jnp.int32)
    member = jnp.any(named, axis=1)
    count = member.astype(jnp.int32)
    place = jnp.where(member, jnp.cumsum(count, axis=0) - count, -1)
    route_gate = jnp.sum(jnp.where(named, gate_weights[0][:, :, None], 0.0), axis=1)
    routing = jnp.stack([place.astype(f32), route_gate]).transpose(0, 2, 1)

    normed, q, kv, att, att_low, lse, mid, nf, g_all, routing_all = forward_to_experts(
        x, gain_one, key_matrix, value_matrix, cosine, sine, positions[:, None],
        jnp.stack(key_positions)[:, None, :], gain_two, w_query, w_out, g, routing,
    )
    routing = jnp.concatenate([routing[None], routing_all[1:]], axis=0)
    routing = lax.dynamic_slice_in_dim(routing, EXP_DEV * exp_here, EXP_DEV, 2)
    pos, gates = routing[:, 0].astype(jnp.int32), routing[:, 1]

    swapped = core_swap(nf)
    nf_blocks = [nf, swapped]
    nf, swapped = tie(nf, swapped)
    y_parts, dx_parts, kept = [], [], None
    for first in range(0, exp_size, 2):
        here = slice(first, first + 2)
        if first:
            same, dx_parts[-1] = tie(chip_shift(nf, first // 2), dx_parts[-1])
            nf_blocks += [core_swap(same), same]
        y_part, dx_part, kept = expert_blocks(
            first, exp_size, capacity, pos[here], gates[here], nf_blocks[here], g, g_all,
            expert_gate_up, expert_down, kept,
        )
        y_parts += y_part
        dx_parts += dx_part
    nf_grad_terms = return_blocks(dx_parts)
    slot_rows, hidden, slot_grad, projected_grad = (
        a.reshape(EXP_DEV, exp_size * capacity, a.shape[-1]) for a in kept
    )
    dp_size, dp_here = lax.axis_size("dp"), lax.axis_index("dp")
    half, down_half = MODEL_WIDTH // dp_size, FF // dp_size
    other = (dp_here - 1) % dp_size
    theirs = [weight_grad(0, 1, other, half, slot_rows, projected_grad)[0]]
    slot_rows, hidden, theirs = tie(slot_rows, hidden, theirs)
    came = shifted(theirs[0], "dp", 1)
    theirs.append(weight_grad(1, 1, other, half, slot_rows, projected_grad)[0])
    mine = [
        weight_grad(e, 1, dp_here, half, slot_rows, projected_grad)[0] for e in range(EXP_DEV)
    ]
    other_down = weight_grad(0, EXP_DEV, other, down_half, hidden, slot_grad)
    mine_down = weight_grad(0, EXP_DEV, dp_here, down_half, hidden, slot_grad)
    nf_grad_terms, mine, mine_down, other_down, y_parts, theirs = tie(
        nf_grad_terms, mine, mine_down, other_down, y_parts, theirs
    )

    mid_grad, mid_grad_low, att_grad, delta, ffn_gain_part = middle_backward(
        nf_grad_terms, mid, g, gain_two, w_out, att
    )
    mid_grad_low, came = tie(mid_grad_low, came)
    w_out_grad = by_owner(dot_tn(att_low, mid_grad_low).astype(bf16), 0)
    y_terms = return_blocks(y_parts)

    dql, dkv, gate_up_first, gate_up_next, down_sum, w_out_sum = attention_backward(
        q, att_grad, kv, lse, delta, jnp.stack(key_positions)[:, :, None], positions[None, :],
        cosine, sine, mine[0], came, w_out_grad, theirs[1], mine[1], other_down, mine_down,
    )
    gate_up_second, down_share, tokens_grad, gains, attention = last_part(
        gate_up_next, down_sum, mine_down, other_down, dql, dkv, by_owner(normed, 1), w_query, key_matrix,
        value_matrix, cosine, sine, x, gain_one, mid_grad, ffn_gain_part, w_out_sum,
    )
    w_query_share, w_kv_share, w_out_share = attention
    layer_output = mid
    for term in y_terms:
        layer_output = layer_output + term.astype(f32)
    layer_output = layer_output.astype(bf16)
    owner = (lax.axis_index("dp") * ctx_size + ctx_here) * exp_size + exp_here
    gain_share = MODEL_WIDTH // (dp_size * ctx_size * exp_size)
    gains = lax.dynamic_slice_in_dim(gains, owner * gain_share, gain_share, 1)
    return (
        layer_output[None],
        tokens_grad[None],
        gains[0],
        w_query_share,
        w_kv_share[:, :KV_WIDTH],
        w_kv_share[:, KV_WIDTH:],
        w_out_share,
        gains[1],
        jnp.stack([gate_up_first, gate_up_second]),
        down_share,
    )


def solution(mesh):
    by_row = P(("dp", "exp"), "ctx", None)
    share = P(("dp", "ctx", "exp"))
    share_rows = P(("dp", "ctx", "exp"), None)
    return jax.shard_map(
        per_device,
        mesh=mesh,
        in_specs=(
            by_row, P(), P(), P(), P(), P(), P(), P("exp", None, None), P("exp", None, None),
            by_row, by_row, P(("dp", "exp"), None), by_row,
        ),
        out_specs=(
            by_row, by_row, share, share_rows, share_rows, share_rows, share_rows, share,
            P("exp", ("dp", "ctx"), None), P("exp", ("dp", "ctx"), None),
        ),
        check_vma=False,
    )
```

```python
import functools
import math

import jax
import jax.numpy as jnp
from jax import lax
from jax.experimental import pallas as pl
from jax.experimental.pallas import tpu as pltpu
from jax.sharding import PartitionSpec as P

MODEL_WIDTH = 1536
QUERY_HEADS = 12
KEY_VALUE_HEADS = 2
GROUP = QUERY_HEADS // KEY_VALUE_HEADS
HEAD_SIZE = 128
KV_WIDTH = KEY_VALUE_HEADS * HEAD_SIZE
FF = 768
TOPK = 4
EXP_DEV = 2
TOK_DEV = 512
HALF = 256

epsilon = 1e-06
rope_base = 1000000.0
masked_score = -1e30
score_scale = HEAD_SIZE ** (-0.5)
score_to_log2 = score_scale * math.log2(math.e)
gelu_c = math.sqrt(2.0 / math.pi)

f32 = jnp.float32
bf16 = jnp.bfloat16
NT = (((1,), (1,)), ((), ()))
TN = (((0,), (0,)), ((), ()))
VMEM_BYTES = 63 * 1024 * 1024
MESH = pl.DeviceIdType.MESH


def dot(a, b):
    return jnp.dot(a, b, preferred_element_type=f32)


def dot_nt(a, b):
    return lax.dot_general(a, b, NT, preferred_element_type=f32)


def dot_tn(a, b):
    return lax.dot_general(a, b, TN, preferred_element_type=f32)


def params(**more):
    return pltpu.CompilerParams(vmem_limit_bytes=VMEM_BYTES, **more)


def cost(flops, size, exps=0):
    return pl.CostEstimate(flops=int(flops) // 32, bytes_accessed=int(size) // 32, transcendentals=int(exps) // 32)


def whole(shape):
    return pl.BlockSpec(shape, lambda *_: (0,) * len(shape))


def rotate(values, cosine, signed_sine):
    return values * cosine + pltpu.roll(values, HEAD_SIZE // 2, 1) * signed_sine


def rotate_back(values, cosine, signed_sine):
    return values * cosine - pltpu.roll(values, HEAD_SIZE // 2, 1) * signed_sine


HEAD_ROWS = 16


class Gather:
    def __init__(self, own, slots, send_sem, recv_sem):
        self.own, self.slots, self.send_sem, self.recv_sem = own, slots, send_sem, recv_sem
        self.chips = lax.axis_size("exp") // 2
        exp = lax.axis_index("exp")
        core, chip = lax.rem(exp, 2), exp // 2
        self.other = {"exp": chip * 2 + 1 - core}
        self.ahead = [
            {"exp": lax.rem(chip + s, self.chips) * 2 + core} for s in range(self.chips)
        ]
        self.behind = [
            {"exp": lax.rem(chip + self.chips - s, self.chips) * 2 + core}
            for s in range(self.chips)
        ]

    def neighbours(self):
        if self.chips == 2:
            return [self.other, self.ahead[1]]
        return [self.other] + self.ahead[1:]

    def copy(self, slot):
        source, device = self.own, self.other
        if slot > 1 and slot % 2 == 0:
            source = self.slots.at[slot + 1]
        elif slot > 1:
            device = self.ahead[slot // 2]
        return remote(
            source, self.slots.at[slot], self.send_sem.at[slot], self.recv_sem.at[slot], device
        )

    def keep(self):
        return pltpu.make_async_copy(self.own, self.slots.at[0], self.recv_sem.at[0])

    def start(self):
        self.copy(1).start()
        for s in range(1, self.chips):
            self.copy(2 * s + 1).start()

    def cross(self):
        for s in range(1, self.chips):
            self.copy(2 * s + 1).wait_recv()
            self.copy(2 * s).start()

    def finish(self):
        self.copy(1).wait_recv()
        for s in range(1, self.chips):
            self.copy(2 * s).wait_recv()
        self.finish_sends()

    def finish_sends(self):
        for slot in range(1, 2 * self.chips):
            self.copy(slot).wait_send()


def forward_kernel(
    n, x_ref, gain_ref, wk_ref, wv_ref, cos_ref, sin_ref, qpos_ref, kpos_ref, ffn_gain_ref, wq_hbm,
    wo_hbm, g_hbm, routing_hbm, normed_ref, q_ref, kv_ref, att_ref, att_low_ref, lse_ref, mid_ref,
    nf_ref, g_all, routing_all, wq_ref, wo_ref, tops, totals, load_sem, send_sem, recv_sem,
    g_send_sem, g_recv_sem, routing_send_sem, routing_recv_sem,
):
    load_q = pltpu.make_async_copy(wq_hbm, wq_ref, load_sem.at[0])
    load_o = pltpu.make_async_copy(wo_hbm, wo_ref, load_sem.at[1])
    load_q.start()
    load_o.start()
    ctx = Axis("ctx")
    gathers = [
        Gather(routing_hbm, routing_all, routing_send_sem, routing_recv_sem),
        Gather(g_hbm, g_all, g_send_sem, g_recv_sem),
    ]
    signal_and_wait(ctx.neighbours() + gathers[0].neighbours())
    for gather in gathers:
        gather.start()
        gather.keep().start()

    def pass_on(step):
        return remote(
            kv_ref.at[step], kv_ref.at[step + 1], send_sem.at[step], recv_sem.at[step], ctx.next
        )

    rows = x_ref.shape[0]
    x = x_ref[...].astype(f32)
    r = lax.rsqrt(jnp.mean(x * x, axis=-1, keepdims=True) + epsilon)
    normed_ref[...] = (x * r * gain_ref[...]).astype(bf16)
    normed = normed_ref[...]
    cosine, sine = cos_ref[...], sin_ref[...]
    keys = dot(normed, wk_ref[...])
    for head in range(KEY_VALUE_HEADS):
        span = slice(head * HEAD_SIZE, (head + 1) * HEAD_SIZE)
        kv_ref[0, :, span] = rotate(keys[:, span], cosine, sine).astype(bf16)
    kv_ref[0, :, KV_WIDTH:] = dot(normed, wv_ref[...]).astype(bf16)
    pass_on(0).start()
    load_q.wait()
    for start in range(0, MODEL_WIDTH, WIDTH_TILE):
        queries = dot(normed, wq_ref[:, start : start + WIDTH_TILE])
        for offset in range(0, WIDTH_TILE, HEAD_SIZE):
            span = slice(start + offset, start + offset + HEAD_SIZE)
            part = queries[:, offset : offset + HEAD_SIZE]
            q_ref[:, span] = rotate(part, cosine, sine).astype(bf16)

    for step in range(n):
        if step:
            pass_on(step - 1).wait_recv()
            if step < n - 1:
                pass_on(step).start()
        allowed = kpos_ref[step] <= qpos_ref[...]

        def one_group(group, carry):
            keys = kv_ref[step, :, pl.ds(pl.multiple_of(group * HEAD_SIZE, HEAD_SIZE), HEAD_SIZE)]
            start = pl.multiple_of(KV_WIDTH + group * HEAD_SIZE, HEAD_SIZE)
            values = kv_ref[step, :, pl.ds(start, HEAD_SIZE)]
            for member in range(GROUP):
                head = group * GROUP + member
                columns = pl.ds(pl.multiple_of(head * HEAD_SIZE, HEAD_SIZE), HEAD_SIZE)
                lane = slice(member, member + 1)
                scores = jnp.where(allowed, dot_nt(q_ref[:, columns], keys), masked_score)
                top = jnp.max(scores, axis=-1, keepdims=True) * score_to_log2
                if step:
                    before = tops[group, :, lane]
                    top = jnp.maximum(before, top)
                    rescale = jnp.exp2(before - top)
                weights = jnp.exp2(scores * score_to_log2 - top)
                total = jnp.sum(weights, axis=-1, keepdims=True)
                out = dot(weights.astype(bf16), values)
                if step:
                    total += totals[group, :, lane] * rescale
                    out += att_ref[:, columns] * rescale
                if step < n - 1:
                    tops[group, :, lane] = top
                    totals[group, :, lane] = total
                else:
                    out /= total
                    att_low_ref[:, columns] = out.astype(bf16)
                    tops[group, :, lane] = top + jnp.log2(total)
                att_ref[:, columns] = out
            return carry

        lax.fori_loop(0, KEY_VALUE_HEADS, one_group, 0)
    for group in range(KEY_VALUE_HEADS):
        lse_ref[group * GROUP : (group + 1) * GROUP, :] = tops[group].T[:GROUP, :]
    lse_ref[QUERY_HEADS:, :] = jnp.zeros((HEAD_ROWS - QUERY_HEADS, rows), f32)
    for gather in gathers:
        gather.cross()
    load_o.wait()
    half = rows // 2
    for part in range(2):
        band = slice(part * half, (part + 1) * half)
        mid = x_ref[band, :].astype(f32) + dot(att_low_ref[band, :], wo_ref[...])
        mid_ref[band, :] = mid
        r = lax.rsqrt(jnp.mean(mid * mid, axis=-1, keepdims=True) + epsilon)
        nf_ref[band, :] = (mid * r * ffn_gain_ref[...]).astype(bf16)
    for step in range(n - 1):
        pass_on(step).wait_send()
    for gather in gathers:
        gather.keep().wait()
        gather.finish()


def forward_to_experts(
    x, gain, wk, wv, cosine, sine, qpos_col, kpos_rows, ffn_gain, wq, wo, g, routing
):
    exp_size = lax.axis_size("exp")
    rows, n = x.shape[0], kpos_rows.shape[0]
    vmem = pl.BlockSpec(memory_space=pltpu.VMEM)
    hbm = pl.BlockSpec(memory_space=pl.ANY)
    wide = (rows, MODEL_WIDTH)
    return pl.pallas_call(
        functools.partial(forward_kernel, n),
        in_specs=[vmem] * 9 + [hbm] * 4,
        out_specs=(vmem,) * 8 + (hbm,) * 2,
        out_shape=(
            jax.ShapeDtypeStruct(wide, bf16),
            jax.ShapeDtypeStruct(wide, bf16),
            jax.ShapeDtypeStruct((n, rows, 2 * KV_WIDTH), bf16),
            jax.ShapeDtypeStruct(wide, f32),
            jax.ShapeDtypeStruct(wide, bf16),
            jax.ShapeDtypeStruct((HEAD_ROWS, rows), f32),
            jax.ShapeDtypeStruct(wide, f32),
            jax.ShapeDtypeStruct(wide, bf16),
            jax.ShapeDtypeStruct((exp_size, *g.shape), bf16),
            jax.ShapeDtypeStruct((exp_size, *routing.shape), f32),
        ),
        scratch_shapes=[
            pltpu.VMEM((MODEL_WIDTH, MODEL_WIDTH), bf16),
            pltpu.VMEM((MODEL_WIDTH, MODEL_WIDTH), bf16),
            pltpu.VMEM((KEY_VALUE_HEADS, rows, HEAD_SIZE), f32),
            pltpu.VMEM((KEY_VALUE_HEADS, rows, HEAD_SIZE), f32),
            pltpu.SemaphoreType.DMA((2,)),
            pltpu.SemaphoreType.DMA((n - 1,)),
            pltpu.SemaphoreType.DMA((n - 1,)),
        ]
        + [pltpu.SemaphoreType.DMA((exp_size,))] * 4,
        compiler_params=params(collective_id=3, has_side_effects=True),
        cost_estimate=cost(
            4 * n * rows * rows * MODEL_WIDTH + 5 * rows * MODEL_WIDTH * MODEL_WIDTH, 4e7,
            n * rows * rows * QUERY_HEADS,
        ),
        name="forward_to_experts",
    )(x, gain, wk, wv, cosine, sine, qpos_col, kpos_rows, ffn_gain, wq, wo, g, routing)


FF_TILE = 256
WIDTH_TILE = 512


def expert_kernel(
    pos_row_ref, pos_col_ref, gate_row_ref, nf_hbm, g_ref, wgu_ref, wd_ref, dx_chip, y_chip, dx_far,
    y_far, rows_ref, hidden_ref, slot_grad_ref, pg_ref, x_all, x_ref, place, result, rows_grad,
    dx_out, y_out, dx_came, y_came, load_sem, gather_send, gather_recv, back_send, back_recv,
):
    block, expert = pl.program_id(0), pl.program_id(1)
    capacity = rows_ref.shape[-2]
    tokens = x_ref.shape[0]
    gather = Gather(nf_hbm, x_all, gather_send, gather_recv)
    chips = gather.chips

    def load(source):
        copy = pltpu.make_async_copy(source, x_ref, load_sem.at[0])
        copy.start()
        copy.wait()

    def back(slot):
        return [
            remote(out, came.at[slot], back_send.at[i, slot], back_recv.at[i, slot], gather.other)
            for i, (out, came) in enumerate(((dx_out, dx_came), (y_out, y_came)))
        ]

    @pl.when((block == 0) & (expert == 0))
    def _():
        signal_and_wait(gather.neighbours())
        gather.start()
        load(nf_hbm)

    @pl.when((block == 1) & (expert == 0))
    def _():
        gather.copy(1).wait_recv()
        load(x_all.at[1])

    for s in range(1, chips):

        @pl.when((block == 2 * s) & (expert == 0))
        def _():
            if s == 1:
                gather.cross()
            gather.copy(2 * s).wait_recv()
            load(x_all.at[2 * s])

        @pl.when((block == 2 * s + 1) & (expert == 0))
        def _():
            load(x_all.at[2 * s + 1])

    slot_r = lax.broadcasted_iota(jnp.int32, (capacity, tokens), 0)
    slot_c = lax.broadcasted_iota(jnp.int32, (tokens, capacity), 1)
    match = slot_r == pos_row_ref[0, 0]
    pick = match.astype(bf16)
    place[expert] = (slot_c == pos_col_ref[0, 0]).astype(bf16)
    gates = jnp.sum(jnp.where(match, gate_row_ref[0, 0], 0.0), axis=1, keepdims=True)
    for start in range(0, MODEL_WIDTH, WIDTH_TILE):
        span = slice(start, start + WIDTH_TILE)
        rows_ref[0, 0, :, span] = dot(pick, x_ref[:, span]).astype(bf16)
        slot_grad_ref[0, 0, :, span] = (dot(pick, g_ref[0, :, span]) * gates).astype(bf16)
    rows = rows_ref[0, 0]
    slot_grad = slot_grad_ref[0, 0]
    for start in range(0, FF, FF_TILE):
        span = slice(start, start + FF_TILE)
        up_span = slice(FF + start, FF + start + FF_TILE)
        gate = dot(rows, wgu_ref[0, :, span])
        up = dot(rows, wgu_ref[0, :, up_span])
        hidden_grad = dot_nt(slot_grad, wd_ref[0, span, :])
        square = gate * gate
        tangent = jnp.tanh(gate * (gelu_c + (gelu_c * 0.044715) * square))
        half_plus = 0.5 + 0.5 * tangent
        activated = gate * half_plus
        slope = half_plus + activated * (1.0 - tangent) * (
            gelu_c + (3.0 * 0.044715 * gelu_c) * square
        )
        hidden_ref[0, 0, :, span] = (activated * up).astype(bf16)
        pg_ref[0, 0, :, span] = (hidden_grad * up * slope).astype(bf16)
        pg_ref[0, 0, :, up_span] = (hidden_grad * activated).astype(bf16)
    hidden = hidden_ref[0, 0]
    projected_grad = pg_ref[0, 0]
    for start in range(0, MODEL_WIDTH, WIDTH_TILE):
        span = slice(start, start + WIDTH_TILE)
        result[expert, :, span] = (dot(hidden, wd_ref[0, :, span]) * gates).astype(bf16)
        rows_grad[expert, :, span] = dot_nt(projected_grad, wgu_ref[0, span, :]).astype(bf16)

    last = expert == EXP_DEV - 1
    for sent in [1] + [2 * s for s in range(1, chips)]:

        @pl.when(last & (block == sent + 1))
        def _():
            for copy in back(sent // 2):
                copy.wait_send()

    @pl.when(last)
    def _():
        both = jnp.concatenate([place[e] for e in range(EXP_DEV)], axis=1)
        for start in range(0, MODEL_WIDTH, WIDTH_TILE):
            span = slice(start, start + WIDTH_TILE)
            for out_ref, terms in ((y_out, result), (dx_out, rows_grad)):
                stacked = terms[:, :, span].reshape(EXP_DEV * capacity, WIDTH_TILE)
                out_ref[:, span] = dot(both, stacked).astype(bf16)

    @pl.when(last & (block == 0))
    def _():
        dx_chip[...] = dx_out[...]
        y_chip[...] = y_out[...]

    for sent in [1] + [2 * s for s in range(1, chips)]:

        @pl.when(last & (block == sent))
        def _():
            for copy in back(sent // 2):
                copy.start()

    def add(target, own, came):
        for start in range(0, tokens, HEAD_SIZE):
            band = slice(start, start + HEAD_SIZE)
            total = own[band, :].astype(f32) + came[band, :].astype(f32)
            target[band, :] = total.astype(bf16)

    for s in range(1, chips):

        @pl.when(last & (block == 2 * s + 1))
        def _():
            for copy in back(s):
                copy.wait_recv()
            add(dx_far.at[s - 1], dx_out, dx_came.at[s])
            add(y_far.at[s - 1], y_out, y_came.at[s])

    @pl.when(last & (block == 2 * chips - 1))
    def _():
        for copy in back(0):
            copy.wait_recv()
        add(dx_chip, dx_chip, dx_came.at[0])
        add(y_chip, y_chip, y_came.at[0])
        gather.finish_sends()


def expert_blocks(capacity, pos, gates, nf, g_all, wgu, wd):
    blocks, tokens, _ = g_all.shape
    chips = blocks // 2
    kept_shapes = tuple(
        jax.ShapeDtypeStruct((EXP_DEV, blocks, capacity, width), bf16)
        for width in (MODEL_WIDTH, FF, MODEL_WIDTH, 2 * FF)
    )
    kept_specs = tuple(
        pl.BlockSpec((1, 1, capacity, s.shape[-1]), lambda b, e: (e, b, 0, 0)) for s in kept_shapes
    )
    flops = blocks * EXP_DEV * 2 * capacity * (4 * tokens * MODEL_WIDTH + 9 * MODEL_WIDTH * FF)
    wide = (tokens, MODEL_WIDTH)
    result = jax.ShapeDtypeStruct(wide, bf16)
    far = jax.ShapeDtypeStruct((chips - 1, *wide), bf16)
    hbm = pl.BlockSpec(memory_space=pl.ANY)

    def once(shape):
        return pl.BlockSpec(
            shape, lambda b, e: (0,) * len(shape), pipeline_mode=pl.Buffered(1)
        )

    return pl.pallas_call(
        expert_kernel,
        grid=(blocks, EXP_DEV),
        in_specs=[
            pl.BlockSpec((1, 1, 1, tokens), lambda b, e: (b, e, 0, 0)),
            pl.BlockSpec((1, 1, tokens, 1), lambda b, e: (b, e, 0, 0)),
            pl.BlockSpec((1, 1, 1, tokens), lambda b, e: (b, e, 0, 0)),
            hbm,
            pl.BlockSpec((1, tokens, MODEL_WIDTH), lambda b, e: (b, 0, 0)),
            pl.BlockSpec((1, MODEL_WIDTH, 2 * FF), lambda b, e: (e, 0, 0)),
            pl.BlockSpec((1, FF, MODEL_WIDTH), lambda b, e: (e, 0, 0)),
        ],
        out_specs=(once(wide), once(wide), once(far.shape), once(far.shape)) + kept_specs + (hbm,),
        out_shape=(result, result, far, far)
        + kept_shapes
        + (jax.ShapeDtypeStruct((blocks, *wide), bf16),),
        scratch_shapes=[
            pltpu.VMEM(wide, bf16),
            pltpu.VMEM((EXP_DEV, tokens, capacity), bf16),
            pltpu.VMEM((EXP_DEV, capacity, MODEL_WIDTH), bf16),
            pltpu.VMEM((EXP_DEV, capacity, MODEL_WIDTH), bf16),
            pltpu.VMEM(wide, bf16),
            pltpu.VMEM(wide, bf16),
            pltpu.VMEM((chips, *wide), bf16),
            pltpu.VMEM((chips, *wide), bf16),
            pltpu.SemaphoreType.DMA((1,)),
            pltpu.SemaphoreType.DMA((blocks,)),
            pltpu.SemaphoreType.DMA((blocks,)),
            pltpu.SemaphoreType.DMA((2, chips)),
            pltpu.SemaphoreType.DMA((2, chips)),
        ],
        compiler_params=params(collective_id=4, has_side_effects=True),
        cost_estimate=cost(flops, 6e7),
        name="expert_blocks",
    )(pos[:, :, None, :], pos[:, :, :, None], gates[:, :, None, :], nf, g_all, wgu, wd)


GRAD_TILE = 384


def weight_grad_kernel(chunk_ref, a_ref, b_ref, out_ref):
    out_ref[0] = dot_tn(a_ref[0], b_ref[0]).astype(bf16)


def weight_grad(first, experts, chunk, size, a, b):
    slots, width = a.shape[1], b.shape[-1]
    tiles = size // GRAD_TILE
    return pl.pallas_call(
        weight_grad_kernel,
        grid_spec=pltpu.PrefetchScalarGridSpec(
            num_scalar_prefetch=1,
            grid=(experts, tiles),
            in_specs=[
                pl.BlockSpec((1, slots, GRAD_TILE), lambda e, t, c: (first + e, 0, c[0] * tiles + t)),
                pl.BlockSpec((1, slots, width), lambda e, t, c: (first + e, 0, 0)),
            ],
            out_specs=pl.BlockSpec((1, GRAD_TILE, width), lambda e, t, c: (e, t, 0)),
        ),
        out_shape=jax.ShapeDtypeStruct((experts, size, width), bf16),
        compiler_params=params(),
        cost_estimate=cost(2 * experts * slots * size * width, 2e7),
        name="weight_grad",
    )(chunk.reshape(1).astype(jnp.int32), a, b)


def other_weight_grads_kernel(
    dp_ref, rows_ref, pg_ref, hidden_ref, slot_grad_ref, theirs_ref, mine0_ref, mine1_ref,
    other_down_ref, mine_down_ref,
):
    step = pl.program_id(0)
    for first, out_ref in ((0, theirs_ref), (2, mine0_ref), (4, mine1_ref)):

        @pl.when((step == first) | (step == first + 1))
        def _():
            out_ref[...] = dot_tn(rows_ref[0], pg_ref[0]).astype(bf16)

    for place, out_ref in enumerate((other_down_ref, mine_down_ref)):

        @pl.when((step == 6 + place) | (step == 8 + place))
        def _():
            out_ref[0] = dot_tn(hidden_ref[0], slot_grad_ref[0]).astype(bf16)


def other_weight_grads(dp_here, dp_size, slot_rows, pg, hidden, slot_grad):
    assert dp_size == 2 and MODEL_WIDTH // dp_size == 2 * GRAD_TILE and FF // dp_size == GRAD_TILE
    slots = slot_rows.shape[1]
    half = (2 * GRAD_TILE, 2 * FF)

    def gate_up_rows(t, d):
        t = jnp.minimum(t, 5)
        expert = jnp.where((t == 2) | (t == 3), 0, 1)
        place = jnp.where(t < 2, 1 - d[0], d[0])
        return expert, 0, place * 2 + t % 2

    def gate_up_right(t, d):
        return gate_up_rows(t, d)[0], 0, 0

    def down_rows(t, d):
        t = jnp.maximum(t, 6) - 6
        return t // 2, 0, jnp.where(t % 2 == 0, 1 - d[0], d[0])

    def down_right(t, d):
        return down_rows(t, d)[0], 0, 0

    def piece(first):
        return pl.BlockSpec((GRAD_TILE, 2 * FF), lambda t, d: (jnp.clip(t - first, 0, 1), 0))

    def down(first):
        return pl.BlockSpec(
            (1, GRAD_TILE, MODEL_WIDTH), lambda t, d: (jnp.clip((t - first) // 2, 0, 1), 0, 0)
        )

    return pl.pallas_call(
        other_weight_grads_kernel,
        grid_spec=pltpu.PrefetchScalarGridSpec(
            num_scalar_prefetch=1,
            grid=(10,),
            in_specs=[
                pl.BlockSpec((1, slots, GRAD_TILE), gate_up_rows),
                pl.BlockSpec((1, slots, 2 * FF), gate_up_right),
                pl.BlockSpec((1, slots, GRAD_TILE), down_rows),
                pl.BlockSpec((1, slots, MODEL_WIDTH), down_right),
            ],
            out_specs=(piece(0), piece(2), piece(4), down(6), down(7)),
        ),
        out_shape=(jax.ShapeDtypeStruct(half, bf16),) * 3
        + (jax.ShapeDtypeStruct((EXP_DEV, GRAD_TILE, MODEL_WIDTH), bf16),) * 2,
        compiler_params=params(),
        cost_estimate=cost(10 * 2 * slots * GRAD_TILE * 2 * FF, 5e7),
        name="other_weight_grads",
    )(dp_here.reshape(1).astype(jnp.int32), slot_rows, pg, hidden, slot_grad)


def middle_kernel(*refs):
    count = len(refs) - 11
    parts = refs[:count]
    mid_ref, g_ref, gain_ref, wo_ref, att_ref = refs[count : count + 5]
    mg_ref, mgl_ref, ag_ref, delta_ref, dgain_ref, delta_cols = refs[count + 5 :]
    rows = mid_ref.shape[0]
    half = rows // 2
    lane = lax.broadcasted_iota(jnp.int32, (half, HEAD_SIZE), 1)
    dgain = jnp.zeros((1, MODEL_WIDTH), f32)
    for part in range(2):
        band = slice(part * half, (part + 1) * half)
        nf_grad = parts[0][band, :].astype(f32)
        for other in parts[1:]:
            nf_grad += other[band, :].astype(f32)
        mid = mid_ref[band, :]
        r = lax.rsqrt(jnp.mean(mid * mid, axis=-1, keepdims=True) + epsilon)
        u = nf_grad * gain_ref[...]
        inner = jnp.mean(u * mid, axis=-1, keepdims=True)
        grad = g_ref[band, :].astype(f32) + r * u - mid * (r * r * r * inner)
        dgain += jnp.sum(nf_grad * mid * r, axis=0, keepdims=True)
        mg_ref[band, :] = grad
        low = grad.astype(bf16)
        mgl_ref[band, :] = low
        att_grad = dot_nt(low, wo_ref[...]).astype(bf16)
        ag_ref[band, :] = att_grad
        delta = jnp.zeros((half, HEAD_SIZE), f32)
        for head in range(QUERY_HEADS):
            span = slice(head * HEAD_SIZE, (head + 1) * HEAD_SIZE)
            one = jnp.sum(att_grad[:, span].astype(f32) * att_ref[band, span], axis=-1, keepdims=True)
            delta = jnp.where(lane == head, one, delta)
        delta_cols[band, :] = delta
    dgain_ref[...] = dgain
    delta_ref[...] = delta_cols[...].T[: delta_ref.shape[0], :]


def middle_backward(parts, mid, g, gain, wo, att):
    rows = mid.shape[0]
    return pl.pallas_call(
        middle_kernel,
        out_shape=(
            jax.ShapeDtypeStruct((rows, MODEL_WIDTH), f32),
            jax.ShapeDtypeStruct((rows, MODEL_WIDTH), bf16),
            jax.ShapeDtypeStruct((rows, MODEL_WIDTH), bf16),
            jax.ShapeDtypeStruct((HEAD_ROWS, rows), f32),
            jax.ShapeDtypeStruct((1, MODEL_WIDTH), f32),
        ),
        scratch_shapes=[pltpu.VMEM((rows, HEAD_SIZE), f32)],
        compiler_params=params(),
        cost_estimate=cost(2 * rows * MODEL_WIDTH * MODEL_WIDTH, 2e7),
        name="middle_backward",
    )(*parts, mid, g, gain, wo, att)


def signal_and_wait(neighbours):
    barrier = pltpu.get_barrier_semaphore()
    for neighbour in neighbours:
        pl.semaphore_signal(barrier, inc=1, device_id=neighbour, device_id_type=MESH)
    pl.semaphore_wait(barrier, len(neighbours))


def remote(source, target, send_sem, recv_sem, device):
    return pltpu.make_async_remote_copy(
        src_ref=source, dst_ref=target, send_sem=send_sem, recv_sem=recv_sem,
        device_id=device, device_id_type=MESH,
    )


class Axis:
    def __init__(self, name):
        if name in ("dp", "ctx"):
            self.count, self.me = lax.axis_size(name), lax.axis_index(name)
            place = lambda i: {name: i}
        else:
            exp = lax.axis_index("exp")
            core, chip = lax.rem(exp, 2), exp // 2
            if name == "core":
                self.count, self.me = 2, core
                place = lambda i: {"exp": chip * 2 + i}
            else:
                self.count, self.me = lax.axis_size("exp") // 2, chip
                place = lambda i: {"exp": i * 2 + core}
        self.next = place(lax.rem(self.me + 1, self.count))
        self.last = place(lax.rem(self.me + self.count - 1, self.count))

    def neighbours(self):
        return [self.next] if self.count == 2 else [self.next, self.last]


class Ring:
    def __init__(self, axis, terms, rows, send, recv, send_sem, recv_sem):
        self.axis, self.count, self.terms, self.rows = axis, axis.count, terms, rows
        self.send, self.recv, self.send_sem, self.recv_sem = send, recv, send_sem, recv_sem

    def here(self, hop):
        part = lax.rem(self.axis.me + self.count - 1 - hop, self.count)
        return pl.ds(pl.multiple_of(part * self.rows, self.rows), self.rows)

    def copy(self, hop):
        if len(self.terms) > 1:
            source = self.send.at[hop]
        elif hop == 0:
            source = self.terms[0].at[self.here(0), :]
        else:
            source = self.send.at[hop - 1]
        return remote(
            source, self.recv.at[hop], self.send_sem.at[hop], self.recv_sem.at[hop], self.axis.next
        )

    def hop(self, hop):
        if hop == 0 and len(self.terms) == 1:
            self.copy(0).start()
            return None
        here = self.here(hop)
        total = self.terms[0][here, :].astype(f32)
        for term in self.terms[1:]:
            total += term[here, :].astype(f32)
        if hop:
            self.copy(hop - 1).wait_recv()
            total += self.recv[hop - 1].astype(f32)
        if hop < self.count - 1:
            self.send[hop - (len(self.terms) == 1)] = total.astype(bf16)
            self.copy(hop).start()
        return total

    def finish(self):
        for hop in range(self.count - 1):
            self.copy(hop).wait_send()


def attention_back_kernel(
    n, q_ref, ag_ref, kv_ref, lse_ref, delta_ref, kpos_ref, qpos_ref, cos_ref, sin_ref, mine_ref,
    came_ref, wo_grad_ref, next_ref, next_mine_ref, down_ref, down_mine_ref, dql_ref, dkv_ref,
    share_ref, next_sum_ref, down_sum_ref, wo_sum_ref, next_came, down_came, next_mine, down_mine,
    dq_acc, held, send, recv, send_sem, recv_sem, next_sem, *scratch,
):
    ctx, core, chip = Axis("ctx"), Axis("core"), Axis("chip")
    right, across = ctx.next, Axis("dp").next
    signal_and_wait(ctx.neighbours() + core.neighbours() + chip.neighbours() + [across])
    core_rows = wo_grad_ref.shape[0] // 2
    wo_chain = Chain(
        [
            Ring(core, [wo_grad_ref], core_rows, *scratch[:4]),
            Ring(chip, [scratch[4]], core_rows // chip.count, *scratch[5:9]),
        ],
        [scratch[4], wo_sum_ref],
    )
    ring = Ring(ctx, [mine_ref, came_ref], share_ref.shape[0], *scratch[9:])
    ring.hop(0)
    wo_chain.step()
    exchanges, loads = [], []
    for i, (source, target, mine_hbm, mine) in enumerate(
        (
            (next_ref, next_came, next_mine_ref, next_mine),
            (down_ref.at[0], down_came, down_mine_ref.at[0], down_mine),
        )
    ):
        exchanges.append(remote(source, target, next_sem.at[i, 0], next_sem.at[i, 1], across))
        loads.append(pltpu.make_async_copy(mine_hbm, mine, next_sem.at[i, 2]))
        exchanges[i].start()
        loads[i].start()
    def dkv_copy(step, group):
        return remote(
            send.at[group, step], recv.at[group, step], send_sem.at[group, step],
            recv_sem.at[group, step], right,
        )

    for step in range(n):
        back = (step + 1) % n
        kpos = kpos_ref[back]

        def one_group(group, carry):
            keys = kv_ref[back, :, pl.ds(pl.multiple_of(group * HEAD_SIZE, HEAD_SIZE), HEAD_SIZE)]
            start = pl.multiple_of(KV_WIDTH + group * HEAD_SIZE, HEAD_SIZE)
            values = kv_ref[back, :, pl.ds(start, HEAD_SIZE)]
            dk = dv = None
            for member in range(GROUP):
                head = group * GROUP + member
                columns = pl.ds(pl.multiple_of(head * HEAD_SIZE, HEAD_SIZE), HEAD_SIZE)
                q, ag = q_ref[:, columns], ag_ref[:, columns]
                scores = dot_nt(keys, q)
                weights = jnp.exp2(scores * score_to_log2 - lse_ref[pl.ds(head, 1), :])
                weights = jnp.where(kpos <= qpos_ref[...], weights, 0.0)
                weights_grad = dot_nt(values, ag)
                score_grad = weights * (weights_grad - delta_ref[pl.ds(head, 1), :]) * score_scale
                score_grad = score_grad.astype(bf16)
                dv_part = dot(weights.astype(bf16), ag)
                dk_part = dot(score_grad, q)
                dv = dv_part if dv is None else dv + dv_part
                dk = dk_part if dk is None else dk + dk_part
                dq = dot_tn(score_grad, keys)
                if step:
                    dq += dq_acc[:, columns]
                dq_acc[:, columns] = dq
            held[group] = jnp.concatenate([dk, dv], axis=1)
            return carry

        lax.fori_loop(0, KEY_VALUE_HEADS, one_group, 0)
        for group in range(KEY_VALUE_HEADS):
            dkv = held[group]
            if step:
                dkv_copy(step - 1, group).wait_recv()
                dkv += recv[group, step - 1].astype(f32)
            if step < n - 1:
                send[group, step] = dkv.astype(bf16)
                dkv_copy(step, group).start()
            else:
                for place in range(2):
                    start = place * KV_WIDTH + group * HEAD_SIZE
                    part = dkv[:, place * HEAD_SIZE : (place + 1) * HEAD_SIZE]
                    dkv_ref[:, start : start + HEAD_SIZE] = part.astype(bf16)
        if step < n - 2:
            ring.hop(step + 1)
        wo_chain.step(2 if step == 0 else 1)
    cosine, sine = cos_ref[...], sin_ref[...]
    for head in range(QUERY_HEADS):
        span = slice(head * HEAD_SIZE, (head + 1) * HEAD_SIZE)
        dql_ref[:, span] = rotate_back(dq_acc[:, span], cosine, sine).astype(bf16)
    share_ref[...] = ring.hop(n - 1)
    ring.finish()
    for step in range(n - 1):
        for group in range(KEY_VALUE_HEADS):
            dkv_copy(step, group).wait_send()
    wo_chain.step(len(wo_chain.hops))
    wo_chain.finish()
    for i, (sum_ref, mine, came) in enumerate(
        ((next_sum_ref, next_mine, next_came), (down_sum_ref, down_mine, down_came))
    ):
        loads[i].wait()
        exchanges[i].wait()
        for start in range(0, sum_ref.shape[0], HEAD_SIZE):
            band = slice(start, start + HEAD_SIZE)
            total = mine[band, :].astype(f32) + came[band, :].astype(f32)
            sum_ref[band, :] = total.astype(bf16)


def attention_backward(
    q, ag, kv, lse, delta, kpos, qpos_row, cosine, sine, mine, came, w_out_grad, following,
    following_mine, other_down, mine_down,
):
    n, keys, _ = kv.shape
    rows = q.shape[0]
    chips = sizes()["chip"]
    wo_rows = w_out_grad.shape[0] // 2
    vmem = pl.BlockSpec(memory_space=pltpu.VMEM)
    hbm = pl.BlockSpec(memory_space=pl.ANY)
    return pl.pallas_call(
        functools.partial(attention_back_kernel, n),
        in_specs=[vmem] * 12 + [hbm] * 4,
        out_specs=(vmem,) * 6,
        out_shape=(
            jax.ShapeDtypeStruct((rows, MODEL_WIDTH), bf16),
            jax.ShapeDtypeStruct((keys, 2 * KV_WIDTH), bf16),
            jax.ShapeDtypeStruct((mine.shape[0] // n, mine.shape[1]), f32),
            jax.ShapeDtypeStruct(following.shape, bf16),
            jax.ShapeDtypeStruct(other_down.shape[1:], bf16),
            jax.ShapeDtypeStruct((wo_rows // chips, MODEL_WIDTH), bf16),
        ),
        scratch_shapes=[
            pltpu.VMEM(following.shape, bf16),
            pltpu.VMEM(other_down.shape[1:], bf16),
            pltpu.VMEM(following.shape, bf16),
            pltpu.VMEM(other_down.shape[1:], bf16),
            pltpu.VMEM((rows, MODEL_WIDTH), f32),
            pltpu.VMEM((KEY_VALUE_HEADS, keys, 2 * HEAD_SIZE), f32),
            pltpu.VMEM((KEY_VALUE_HEADS, n - 1, keys, 2 * HEAD_SIZE), bf16),
            pltpu.VMEM((KEY_VALUE_HEADS, n - 1, keys, 2 * HEAD_SIZE), bf16),
            pltpu.SemaphoreType.DMA((KEY_VALUE_HEADS, n - 1)),
            pltpu.SemaphoreType.DMA((KEY_VALUE_HEADS, n - 1)),
            pltpu.SemaphoreType.DMA((2, 3)),
        ]
        + ring_buffers(2, 1, wo_rows, MODEL_WIDTH)
        + [pltpu.VMEM((wo_rows, MODEL_WIDTH), bf16)]
        + ring_buffers(chips, 1, wo_rows // chips, MODEL_WIDTH)
        + ring_buffers(n, 2, mine.shape[0] // n, mine.shape[1]),
        compiler_params=params(collective_id=1, has_side_effects=True),
        cost_estimate=cost(10 * n * rows * keys * MODEL_WIDTH, 4e7, n * rows * keys * QUERY_HEADS),
        name="attention_backward",
    )(
        q, ag, kv, lse, delta, kpos, qpos_row, cosine, sine, mine, came, w_out_grad, following,
        following_mine, other_down, mine_down,
    )


def ring_buffers(count, terms, rows, width):
    sends = count - 1 if terms > 1 else count - 2
    return [
        pltpu.VMEM((sends, rows, width) if sends else (16, HEAD_SIZE), bf16),
        pltpu.VMEM((count - 1, rows, width), bf16),
        pltpu.SemaphoreType.DMA((count - 1,)),
        pltpu.SemaphoreType.DMA((count - 1,)),
    ]


class Chain:
    def __init__(self, rings, stores):
        self.hops = [(r, h) for r in range(len(rings)) for h in range(rings[r].count)]
        self.rings, self.stores, self.done = rings, stores, 0

    def step(self, times=1):
        for _ in range(times):
            if self.done == len(self.hops):
                return
            index, hop = self.hops[self.done]
            self.done += 1
            ring = self.rings[index]
            total = ring.hop(hop)
            if hop == ring.count - 1:
                store = self.stores[index]
                store[...] = total.astype(store.dtype)

    def finish(self):
        assert self.done == len(self.hops)
        for ring in self.rings:
            ring.finish()


FULL_AXES = ("core", "chip", "dp", "ctx")


def sizes():
    exp = lax.axis_size("exp")
    return {"core": 2, "chip": exp // 2, "dp": lax.axis_size("dp"), "ctx": lax.axis_size("ctx")}


class Total:
    def __init__(self, axis, value, recv, send_sem, recv_sem):
        self.axis, self.value, self.recv = axis, value, recv
        self.send_sem, self.recv_sem = send_sem, recv_sem

    def copy(self, hop):
        source = self.recv.at[hop - 1] if hop else self.value
        return remote(
            source, self.recv.at[hop], self.send_sem.at[hop], self.recv_sem.at[hop], self.axis.next
        )

    def run(self):
        count = self.axis.count
        self.copy(0).start()
        total = self.value[...]
        for hop in range(1, count):
            self.copy(hop - 1).wait_recv()
            total += self.recv[hop - 1]
            if hop < count - 1:
                self.copy(hop).start()
        for hop in range(count - 1):
            self.copy(hop).wait_send()
        self.value[...] = total


GAIN_ROWS = 8


def last_kernel(
    plan, piece_ref, down_sum_ref, mine_down_ref, other_down_ref, dql_ref, dkv_ref, normed_ref, wq_ref,
    wk_ref, wv_ref, cos_ref, sin_ref, x_ref, gain_ref, mg_hbm, ffn_gain_ref, wo_sum_ref,
    gate_up_ref, down_ref, dx_ref, gains_ref, wq_out, wkv_out, wo_out, wq_grad, wkv_grad, dkvl,
    mg_band, mg_sem, *scratch,
):
    scratch = list(scratch)

    def take(number):
        taken = scratch[:number]
        del scratch[:number]
        return taken

    axes = {name: Axis(name) for name in FULL_AXES}
    across = axes["dp"].next
    piece = Chain(
        [Ring(axes["ctx"], [piece_ref], gate_up_ref.shape[0], *take(4))], [gate_up_ref]
    )
    came_down, mine_down, down_sem = take(3)
    exchange = remote(
        other_down_ref.at[1], came_down, down_sem.at[0], down_sem.at[1], across
    )
    load_down = pltpu.make_async_copy(mine_down_ref.at[1], mine_down, down_sem.at[2])
    downs = [
        Chain([Ring(axes["ctx"], terms, down_ref.shape[1], *take(4))], [down_ref.at[expert]])
        for expert, terms in enumerate(([down_sum_ref], [mine_down, came_down]))
    ]
    chains = []
    for (names, rows), array, out in zip(
        plan, (wq_grad, wkv_grad, wo_sum_ref), (wq_out, wkv_out, wo_out)
    ):
        rings, stores, source = [], [], array
        for name in names:
            rows //= axes[name].count
            rings.append(Ring(axes[name], [source], rows, *take(4)))
            source = out if name == names[-1] else take(1)[0]
            stores.append(source)
        chains.append(Chain(rings, stores))
    query, kv, out_chain = chains
    totals = [Total(axes[name], gains_ref, *take(3)) for name in FULL_AXES]
    signal_and_wait([device for axis in axes.values() for device in axis.neighbours()])

    quarter = x_ref.shape[0] // 4

    def load_mid_grad(part):
        band = slice(part * quarter, (part + 1) * quarter)
        return pltpu.make_async_copy(mg_hbm.at[band, :], mg_band.at[part % 2], mg_sem.at[part])

    load_mid_grad(0).start()
    load_mid_grad(1).start()
    load_down.start()
    piece.step()
    exchange.start()
    out_chain.step()
    downs[0].step()
    for start in range(0, MODEL_WIDTH, HALF):
        span = slice(start, start + HALF)
        wq_grad[span, :] = dot_tn(normed_ref[:, span], dql_ref[...]).astype(bf16)
    query.step()
    cosine, sine = cos_ref[...], sin_ref[...]
    for head in range(KEY_VALUE_HEADS):
        span = slice(head * HEAD_SIZE, (head + 1) * HEAD_SIZE)
        dkvl[:, span] = rotate_back(dkv_ref[:, span].astype(f32), cosine, sine).astype(bf16)
    dkvl[:, KV_WIDTH:] = dkv_ref[:, KV_WIDTH:]
    for start in range(0, MODEL_WIDTH, WIDTH_TILE):
        span = slice(start, start + WIDTH_TILE)
        wkv_grad[span, :] = dot_tn(normed_ref[:, span], dkvl[...]).astype(bf16)
    query.step(2)
    kv.step()
    piece.step()
    downs[0].step()
    dgain = jnp.zeros((1, MODEL_WIDTH), f32)
    for part in range(4):
        band = slice(part * quarter, (part + 1) * quarter)
        grad = dot_nt(dql_ref[band, :], wq_ref[...])
        grad += dot_nt(dkvl[band, :KV_WIDTH], wk_ref[...])
        grad += dot_nt(dkvl[band, KV_WIDTH:], wv_ref[...])
        x = x_ref[band, :].astype(f32)
        r = lax.rsqrt(jnp.mean(x * x, axis=-1, keepdims=True) + epsilon)
        v = grad * gain_ref[...]
        inner = jnp.mean(v * x, axis=-1, keepdims=True)
        dgain += jnp.sum(grad * x * r, axis=0, keepdims=True)
        load_mid_grad(part).wait()
        mid_grad = mg_band[part % 2]
        dx_ref[band, :] = (mid_grad + r * v - x * (r * r * r * inner)).astype(bf16)
        if part < 2:
            load_mid_grad(part + 2).start()
        if part == 1:
            kv.step()
    gains_ref[0:1, :] = dgain
    gains_ref[1:2, :] = ffn_gain_ref[...]
    gains_ref[2:, :] = jnp.zeros((GAIN_ROWS - 2, MODEL_WIDTH), f32)
    out_chain.step(2)
    piece.step()
    downs[0].step()
    totals[0].run()
    totals[1].run()
    query.step(2)
    kv.step()
    load_down.wait()
    exchange.wait_recv()
    downs[1].step()
    out_chain.step()
    piece.step()
    downs[0].step()
    totals[2].run()
    downs[1].step()
    out_chain.step()
    kv.step(2)
    query.step(2)
    downs[1].step()
    kv.step(2)
    totals[3].run()
    everything = [query, kv, downs[1], downs[0], out_chain, piece]
    while any(chain.done < len(chain.hops) for chain in everything):
        for chain in everything:
            chain.step()
    for chain in everything:
        chain.finish()
    exchange.wait_send()


def last_part(
    piece, down_sum, mine_down, other_down, dql, dkv, normed, wq, wk, wv, cosine, sine, x, gain,
    mg, ffn_gain_part, wo_sum,
):
    counts = sizes()
    n = counts["ctx"]
    share = MODEL_WIDTH // (2 * counts["chip"] * counts["dp"] * n)
    full = FULL_AXES if share % 16 == 0 else FULL_AXES[:3]
    widths = (MODEL_WIDTH, 2 * KV_WIDTH, MODEL_WIDTH)
    plan = [(full, MODEL_WIDTH), (full, MODEL_WIDTH), (full[2:], wo_sum.shape[0])]
    share, down_share = piece.shape[0] // n, mine_down.shape[1] // n
    shapes = [
        jax.ShapeDtypeStruct((share, 2 * FF), f32),
        jax.ShapeDtypeStruct((EXP_DEV, down_share, mine_down.shape[2]), f32),
        jax.ShapeDtypeStruct(x.shape, bf16),
        jax.ShapeDtypeStruct((GAIN_ROWS, MODEL_WIDTH), f32),
    ]
    scratch = [
        pltpu.VMEM((MODEL_WIDTH, MODEL_WIDTH), bf16),
        pltpu.VMEM((MODEL_WIDTH, 2 * KV_WIDTH), bf16),
        pltpu.VMEM((x.shape[0], 2 * KV_WIDTH), bf16),
        pltpu.VMEM((2, x.shape[0] // 4, MODEL_WIDTH), f32),
        pltpu.SemaphoreType.DMA((4,)),
    ]
    scratch += ring_buffers(n, 1, share, 2 * FF)
    scratch += [pltpu.VMEM(mine_down.shape[1:], bf16)] * 2 + [pltpu.SemaphoreType.DMA((3,))]
    for terms in (1, 2):
        scratch += ring_buffers(n, terms, down_share, mine_down.shape[2])
    for (names, rows), width in zip(plan, widths):
        for name in names:
            rows //= counts[name]
            scratch += ring_buffers(counts[name], 1, rows, width)
            if name != names[-1]:
                scratch.append(pltpu.VMEM((rows, width), bf16))
        shapes.append(jax.ShapeDtypeStruct((rows, width), f32 if "ctx" in names else bf16))
    for name in FULL_AXES:
        hops = counts[name] - 1
        scratch += [
            pltpu.VMEM((hops, GAIN_ROWS, MODEL_WIDTH), f32),
            pltpu.SemaphoreType.DMA((hops,)),
            pltpu.SemaphoreType.DMA((hops,)),
        ]
    vmem, hbm = pl.BlockSpec(memory_space=pltpu.VMEM), pl.BlockSpec(memory_space=pl.ANY)
    gate_up, down, dx, gains, *attention = pl.pallas_call(
        functools.partial(last_kernel, plan),
        in_specs=[vmem] * 2 + [hbm] * 2 + [vmem] * 10 + [hbm] + [vmem] * 2,
        out_specs=(vmem,) * 7,
        out_shape=tuple(shapes),
        scratch_shapes=scratch,
        compiler_params=params(collective_id=2, has_side_effects=True),
        cost_estimate=cost(1e10, 4e7),
        name="last_part",
    )(
        piece, down_sum, mine_down, other_down, dql, dkv, normed, wq, wk, wv, cosine, sine, x, gain,
        mg, ffn_gain_part, wo_sum,
    )
    if "ctx" not in full:
        attention = [
            scatter_axis(a.reshape(n, a.shape[0] // n, a.shape[1]), "ctx").astype(f32)
            for a in attention
        ]
    return gate_up, down, dx, gains, attention


def shifted(value, axis, steps):
    count = lax.axis_size(axis)
    return lax.ppermute(value, axis, [(i, (i + steps) % count) for i in range(count)])


def chip_shift(value, steps):
    count = lax.axis_size("exp")
    return lax.ppermute(value, "exp", [(i, (i + 2 * steps) % count) for i in range(count)])


def ring_part(parts, index, count, step, axis=0):
    return lax.dynamic_index_in_dim(parts, (index - 1 - step) % count, axis, keepdims=False)


def add_low(a, b):
    return (a.astype(f32) + b.astype(f32)).astype(bf16)


def ring_scatter(parts, shift, index, count, axis=0):
    total = ring_part(parts, index, count, 0, axis)
    for step in range(1, count):
        total = add_low(shift(total), ring_part(parts, index, count, step, axis))
    return total


def by_owner(array, axis):
    dp, ctx, exp = (lax.axis_size(a) for a in ("dp", "ctx", "exp"))
    size = array.shape[axis]
    before, after = array.shape[:axis], array.shape[axis + 1 :]
    parts = array.reshape(*before, dp, ctx, exp // 2, 2, size // (dp * ctx * exp), *after)
    order = list(range(axis)) + [axis + i for i in (3, 2, 0, 1, 4)]
    order += list(range(axis + 5, parts.ndim))
    return jnp.transpose(parts, order).reshape(array.shape)


def scatter_axis(parts, axis):
    return ring_scatter(
        parts, lambda v: shifted(v, axis, 1), lax.axis_index(axis), lax.axis_size(axis)
    )


def tie(*values):
    return lax.optimization_barrier(values)


def per_device(
    tokens, attn_gain, w_query, key_matrix, value_matrix, w_out, ffn_gain, expert_gate_up,
    expert_down, expert_ids, gate_weights, span_order, out_grad,
):
    ctx_size, exp_size = lax.axis_size("ctx"), lax.axis_size("exp")
    ctx_here, exp_here = lax.axis_index("ctx"), lax.axis_index("exp")
    experts = EXP_DEV * exp_size
    x, g = tokens[0], out_grad[0]
    rows = x.shape[0]
    capacity = rows * TOPK * 5 // (4 * experts)
    gain_one, gain_two = attn_gain[None, :], ffn_gain[None, :]
    offsets = jnp.arange(HALF, dtype=jnp.int32)

    def device_positions(device):
        pair = lax.dynamic_slice_in_dim(span_order[0], 2 * device, 2, 0)
        return (pair[:, None] * HALF + offsets[None, :]).reshape(-1)

    sources = [(ctx_here - s) % ctx_size for s in range(ctx_size)]
    key_positions = [device_positions(s) for s in sources]
    positions = key_positions[0]
    exponent = jnp.arange(HEAD_SIZE // 2, dtype=f32) * (-2.0 / HEAD_SIZE)
    frequency = jnp.power(f32(rope_base), exponent)
    angles = positions.astype(f32)[:, None] * frequency[None, :]
    cosine, sine = jnp.cos(angles), jnp.sin(angles)
    cosine = jnp.concatenate([cosine, cosine], axis=1)
    sine = jnp.concatenate([-sine, sine], axis=1)

    named = expert_ids[0][:, :, None] == jnp.arange(experts, dtype=jnp.int32)
    member = jnp.any(named, axis=1)
    count = member.astype(jnp.int32)
    place = jnp.where(member, jnp.cumsum(count, axis=0) - count, -1)
    route_gate = jnp.sum(jnp.where(named, gate_weights[0][:, :, None], 0.0), axis=1)
    routing = jnp.stack([place.astype(f32), route_gate]).transpose(0, 2, 1)

    normed, q, kv, att, att_low, lse, mid, nf, g_all, routing_all = forward_to_experts(
        x, gain_one, key_matrix, value_matrix, cosine, sine, positions[:, None],
        jnp.stack(key_positions)[:, None, :], gain_two, w_query, w_out, g, routing,
    )
    routing = lax.dynamic_slice_in_dim(routing_all, EXP_DEV * exp_here, EXP_DEV, 2)
    pos, gates = routing[:, 0].astype(jnp.int32), routing[:, 1]

    dx_chip, y_chip, dx_far, y_far, *kept, _ = expert_blocks(
        capacity, pos, gates, nf, g_all, expert_gate_up, expert_down
    )
    slot_rows, hidden, slot_grad, projected_grad = (
        a.reshape(EXP_DEV, exp_size * capacity, a.shape[-1]) for a in kept
    )
    nf_grad_terms = [dx_chip] + [
        chip_shift(dx_far[s - 1], -s) for s in range(1, exp_size // 2)
    ]
    dp_size, dp_here = lax.axis_size("dp"), lax.axis_index("dp")
    theirs = weight_grad(
        0, 1, (dp_here - 1) % dp_size, MODEL_WIDTH // dp_size, slot_rows, projected_grad
    )[0]
    slot_rows, theirs = tie(slot_rows, theirs)
    came = shifted(theirs, "dp", 1)
    theirs_next, mine, mine_next, other_down, mine_down = other_weight_grads(
        dp_here, dp_size, slot_rows, projected_grad, hidden, slot_grad
    )
    nf_grad_terms, mine, y_far = tie(nf_grad_terms, mine, y_far)

    mid_grad, mid_grad_low, att_grad, delta, ffn_gain_part = middle_backward(
        nf_grad_terms, mid, g, gain_two, w_out, att
    )
    mid_grad_low, came = tie(mid_grad_low, came)
    w_out_grad = by_owner(dot_tn(att_low, mid_grad_low).astype(bf16), 0)
    y_terms = [y_chip] + [chip_shift(y_far[s - 1], -s) for s in range(1, exp_size // 2)]

    dql, dkv, gate_up_first, gate_up_next, down_sum, w_out_sum = attention_backward(
        q, att_grad, kv, lse, delta, jnp.stack(key_positions)[:, :, None], positions[None, :],
        cosine, sine, mine, came, w_out_grad, theirs_next, mine_next, other_down, mine_down,
    )
    gate_up_second, down_share, tokens_grad, gains, attention = last_part(
        gate_up_next, down_sum, mine_down, other_down, dql, dkv, by_owner(normed, 1), w_query, key_matrix,
        value_matrix, cosine, sine, x, gain_one, mid_grad, ffn_gain_part, w_out_sum,
    )
    w_query_share, w_kv_share, w_out_share = attention
    layer_output = mid
    for term in y_terms:
        layer_output = layer_output + term.astype(f32)
    layer_output = layer_output.astype(bf16)
    owner = (lax.axis_index("dp") * ctx_size + ctx_here) * exp_size + exp_here
    gain_share = MODEL_WIDTH // (dp_size * ctx_size * exp_size)
    gains = lax.dynamic_slice_in_dim(gains, owner * gain_share, gain_share, 1)
    return (
        layer_output[None],
        tokens_grad[None],
        gains[0],
        w_query_share,
        w_kv_share[:, :KV_WIDTH],
        w_kv_share[:, KV_WIDTH:],
        w_out_share,
        gains[1],
        jnp.stack([gate_up_first, gate_up_second]),
        down_share,
    )


def solution(mesh):
    by_row = P(("dp", "exp"), "ctx", None)
    share = P(("dp", "ctx", "exp"))
    share_rows = P(("dp", "ctx", "exp"), None)
    return jax.shard_map(
        per_device,
        mesh=mesh,
        in_specs=(
            by_row, P(), P(), P(), P(), P(), P(), P("exp", None, None), P("exp", None, None),
            by_row, by_row, P(("dp", "exp"), None), by_row,
        ),
        out_specs=(
            by_row, by_row, share, share_rows, share_rows, share_rows, share_rows, share,
            P("exp", ("dp", "ctx"), None), P("exp", ("dp", "ctx"), None),
        ),
        check_vma=False,
    )
```

```python
import functools
import math

import jax
import jax.numpy as jnp
from jax import lax
from jax.experimental import pallas as pl
from jax.experimental.pallas import tpu as pltpu
from jax.sharding import PartitionSpec as P

MODEL_WIDTH = 1536
QUERY_HEADS = 12
KEY_VALUE_HEADS = 2
GROUP = QUERY_HEADS // KEY_VALUE_HEADS
HEAD_SIZE = 128
KV_WIDTH = KEY_VALUE_HEADS * HEAD_SIZE
FF = 768
TOPK = 4
EXP_DEV = 2
TOK_DEV = 512
HALF = 256

epsilon = 1e-06
rope_base = 1000000.0
masked_score = -1e30
score_scale = HEAD_SIZE ** (-0.5)
score_to_log2 = score_scale * math.log2(math.e)
gelu_c = math.sqrt(2.0 / math.pi)

f32 = jnp.float32
bf16 = jnp.bfloat16
NT = (((1,), (1,)), ((), ()))
TN = (((0,), (0,)), ((), ()))
VMEM_BYTES = 63 * 1024 * 1024
MESH = pl.DeviceIdType.MESH


def dot(a, b):
    return jnp.dot(a, b, preferred_element_type=f32)


def dot_nt(a, b):
    return lax.dot_general(a, b, NT, preferred_element_type=f32)


def dot_tn(a, b):
    return lax.dot_general(a, b, TN, preferred_element_type=f32)


def params(**more):
    return pltpu.CompilerParams(vmem_limit_bytes=VMEM_BYTES, **more)


def cost(flops, size, exps=0):
    return pl.CostEstimate(flops=int(flops) // 32, bytes_accessed=int(size) // 32, transcendentals=int(exps) // 32)


def whole(shape):
    return pl.BlockSpec(shape, lambda *_: (0,) * len(shape))


def rotate(values, cosine, signed_sine):
    return values * cosine + pltpu.roll(values, HEAD_SIZE // 2, 1) * signed_sine


def rotate_back(values, cosine, signed_sine):
    return values * cosine - pltpu.roll(values, HEAD_SIZE // 2, 1) * signed_sine


HEAD_ROWS = 16


class Gather:
    def __init__(self, own, slots, send_sem, recv_sem):
        self.own, self.slots, self.send_sem, self.recv_sem = own, slots, send_sem, recv_sem
        self.chips = lax.axis_size("exp") // 2
        exp = lax.axis_index("exp")
        core, chip = lax.rem(exp, 2), exp // 2
        self.other = {"exp": chip * 2 + 1 - core}
        self.ahead = [
            {"exp": lax.rem(chip + s, self.chips) * 2 + core} for s in range(self.chips)
        ]
        self.behind = [
            {"exp": lax.rem(chip + self.chips - s, self.chips) * 2 + core}
            for s in range(self.chips)
        ]

    def neighbours(self):
        if self.chips == 2:
            return [self.other, self.ahead[1]]
        return [self.other] + self.ahead[1:]

    def copy(self, slot):
        source, device = self.own, self.other
        if slot > 1 and slot % 2 == 0:
            source = self.slots.at[slot + 1]
        elif slot > 1:
            device = self.ahead[slot // 2]
        return remote(
            source, self.slots.at[slot], self.send_sem.at[slot], self.recv_sem.at[slot], device
        )

    def keep(self):
        return pltpu.make_async_copy(self.own, self.slots.at[0], self.recv_sem.at[0])

    def start(self):
        self.copy(1).start()
        for s in range(1, self.chips):
            self.copy(2 * s + 1).start()

    def cross(self):
        for s in range(1, self.chips):
            self.copy(2 * s + 1).wait_recv()
            self.copy(2 * s).start()

    def finish(self):
        self.copy(1).wait_recv()
        for s in range(1, self.chips):
            self.copy(2 * s).wait_recv()
        self.finish_sends()

    def finish_sends(self):
        for slot in range(1, 2 * self.chips):
            self.copy(slot).wait_send()


def routes(ids_ref, gates_ref, place_cols, routing):
    rows = ids_ref.shape[1]
    lane = lax.broadcasted_iota(jnp.int32, (rows, HEAD_SIZE), 1).astype(f32)
    both = jnp.concatenate([ids_ref[...].astype(f32), gates_ref[...]], axis=0).T
    member = jnp.zeros((rows, HEAD_SIZE), f32)
    gates = jnp.zeros((rows, HEAD_SIZE), f32)
    for k in range(TOPK):
        hit = both[:, k : k + 1] == lane
        member = jnp.where(hit, 1.0, member)
        gates = jnp.where(hit, both[:, TOPK + k : TOPK + k + 1], gates)
    later = lax.broadcasted_iota(jnp.int32, (rows, rows), 0)
    earlier = later > lax.broadcasted_iota(jnp.int32, (rows, rows), 1)
    place = dot(earlier.astype(bf16), member.astype(bf16))
    place = jnp.where(member > 0.0, place, -1.0)
    place_cols[...] = place
    routing[0] = place.T[: routing.shape[1], :]
    routing[1] = gates.T[: routing.shape[1], :]


def forward_kernel(
    n, x_ref, gain_ref, wk_ref, wv_ref, cos_ref, sin_ref, qpos_ref, kpos_ref, ffn_gain_ref, wq_hbm,
    wo_hbm, g_hbm, ids_ref, gates_ref, normed_ref, q_ref, kv_ref, att_ref, att_low_ref, lse_ref,
    mid_ref, nf_ref, g_all, place_cols_all, routing_all, wq_ref, wo_ref, tops, totals, place_cols,
    routing, load_sem, send_sem, recv_sem, *gather_sems,
):
    load_q = pltpu.make_async_copy(wq_hbm, wq_ref, load_sem.at[0])
    load_o = pltpu.make_async_copy(wo_hbm, wo_ref, load_sem.at[1])
    load_q.start()
    load_o.start()
    ctx = Axis("ctx")
    gathers = [
        Gather(g_hbm, g_all, *gather_sems[0:2]),
        Gather(place_cols, place_cols_all, *gather_sems[2:4]),
        Gather(routing, routing_all, *gather_sems[4:6]),
    ]
    signal_and_wait(ctx.neighbours() + gathers[0].neighbours())

    def pass_on(step):
        return remote(
            kv_ref.at[step], kv_ref.at[step + 1], send_sem.at[step], recv_sem.at[step], ctx.next
        )

    rows = x_ref.shape[0]
    x = x_ref[...].astype(f32)
    r = lax.rsqrt(jnp.mean(x * x, axis=-1, keepdims=True) + epsilon)
    normed_ref[...] = (x * r * gain_ref[...]).astype(bf16)
    normed = normed_ref[...]
    cosine, sine = cos_ref[...], sin_ref[...]
    keys = dot(normed, wk_ref[...])
    for head in range(KEY_VALUE_HEADS):
        span = slice(head * HEAD_SIZE, (head + 1) * HEAD_SIZE)
        kv_ref[0, :, span] = rotate(keys[:, span], cosine, sine).astype(bf16)
    kv_ref[0, :, KV_WIDTH:] = dot(normed, wv_ref[...]).astype(bf16)
    pass_on(0).start()
    routes(ids_ref, gates_ref, place_cols, routing)
    for gather in gathers:
        gather.start()
        gather.keep().start()
    load_q.wait()
    for start in range(0, MODEL_WIDTH, WIDTH_TILE):
        queries = dot(normed, wq_ref[:, start : start + WIDTH_TILE])
        for offset in range(0, WIDTH_TILE, HEAD_SIZE):
            span = slice(start + offset, start + offset + HEAD_SIZE)
            part = queries[:, offset : offset + HEAD_SIZE]
            q_ref[:, span] = rotate(part, cosine, sine).astype(bf16)

    for step in range(n):
        if step:
            pass_on(step - 1).wait_recv()
            if step < n - 1:
                pass_on(step).start()
        allowed = kpos_ref[step] <= qpos_ref[...]

        def one_group(group, carry):
            keys = kv_ref[step, :, pl.ds(pl.multiple_of(group * HEAD_SIZE, HEAD_SIZE), HEAD_SIZE)]
            start = pl.multiple_of(KV_WIDTH + group * HEAD_SIZE, HEAD_SIZE)
            values = kv_ref[step, :, pl.ds(start, HEAD_SIZE)]
            for member in range(GROUP):
                head = group * GROUP + member
                columns = pl.ds(pl.multiple_of(head * HEAD_SIZE, HEAD_SIZE), HEAD_SIZE)
                lane = slice(member, member + 1)
                scores = jnp.where(allowed, dot_nt(q_ref[:, columns], keys), masked_score)
                top = jnp.max(scores, axis=-1, keepdims=True) * score_to_log2
                if step:
                    before = tops[group, :, lane]
                    top = jnp.maximum(before, top)
                    rescale = jnp.exp2(before - top)
                weights = jnp.exp2(scores * score_to_log2 - top)
                total = jnp.sum(weights, axis=-1, keepdims=True)
                out = dot(weights.astype(bf16), values)
                if step:
                    total += totals[group, :, lane] * rescale
                    out += att_ref[:, columns] * rescale
                if step < n - 1:
                    tops[group, :, lane] = top
                    totals[group, :, lane] = total
                else:
                    out /= total
                    att_low_ref[:, columns] = out.astype(bf16)
                    tops[group, :, lane] = top + jnp.log2(total)
                att_ref[:, columns] = out
            return carry

        lax.fori_loop(0, KEY_VALUE_HEADS, one_group, 0)
    for group in range(KEY_VALUE_HEADS):
        lse_ref[group * GROUP : (group + 1) * GROUP, :] = tops[group].T[:GROUP, :]
    lse_ref[QUERY_HEADS:, :] = jnp.zeros((HEAD_ROWS - QUERY_HEADS, rows), f32)
    for gather in gathers:
        gather.cross()
    load_o.wait()
    half = rows // 2
    for part in range(2):
        band = slice(part * half, (part + 1) * half)
        mid = x_ref[band, :].astype(f32) + dot(att_low_ref[band, :], wo_ref[...])
        mid_ref[band, :] = mid
        r = lax.rsqrt(jnp.mean(mid * mid, axis=-1, keepdims=True) + epsilon)
        nf_ref[band, :] = (mid * r * ffn_gain_ref[...]).astype(bf16)
    for step in range(n - 1):
        pass_on(step).wait_send()
    for gather in gathers:
        gather.keep().wait()
        gather.finish()


def forward_to_experts(
    x, gain, wk, wv, cosine, sine, qpos_col, kpos_rows, ffn_gain, wq, wo, g, ids, gates
):
    exp_size = lax.axis_size("exp")
    routing = (2, EXP_DEV * exp_size, x.shape[0])
    rows, n = x.shape[0], kpos_rows.shape[0]
    vmem = pl.BlockSpec(memory_space=pltpu.VMEM)
    hbm = pl.BlockSpec(memory_space=pl.ANY)
    wide = (rows, MODEL_WIDTH)
    return pl.pallas_call(
        functools.partial(forward_kernel, n),
        in_specs=[vmem] * 9 + [hbm] * 3 + [vmem] * 2,
        out_specs=(vmem,) * 8 + (hbm,) * 3,
        out_shape=(
            jax.ShapeDtypeStruct(wide, bf16),
            jax.ShapeDtypeStruct(wide, bf16),
            jax.ShapeDtypeStruct((n, rows, 2 * KV_WIDTH), bf16),
            jax.ShapeDtypeStruct(wide, f32),
            jax.ShapeDtypeStruct(wide, bf16),
            jax.ShapeDtypeStruct((HEAD_ROWS, rows), f32),
            jax.ShapeDtypeStruct(wide, f32),
            jax.ShapeDtypeStruct(wide, bf16),
            jax.ShapeDtypeStruct((exp_size, *g.shape), bf16),
            jax.ShapeDtypeStruct((exp_size, rows, HEAD_SIZE), f32),
            jax.ShapeDtypeStruct((exp_size, *routing), f32),
        ),
        scratch_shapes=[
            pltpu.VMEM((MODEL_WIDTH, MODEL_WIDTH), bf16),
            pltpu.VMEM((MODEL_WIDTH, MODEL_WIDTH), bf16),
            pltpu.VMEM((KEY_VALUE_HEADS, rows, HEAD_SIZE), f32),
            pltpu.VMEM((KEY_VALUE_HEADS, rows, HEAD_SIZE), f32),
            pltpu.VMEM((rows, HEAD_SIZE), f32),
            pltpu.VMEM(routing, f32),
            pltpu.SemaphoreType.DMA((2,)),
            pltpu.SemaphoreType.DMA((n - 1,)),
            pltpu.SemaphoreType.DMA((n - 1,)),
        ]
        + [pltpu.SemaphoreType.DMA((exp_size,))] * 6,
        compiler_params=params(collective_id=3, has_side_effects=True),
        cost_estimate=cost(
            4 * n * rows * rows * MODEL_WIDTH + 5 * rows * MODEL_WIDTH * MODEL_WIDTH, 4e7,
            n * rows * rows * QUERY_HEADS,
        ),
        name="forward_to_experts",
    )(x, gain, wk, wv, cosine, sine, qpos_col, kpos_rows, ffn_gain, wq, wo, g, ids, gates)


FF_TILE = 256
WIDTH_TILE = 512


def expert_kernel(
    place_cols_ref, routing_ref, nf_hbm, g_ref, wgu_ref, wd_ref, dx_chip, y_chip, dx_far,
    y_far, rows_ref, hidden_ref, slot_grad_ref, pg_ref, x_all, x_ref, place, result, rows_grad,
    dx_out, y_out, dx_came, y_came, load_sem, gather_send, gather_recv, back_send, back_recv,
):
    block, expert = pl.program_id(0), pl.program_id(1)
    capacity = rows_ref.shape[-2]
    tokens = x_ref.shape[0]
    gather = Gather(nf_hbm, x_all, gather_send, gather_recv)
    chips = gather.chips

    def load(source):
        copy = pltpu.make_async_copy(source, x_ref, load_sem.at[0])
        copy.start()
        copy.wait()

    def back(slot):
        return [
            remote(out, came.at[slot], back_send.at[i, slot], back_recv.at[i, slot], gather.other)
            for i, (out, came) in enumerate(((dx_out, dx_came), (y_out, y_came)))
        ]

    @pl.when((block == 0) & (expert == 0))
    def _():
        signal_and_wait(gather.neighbours())
        gather.start()
        load(nf_hbm)

    @pl.when((block == 1) & (expert == 0))
    def _():
        gather.copy(1).wait_recv()
        load(x_all.at[1])

    for s in range(1, chips):

        @pl.when((block == 2 * s) & (expert == 0))
        def _():
            if s == 1:
                gather.cross()
            gather.copy(2 * s).wait_recv()
            load(x_all.at[2 * s])

        @pl.when((block == 2 * s + 1) & (expert == 0))
        def _():
            load(x_all.at[2 * s + 1])

    mine = lax.axis_index("exp") * EXP_DEV + expert
    slot_r = lax.broadcasted_iota(jnp.int32, (capacity, tokens), 0).astype(f32)
    slot_c = lax.broadcasted_iota(jnp.int32, (tokens, capacity), 1).astype(f32)
    match = slot_r == routing_ref[0, 0, pl.ds(mine, 1), :]
    pick = match.astype(bf16)
    lane = lax.broadcasted_iota(jnp.int32, (tokens, HEAD_SIZE), 1)
    place_col = jnp.sum(jnp.where(lane == mine, place_cols_ref[0], 0.0), axis=1, keepdims=True)
    place[expert] = (slot_c == place_col).astype(bf16)
    gate_row = routing_ref[0, 1, pl.ds(mine, 1), :]
    gates = jnp.sum(jnp.where(match, gate_row, 0.0), axis=1, keepdims=True)
    for start in range(0, MODEL_WIDTH, WIDTH_TILE):
        span = slice(start, start + WIDTH_TILE)
        rows_ref[0, 0, :, span] = dot(pick, x_ref[:, span]).astype(bf16)
        slot_grad_ref[0, 0, :, span] = (dot(pick, g_ref[0, :, span]) * gates).astype(bf16)
    rows = rows_ref[0, 0]
    slot_grad = slot_grad_ref[0, 0]
    for start in range(0, FF, FF_TILE):
        span = slice(start, start + FF_TILE)
        up_span = slice(FF + start, FF + start + FF_TILE)
        gate = dot(rows, wgu_ref[0, :, span])
        up = dot(rows, wgu_ref[0, :, up_span])
        hidden_grad = dot_nt(slot_grad, wd_ref[0, span, :])
        square = gate * gate
        tangent = jnp.tanh(gate * (gelu_c + (gelu_c * 0.044715) * square))
        half_plus = 0.5 + 0.5 * tangent
        activated = gate * half_plus
        slope = half_plus + activated * (1.0 - tangent) * (
            gelu_c + (3.0 * 0.044715 * gelu_c) * square
        )
        hidden_ref[0, 0, :, span] = (activated * up).astype(bf16)
        pg_ref[0, 0, :, span] = (hidden_grad * up * slope).astype(bf16)
        pg_ref[0, 0, :, up_span] = (hidden_grad * activated).astype(bf16)
    hidden = hidden_ref[0, 0]
    projected_grad = pg_ref[0, 0]
    for start in range(0, MODEL_WIDTH, WIDTH_TILE):
        span = slice(start, start + WIDTH_TILE)
        result[expert, :, span] = (dot(hidden, wd_ref[0, :, span]) * gates).astype(bf16)
        rows_grad[expert, :, span] = dot_nt(projected_grad, wgu_ref[0, span, :]).astype(bf16)

    last = expert == EXP_DEV - 1
    for sent in [1] + [2 * s for s in range(1, chips)]:

        @pl.when(last & (block == sent + 1))
        def _():
            for copy in back(sent // 2):
                copy.wait_send()

    @pl.when(last)
    def _():
        both = jnp.concatenate([place[e] for e in range(EXP_DEV)], axis=1)
        for start in range(0, MODEL_WIDTH, WIDTH_TILE):
            span = slice(start, start + WIDTH_TILE)
            for out_ref, terms in ((y_out, result), (dx_out, rows_grad)):
                stacked = terms[:, :, span].reshape(EXP_DEV * capacity, WIDTH_TILE)
                out_ref[:, span] = dot(both, stacked).astype(bf16)

    @pl.when(last & (block == 0))
    def _():
        dx_chip[...] = dx_out[...]
        y_chip[...] = y_out[...]

    for sent in [1] + [2 * s for s in range(1, chips)]:

        @pl.when(last & (block == sent))
        def _():
            for copy in back(sent // 2):
                copy.start()

    def add(target, own, came):
        for start in range(0, tokens, HEAD_SIZE):
            band = slice(start, start + HEAD_SIZE)
            total = own[band, :].astype(f32) + came[band, :].astype(f32)
            target[band, :] = total.astype(bf16)

    for s in range(1, chips):

        @pl.when(last & (block == 2 * s + 1))
        def _():
            for copy in back(s):
                copy.wait_recv()
            add(dx_far.at[s - 1], dx_out, dx_came.at[s])
            add(y_far.at[s - 1], y_out, y_came.at[s])

    @pl.when(last & (block == 2 * chips - 1))
    def _():
        for copy in back(0):
            copy.wait_recv()
        add(dx_chip, dx_chip, dx_came.at[0])
        add(y_chip, y_chip, y_came.at[0])
        gather.finish_sends()


def expert_blocks(capacity, place_cols, routing, nf, g_all, wgu, wd):
    blocks, tokens, _ = g_all.shape
    chips = blocks // 2
    kept_shapes = tuple(
        jax.ShapeDtypeStruct((EXP_DEV, blocks, capacity, width), bf16)
        for width in (MODEL_WIDTH, FF, MODEL_WIDTH, 2 * FF)
    )
    kept_specs = tuple(
        pl.BlockSpec((1, 1, capacity, s.shape[-1]), lambda b, e: (e, b, 0, 0)) for s in kept_shapes
    )
    flops = blocks * EXP_DEV * 2 * capacity * (4 * tokens * MODEL_WIDTH + 9 * MODEL_WIDTH * FF)
    wide = (tokens, MODEL_WIDTH)
    result = jax.ShapeDtypeStruct(wide, bf16)
    far = jax.ShapeDtypeStruct((chips - 1, *wide), bf16)
    hbm = pl.BlockSpec(memory_space=pl.ANY)

    def once(shape):
        return pl.BlockSpec(
            shape, lambda b, e: (0,) * len(shape), pipeline_mode=pl.Buffered(1)
        )

    return pl.pallas_call(
        expert_kernel,
        grid=(blocks, EXP_DEV),
        in_specs=[
            pl.BlockSpec((1, tokens, HEAD_SIZE), lambda b, e: (b, 0, 0)),
            pl.BlockSpec((1, *routing.shape[1:]), lambda b, e: (b, 0, 0, 0)),
            hbm,
            pl.BlockSpec((1, tokens, MODEL_WIDTH), lambda b, e: (b, 0, 0)),
            pl.BlockSpec((1, MODEL_WIDTH, 2 * FF), lambda b, e: (e, 0, 0)),
            pl.BlockSpec((1, FF, MODEL_WIDTH), lambda b, e: (e, 0, 0)),
        ],
        out_specs=(once(wide), once(wide), once(far.shape), once(far.shape)) + kept_specs + (hbm,),
        out_shape=(result, result, far, far)
        + kept_shapes
        + (jax.ShapeDtypeStruct((blocks, *wide), bf16),),
        scratch_shapes=[
            pltpu.VMEM(wide, bf16),
            pltpu.VMEM((EXP_DEV, tokens, capacity), bf16),
            pltpu.VMEM((EXP_DEV, capacity, MODEL_WIDTH), bf16),
            pltpu.VMEM((EXP_DEV, capacity, MODEL_WIDTH), bf16),
            pltpu.VMEM(wide, bf16),
            pltpu.VMEM(wide, bf16),
            pltpu.VMEM((chips, *wide), bf16),
            pltpu.VMEM((chips, *wide), bf16),
            pltpu.SemaphoreType.DMA((1,)),
            pltpu.SemaphoreType.DMA((blocks,)),
            pltpu.SemaphoreType.DMA((blocks,)),
            pltpu.SemaphoreType.DMA((2, chips)),
            pltpu.SemaphoreType.DMA((2, chips)),
        ],
        compiler_params=params(collective_id=4, has_side_effects=True),
        cost_estimate=cost(flops, 6e7),
        name="expert_blocks",
    )(place_cols, routing, nf, g_all, wgu, wd)


GRAD_TILE = 384


def weight_grad_kernel(chunk_ref, a_ref, b_ref, out_ref):
    out_ref[0] = dot_tn(a_ref[0], b_ref[0]).astype(bf16)


def weight_grad(first, experts, chunk, size, a, b):
    slots, width = a.shape[1], b.shape[-1]
    tiles = size // GRAD_TILE
    return pl.pallas_call(
        weight_grad_kernel,
        grid_spec=pltpu.PrefetchScalarGridSpec(
            num_scalar_prefetch=1,
            grid=(experts, tiles),
            in_specs=[
                pl.BlockSpec((1, slots, GRAD_TILE), lambda e, t, c: (first + e, 0, c[0] * tiles + t)),
                pl.BlockSpec((1, slots, width), lambda e, t, c: (first + e, 0, 0)),
            ],
            out_specs=pl.BlockSpec((1, GRAD_TILE, width), lambda e, t, c: (e, t, 0)),
        ),
        out_shape=jax.ShapeDtypeStruct((experts, size, width), bf16),
        compiler_params=params(),
        cost_estimate=cost(2 * experts * slots * size * width, 2e7),
        name="weight_grad",
    )(chunk.reshape(1).astype(jnp.int32), a, b)


def other_weight_grads_kernel(
    dp_ref, rows_ref, pg_ref, hidden_ref, slot_grad_ref, theirs_ref, mine0_ref, mine1_ref,
    other_down_ref, mine_down_ref,
):
    step = pl.program_id(0)
    for first, out_ref in ((0, theirs_ref), (2, mine0_ref), (4, mine1_ref)):

        @pl.when((step == first) | (step == first + 1))
        def _():
            out_ref[...] = dot_tn(rows_ref[0], pg_ref[0]).astype(bf16)

    for place, out_ref in enumerate((other_down_ref, mine_down_ref)):

        @pl.when((step == 6 + place) | (step == 8 + place))
        def _():
            out_ref[0] = dot_tn(hidden_ref[0], slot_grad_ref[0]).astype(bf16)


def other_weight_grads(dp_here, dp_size, slot_rows, pg, hidden, slot_grad):
    assert dp_size == 2 and MODEL_WIDTH // dp_size == 2 * GRAD_TILE and FF // dp_size == GRAD_TILE
    slots = slot_rows.shape[1]
    half = (2 * GRAD_TILE, 2 * FF)

    def gate_up_rows(t, d):
        t = jnp.minimum(t, 5)
        expert = jnp.where((t == 2) | (t == 3), 0, 1)
        place = jnp.where(t < 2, 1 - d[0], d[0])
        return expert, 0, place * 2 + t % 2

    def gate_up_right(t, d):
        return gate_up_rows(t, d)[0], 0, 0

    def down_rows(t, d):
        t = jnp.maximum(t, 6) - 6
        return t // 2, 0, jnp.where(t % 2 == 0, 1 - d[0], d[0])

    def down_right(t, d):
        return down_rows(t, d)[0], 0, 0

    def piece(first):
        return pl.BlockSpec((GRAD_TILE, 2 * FF), lambda t, d: (jnp.clip(t - first, 0, 1), 0))

    def down(first):
        return pl.BlockSpec(
            (1, GRAD_TILE, MODEL_WIDTH), lambda t, d: (jnp.clip((t - first) // 2, 0, 1), 0, 0)
        )

    return pl.pallas_call(
        other_weight_grads_kernel,
        grid_spec=pltpu.PrefetchScalarGridSpec(
            num_scalar_prefetch=1,
            grid=(10,),
            in_specs=[
                pl.BlockSpec((1, slots, GRAD_TILE), gate_up_rows),
                pl.BlockSpec((1, slots, 2 * FF), gate_up_right),
                pl.BlockSpec((1, slots, GRAD_TILE), down_rows),
                pl.BlockSpec((1, slots, MODEL_WIDTH), down_right),
            ],
            out_specs=(piece(0), piece(2), piece(4), down(6), down(7)),
        ),
        out_shape=(jax.ShapeDtypeStruct(half, bf16),) * 3
        + (jax.ShapeDtypeStruct((EXP_DEV, GRAD_TILE, MODEL_WIDTH), bf16),) * 2,
        compiler_params=params(),
        cost_estimate=cost(10 * 2 * slots * GRAD_TILE * 2 * FF, 5e7),
        name="other_weight_grads",
    )(dp_here.reshape(1).astype(jnp.int32), slot_rows, pg, hidden, slot_grad)


def middle_kernel(*refs):
    count = len(refs) - 13
    parts = refs[:count]
    mid_ref, g_ref, gain_ref, wo_ref, att_ref, att_low_ref = refs[count : count + 6]
    mg_ref, ag_ref, delta_ref, dgain_ref, wo_grad_ref, mgl_ref, delta_cols = refs[count + 6 :]
    rows = mid_ref.shape[0]
    half = rows // 2
    lane = lax.broadcasted_iota(jnp.int32, (half, HEAD_SIZE), 1)
    dgain = jnp.zeros((1, MODEL_WIDTH), f32)
    for part in range(2):
        band = slice(part * half, (part + 1) * half)
        nf_grad = parts[0][band, :].astype(f32)
        for other in parts[1:]:
            nf_grad += other[band, :].astype(f32)
        mid = mid_ref[band, :]
        r = lax.rsqrt(jnp.mean(mid * mid, axis=-1, keepdims=True) + epsilon)
        u = nf_grad * gain_ref[...]
        inner = jnp.mean(u * mid, axis=-1, keepdims=True)
        grad = g_ref[band, :].astype(f32) + r * u - mid * (r * r * r * inner)
        dgain += jnp.sum(nf_grad * mid * r, axis=0, keepdims=True)
        mg_ref[band, :] = grad
        low = grad.astype(bf16)
        mgl_ref[band, :] = low
        att_grad = dot_nt(low, wo_ref[...]).astype(bf16)
        ag_ref[band, :] = att_grad
        delta = jnp.zeros((half, HEAD_SIZE), f32)
        for head in range(QUERY_HEADS):
            span = slice(head * HEAD_SIZE, (head + 1) * HEAD_SIZE)
            one = jnp.sum(att_grad[:, span].astype(f32) * att_ref[band, span], axis=-1, keepdims=True)
            delta = jnp.where(lane == head, one, delta)
        delta_cols[band, :] = delta
    dgain_ref[...] = dgain
    delta_ref[...] = delta_cols[...].T[: delta_ref.shape[0], :]
    store_by_owner(wo_grad_ref, att_low_ref, mgl_ref[...])


def middle_backward(parts, mid, g, gain, wo, att, att_low):
    rows = mid.shape[0]
    return pl.pallas_call(
        middle_kernel,
        out_shape=(
            jax.ShapeDtypeStruct((rows, MODEL_WIDTH), f32),
            jax.ShapeDtypeStruct((rows, MODEL_WIDTH), bf16),
            jax.ShapeDtypeStruct((HEAD_ROWS, rows), f32),
            jax.ShapeDtypeStruct((1, MODEL_WIDTH), f32),
            jax.ShapeDtypeStruct((MODEL_WIDTH, MODEL_WIDTH), bf16),
        ),
        scratch_shapes=[
            pltpu.VMEM((rows, MODEL_WIDTH), bf16),
            pltpu.VMEM((rows, HEAD_SIZE), f32),
        ],
        compiler_params=params(),
        cost_estimate=cost(4 * rows * MODEL_WIDTH * MODEL_WIDTH, 3e7),
        name="middle_backward",
    )(*parts, mid, g, gain, wo, att, att_low)


def signal_and_wait(neighbours):
    barrier = pltpu.get_barrier_semaphore()
    for neighbour in neighbours:
        pl.semaphore_signal(barrier, inc=1, device_id=neighbour, device_id_type=MESH)
    pl.semaphore_wait(barrier, len(neighbours))


def remote(source, target, send_sem, recv_sem, device):
    return pltpu.make_async_remote_copy(
        src_ref=source, dst_ref=target, send_sem=send_sem, recv_sem=recv_sem,
        device_id=device, device_id_type=MESH,
    )


class Axis:
    def __init__(self, name):
        if name in ("dp", "ctx"):
            self.count, self.me = lax.axis_size(name), lax.axis_index(name)
            place = lambda i: {name: i}
        else:
            exp = lax.axis_index("exp")
            core, chip = lax.rem(exp, 2), exp // 2
            if name == "core":
                self.count, self.me = 2, core
                place = lambda i: {"exp": chip * 2 + i}
            else:
                self.count, self.me = lax.axis_size("exp") // 2, chip
                place = lambda i: {"exp": i * 2 + core}
        self.place = place
        self.next = place(lax.rem(self.me + 1, self.count))
        self.last = place(lax.rem(self.me + self.count - 1, self.count))

    def neighbours(self):
        return [self.next] if self.count == 2 else [self.next, self.last]

    def others(self):
        return [self.place(lax.rem(self.me + s, self.count)) for s in range(1, self.count)]


class Direct:
    def __init__(self, axis, source, rows, recv, send_sem, recv_sem):
        self.axis, self.count, self.source, self.rows = axis, 2, source, rows
        self.recv, self.send_sem, self.recv_sem = recv, send_sem, recv_sem

    def part(self, place):
        return pl.ds(pl.multiple_of(place * self.rows, self.rows), self.rows)

    def copies(self):
        axis, out = self.axis, []
        for s in range(1, axis.count):
            place = lax.rem(axis.me + s, axis.count)
            out.append(
                remote(
                    self.source.at[self.part(place), :], self.recv.at[s - 1],
                    self.send_sem.at[s - 1], self.recv_sem.at[s - 1], axis.place(place),
                )
            )
        return out

    def hop(self, hop):
        if hop == 0:
            for copy in self.copies():
                copy.start()
            return None
        total = self.source[self.part(self.axis.me), :].astype(f32)
        for i, copy in enumerate(self.copies()):
            copy.wait_recv()
            total += self.recv[i].astype(f32)
        return total

    def finish(self):
        for copy in self.copies():
            copy.wait_send()


class Ring:
    def __init__(self, axis, terms, rows, send, recv, send_sem, recv_sem, first=None, own=False):
        self.axis, self.count, self.terms, self.rows = axis, axis.count, terms, rows
        self.first, self.own = terms[0] if first is None else first, own
        self.send, self.recv, self.send_sem, self.recv_sem = send, recv, send_sem, recv_sem

    def here(self, hop):
        part = lax.rem(self.axis.me + self.count - 1 - hop, self.count)
        return pl.ds(pl.multiple_of(part * self.rows, self.rows), self.rows)

    def copy(self, hop):
        if len(self.terms) > 1:
            source = self.send.at[hop]
        elif hop == 0:
            source = self.first.at[self.here(0), :]
        else:
            source = self.send.at[hop - 1]
        return remote(
            source, self.recv.at[hop], self.send_sem.at[hop], self.recv_sem.at[hop], self.axis.next
        )

    def hop(self, hop):
        if hop == 0 and len(self.terms) == 1:
            self.copy(0).start()
            return None
        here = slice(0, self.rows) if self.own else self.here(hop)
        total = self.terms[0][here, :].astype(f32)
        for term in self.terms[1:]:
            total += term[here, :].astype(f32)
        if hop:
            self.copy(hop - 1).wait_recv()
            total += self.recv[hop - 1].astype(f32)
        if hop < self.count - 1:
            self.send[hop - (len(self.terms) == 1)] = total.astype(bf16)
            self.copy(hop).start()
        return total

    def finish(self):
        for hop in range(self.count - 1):
            self.copy(hop).wait_send()


def attention_back_kernel(
    n, q_ref, ag_ref, kv_ref, lse_ref, delta_ref, kpos_ref, qpos_ref, cos_ref, sin_ref, mine_hbm,
    came_hbm, wo_grad_hbm, next_ref, next_mine_ref, down_ref, down_mine_ref, dql_ref, dkv_ref,
    share_ref, next_sum_ref, down_sum_ref, wo_sum_ref, next_came, down_came, next_mine, down_mine,
    mine_ref, came_ref, wo_grad_ref, dq_acc, held, send, recv, send_sem, recv_sem, next_sem,
    load_sem, *scratch,
):
    ctx, core, chip = Axis("ctx"), Axis("core"), Axis("chip")
    right, across = ctx.next, Axis("dp").next
    signal_and_wait(ctx.neighbours() + core.neighbours() + chip.neighbours() + [across])
    core_rows = wo_grad_ref.shape[0]
    own_rows = pl.ds(pl.multiple_of(core.me * core_rows, core_rows), core_rows)
    wo_chain = Chain(
        [
            Ring(core, [wo_grad_ref], core_rows, *scratch[:4], wo_grad_hbm, True),
            Ring(chip, [scratch[4]], core_rows // chip.count, *scratch[5:9]),
        ],
        [scratch[4], wo_sum_ref],
    )
    ring = Ring(ctx, [mine_ref, came_ref], share_ref.shape[0], *scratch[9:])
    first_loads = [
        pltpu.make_async_copy(source, target, load_sem.at[i])
        for i, (source, target) in enumerate(
            ((mine_hbm, mine_ref), (came_hbm, came_ref), (wo_grad_hbm.at[own_rows, :], wo_grad_ref))
        )
    ]
    for load in first_loads:
        load.start()
    exchanges, loads = [], []
    for i, (source, target, mine_hbm, mine) in enumerate(
        (
            (next_ref, next_came, next_mine_ref, next_mine),
            (down_ref.at[0], down_came, down_mine_ref.at[0], down_mine),
        )
    ):
        exchanges.append(remote(source, target, next_sem.at[i, 0], next_sem.at[i, 1], across))
        loads.append(pltpu.make_async_copy(mine_hbm, mine, next_sem.at[i, 2]))
        exchanges[i].start()
        loads[i].start()
    wo_chain.step()
    for load in first_loads:
        load.wait()
    ring.hop(0)

    def dkv_copy(step, group):
        return remote(
            send.at[group, step], recv.at[group, step], send_sem.at[group, step],
            recv_sem.at[group, step], right,
        )

    qpos = qpos_ref[...].astype(f32)
    for step in range(n):
        back = (step + 1) % n
        kpos = jnp.broadcast_to(kpos_ref[back].astype(f32), (8, kpos_ref.shape[-1])).T[:, :1]

        def one_group(group, carry):
            keys = kv_ref[back, :, pl.ds(pl.multiple_of(group * HEAD_SIZE, HEAD_SIZE), HEAD_SIZE)]
            start = pl.multiple_of(KV_WIDTH + group * HEAD_SIZE, HEAD_SIZE)
            values = kv_ref[back, :, pl.ds(start, HEAD_SIZE)]
            dk = dv = None
            for member in range(GROUP):
                head = group * GROUP + member
                columns = pl.ds(pl.multiple_of(head * HEAD_SIZE, HEAD_SIZE), HEAD_SIZE)
                q, ag = q_ref[:, columns], ag_ref[:, columns]
                scores = dot_nt(keys, q)
                weights = jnp.exp2(scores * score_to_log2 - lse_ref[pl.ds(head, 1), :])
                weights = jnp.where(kpos <= qpos, weights, 0.0)
                weights_grad = dot_nt(values, ag)
                score_grad = weights * (weights_grad - delta_ref[pl.ds(head, 1), :]) * score_scale
                score_grad = score_grad.astype(bf16)
                dv_part = dot(weights.astype(bf16), ag)
                dk_part = dot(score_grad, q)
                dv = dv_part if dv is None else dv + dv_part
                dk = dk_part if dk is None else dk + dk_part
                dq = dot_tn(score_grad, keys)
                if step:
                    dq += dq_acc[:, columns]
                dq_acc[:, columns] = dq
            held[group] = jnp.concatenate([dk, dv], axis=1)
            return carry

        lax.fori_loop(0, KEY_VALUE_HEADS, one_group, 0)
        for group in range(KEY_VALUE_HEADS):
            dkv = held[group]
            if step:
                dkv_copy(step - 1, group).wait_recv()
                dkv += recv[group, step - 1].astype(f32)
            if step < n - 1:
                send[group, step] = dkv.astype(bf16)
                dkv_copy(step, group).start()
            else:
                for place in range(2):
                    start = place * KV_WIDTH + group * HEAD_SIZE
                    part = dkv[:, place * HEAD_SIZE : (place + 1) * HEAD_SIZE]
                    dkv_ref[:, start : start + HEAD_SIZE] = part.astype(bf16)
        if step < n - 2:
            ring.hop(step + 1)
        wo_chain.step(2 if step == 0 else 1)
    cosine, sine = cos_ref[...], sin_ref[...]
    for head in range(QUERY_HEADS):
        span = slice(head * HEAD_SIZE, (head + 1) * HEAD_SIZE)
        dql_ref[:, span] = rotate_back(dq_acc[:, span], cosine, sine).astype(bf16)
    share_ref[...] = ring.hop(n - 1)
    ring.finish()
    for step in range(n - 1):
        for group in range(KEY_VALUE_HEADS):
            dkv_copy(step, group).wait_send()
    wo_chain.step(len(wo_chain.hops))
    wo_chain.finish()
    for i, (sum_ref, mine, came) in enumerate(
        ((next_sum_ref, next_mine, next_came), (down_sum_ref, down_mine, down_came))
    ):
        loads[i].wait()
        exchanges[i].wait()
        for start in range(0, sum_ref.shape[0], HEAD_SIZE):
            band = slice(start, start + HEAD_SIZE)
            total = mine[band, :].astype(f32) + came[band, :].astype(f32)
            sum_ref[band, :] = total.astype(bf16)


def attention_backward(
    q, ag, kv, lse, delta, kpos, qpos_row, cosine, sine, mine, came, w_out_grad, following,
    following_mine, other_down, mine_down,
):
    n, keys, _ = kv.shape
    rows = q.shape[0]
    chips = sizes()["chip"]
    wo_rows = w_out_grad.shape[0] // 2
    vmem = pl.BlockSpec(memory_space=pltpu.VMEM)
    hbm = pl.BlockSpec(memory_space=pl.ANY)
    return pl.pallas_call(
        functools.partial(attention_back_kernel, n),
        in_specs=[vmem] * 9 + [hbm] * 7,
        out_specs=(vmem,) * 6,
        out_shape=(
            jax.ShapeDtypeStruct((rows, MODEL_WIDTH), bf16),
            jax.ShapeDtypeStruct((keys, 2 * KV_WIDTH), bf16),
            jax.ShapeDtypeStruct((mine.shape[0] // n, mine.shape[1]), f32),
            jax.ShapeDtypeStruct(following.shape, bf16),
            jax.ShapeDtypeStruct(other_down.shape[1:], bf16),
            jax.ShapeDtypeStruct((wo_rows // chips, MODEL_WIDTH), bf16),
        ),
        scratch_shapes=[
            pltpu.VMEM(following.shape, bf16),
            pltpu.VMEM(other_down.shape[1:], bf16),
            pltpu.VMEM(following.shape, bf16),
            pltpu.VMEM(other_down.shape[1:], bf16),
            pltpu.VMEM(mine.shape, bf16),
            pltpu.VMEM(came.shape, bf16),
            pltpu.VMEM((wo_rows, MODEL_WIDTH), bf16),
            pltpu.VMEM((rows, MODEL_WIDTH), f32),
            pltpu.VMEM((KEY_VALUE_HEADS, keys, 2 * HEAD_SIZE), f32),
            pltpu.VMEM((KEY_VALUE_HEADS, n - 1, keys, 2 * HEAD_SIZE), bf16),
            pltpu.VMEM((KEY_VALUE_HEADS, n - 1, keys, 2 * HEAD_SIZE), bf16),
            pltpu.SemaphoreType.DMA((KEY_VALUE_HEADS, n - 1)),
            pltpu.SemaphoreType.DMA((KEY_VALUE_HEADS, n - 1)),
            pltpu.SemaphoreType.DMA((2, 3)),
            pltpu.SemaphoreType.DMA((3,)),
        ]
        + ring_buffers(2, 1, wo_rows, MODEL_WIDTH)
        + [pltpu.VMEM((wo_rows, MODEL_WIDTH), bf16)]
        + ring_buffers(chips, 1, wo_rows // chips, MODEL_WIDTH)
        + ring_buffers(n, 2, mine.shape[0] // n, mine.shape[1]),
        compiler_params=params(collective_id=1, has_side_effects=True),
        cost_estimate=cost(10 * n * rows * keys * MODEL_WIDTH, 4e7, n * rows * keys * QUERY_HEADS),
        name="attention_backward",
    )(
        q, ag, kv, lse, delta, kpos, qpos_row, cosine, sine, mine, came, w_out_grad, following,
        following_mine, other_down, mine_down,
    )


def ring_buffers(count, terms, rows, width):
    sends = count - 1 if terms > 1 else count - 2
    return [
        pltpu.VMEM((sends, rows, width) if sends else (16, HEAD_SIZE), bf16),
        pltpu.VMEM((count - 1, rows, width), bf16),
        pltpu.SemaphoreType.DMA((count - 1,)),
        pltpu.SemaphoreType.DMA((count - 1,)),
    ]


class Chain:
    def __init__(self, rings, stores):
        self.hops = [(r, h) for r in range(len(rings)) for h in range(rings[r].count)]
        self.rings, self.stores, self.done = rings, stores, 0

    def step(self, times=1):
        for _ in range(times):
            if self.done == len(self.hops):
                return
            index, hop = self.hops[self.done]
            self.done += 1
            ring = self.rings[index]
            total = ring.hop(hop)
            if hop == ring.count - 1:
                store = self.stores[index]
                store[...] = total.astype(store.dtype)

    def finish(self):
        assert self.done == len(self.hops)
        for ring in self.rings:
            ring.finish()


FULL_AXES = ("core", "chip", "dp", "ctx")
OWNER_TILE = 384


def owner_rows():
    counts = sizes()
    return MODEL_WIDTH // (2 * counts["chip"] * counts["dp"] * counts["ctx"])


def ordered_in_kernel():
    return owner_rows() % 16 == 0


def store_by_owner(target, a, b):
    share, counts = owner_rows(), sizes()
    for start in range(0, MODEL_WIDTH, OWNER_TILE):
        rows = dot_tn(a[:, start : start + OWNER_TILE], b).astype(bf16)
        if not ordered_in_kernel():
            target[start : start + OWNER_TILE, :] = rows
            continue
        for offset in range(0, OWNER_TILE, share):
            device = (start + offset) // share
            device, core = divmod(device, 2)
            device, chip = divmod(device, counts["chip"])
            dp, ctx = divmod(device, counts["ctx"])
            place = ((core * counts["chip"] + chip) * counts["dp"] + dp) * counts["ctx"] + ctx
            target[place * share : (place + 1) * share, :] = rows[offset : offset + share, :]


def sizes():
    exp = lax.axis_size("exp")
    return {"core": 2, "chip": exp // 2, "dp": lax.axis_size("dp"), "ctx": lax.axis_size("ctx")}


class Total:
    def __init__(self, axis, value, recv, send_sem, recv_sem):
        self.axis, self.value, self.recv = axis, value, recv
        self.send_sem, self.recv_sem = send_sem, recv_sem

    def copy(self, hop):
        source = self.recv.at[hop - 1] if hop else self.value
        return remote(
            source, self.recv.at[hop], self.send_sem.at[hop], self.recv_sem.at[hop], self.axis.next
        )

    def run(self):
        count = self.axis.count
        self.copy(0).start()
        total = self.value[...]
        for hop in range(1, count):
            self.copy(hop - 1).wait_recv()
            total += self.recv[hop - 1]
            if hop < count - 1:
                self.copy(hop).start()
        for hop in range(count - 1):
            self.copy(hop).wait_send()
        self.value[...] = total


GAIN_ROWS = 8


def last_kernel(
    plan, piece_hbm, down_sum_hbm, mine_down_ref, other_down_ref, dql_ref, dkv_ref, normed_ref, wq_hbm,
    wk_hbm, wv_hbm, cos_ref, sin_ref, x_hbm, gain_ref, mg_hbm, ffn_gain_ref, wo_sum_hbm,
    gate_up_ref, down_ref, dx_ref, gains_ref, wq_out, wkv_out, wo_out, wq_grad, wkv_grad, dkvl,
    mg_band, mg_sem, *scratch,
):
    scratch = list(scratch)

    def take(number):
        taken = scratch[:number]
        del scratch[:number]
        return taken

    piece_ref, down_sum_ref, wo_sum_ref, wq_ref, wk_ref, wv_ref, x_ref, load_sem = take(8)
    loads = [
        pltpu.make_async_copy(source, target, load_sem.at[i])
        for i, (source, target) in enumerate(
            (
                (piece_hbm, piece_ref), (down_sum_hbm, down_sum_ref), (wq_hbm, wq_ref),
                (wk_hbm, wk_ref), (wv_hbm, wv_ref), (x_hbm, x_ref), (wo_sum_hbm, wo_sum_ref),
            )
        )
    ]
    axes = {name: Axis(name) for name in FULL_AXES}
    across = axes["dp"].next
    piece = Chain(
        [Ring(axes["ctx"], [piece_ref], gate_up_ref.shape[0], *take(4), piece_hbm)],
        [gate_up_ref],
    )
    came_down, mine_down, down_sem = take(3)
    exchange = remote(
        other_down_ref.at[1], came_down, down_sem.at[0], down_sem.at[1], across
    )
    load_down = pltpu.make_async_copy(mine_down_ref.at[1], mine_down, down_sem.at[2])
    downs = [
        Chain([Ring(axes["ctx"], terms, down_ref.shape[1], *take(4), first)], [down_ref.at[expert]])
        for expert, (terms, first) in enumerate(
            (([down_sum_ref], down_sum_hbm), ([mine_down, came_down], None))
        )
    ]
    chains = []
    for (names, rows), array, out in zip(
        plan, (wq_grad, wkv_grad, wo_sum_ref), (wq_out, wkv_out, wo_out)
    ):
        rings, stores, source = [], [], array
        for name in names:
            rows //= axes[name].count
            if name == "ctx":
                rings.append(Direct(axes[name], source, rows, *take(3)))
            else:
                first = wo_sum_hbm if source is wo_sum_ref else None
                rings.append(Ring(axes[name], [source], rows, *take(4), first))
            source = out if name == names[-1] else take(1)[0]
            stores.append(source)
        chains.append(Chain(rings, stores))
    query, kv, out_chain = chains
    totals = [Total(axes[name], gains_ref, *take(3)) for name in FULL_AXES]
    signal_and_wait([device for axis in axes.values() for device in axis.others()])

    quarter = x_hbm.shape[0] // 4

    def load_mid_grad(part):
        band = slice(part * quarter, (part + 1) * quarter)
        return pltpu.make_async_copy(mg_hbm.at[band, :], mg_band.at[part % 2], mg_sem.at[part])

    piece.step()
    exchange.start()
    out_chain.step()
    downs[0].step()
    for load in loads:
        load.start()
    load_mid_grad(0).start()
    load_mid_grad(1).start()
    load_down.start()
    store_by_owner(wq_grad, normed_ref, dql_ref[...])
    query.step()
    cosine, sine = cos_ref[...], sin_ref[...]
    for head in range(KEY_VALUE_HEADS):
        span = slice(head * HEAD_SIZE, (head + 1) * HEAD_SIZE)
        dkvl[:, span] = rotate_back(dkv_ref[:, span].astype(f32), cosine, sine).astype(bf16)
    dkvl[:, KV_WIDTH:] = dkv_ref[:, KV_WIDTH:]
    store_by_owner(wkv_grad, normed_ref, dkvl[...])
    query.step(2)
    kv.step()
    for load in loads:
        load.wait()
    piece.step()
    downs[0].step()
    dgain = jnp.zeros((1, MODEL_WIDTH), f32)
    for part in range(4):
        band = slice(part * quarter, (part + 1) * quarter)
        grad = dot_nt(dql_ref[band, :], wq_ref[...])
        grad += dot_nt(dkvl[band, :KV_WIDTH], wk_ref[...])
        grad += dot_nt(dkvl[band, KV_WIDTH:], wv_ref[...])
        x = x_ref[band, :].astype(f32)
        r = lax.rsqrt(jnp.mean(x * x, axis=-1, keepdims=True) + epsilon)
        v = grad * gain_ref[...]
        inner = jnp.mean(v * x, axis=-1, keepdims=True)
        dgain += jnp.sum(grad * x * r, axis=0, keepdims=True)
        load_mid_grad(part).wait()
        mid_grad = mg_band[part % 2]
        dx_ref[band, :] = (mid_grad + r * v - x * (r * r * r * inner)).astype(bf16)
        if part < 2:
            load_mid_grad(part + 2).start()
        if part == 1:
            kv.step()
    gains_ref[0:1, :] = dgain
    gains_ref[1:2, :] = ffn_gain_ref[...]
    gains_ref[2:, :] = jnp.zeros((GAIN_ROWS - 2, MODEL_WIDTH), f32)
    out_chain.step(2)
    totals[0].run()
    totals[1].run()
    totals[2].run()
    piece.step()
    downs[0].step()
    query.step(2)
    kv.step()
    load_down.wait()
    exchange.wait_recv()
    downs[1].step()
    out_chain.step()
    totals[3].run()
    kv.step(2)
    query.step(2)
    out_chain.step()
    downs[1].step()
    kv.step(2)
    piece.step()
    downs[0].step()
    query.step()
    downs[1].step()
    kv.step()
    everything = [query, kv, downs[1], downs[0], out_chain, piece]
    while any(chain.done < len(chain.hops) for chain in everything):
        for chain in everything:
            chain.step()
    for chain in everything:
        chain.finish()
    exchange.wait_send()


def last_part(
    piece, down_sum, mine_down, other_down, dql, dkv, normed, wq, wk, wv, cosine, sine, x, gain,
    mg, ffn_gain_part, wo_sum,
):
    counts = sizes()
    n = counts["ctx"]
    full = FULL_AXES if ordered_in_kernel() else FULL_AXES[:3]
    widths = (MODEL_WIDTH, 2 * KV_WIDTH, MODEL_WIDTH)
    plan = [(full, MODEL_WIDTH), (full, MODEL_WIDTH), (full[2:], wo_sum.shape[0])]
    share, down_share = piece.shape[0] // n, mine_down.shape[1] // n
    shapes = [
        jax.ShapeDtypeStruct((share, 2 * FF), f32),
        jax.ShapeDtypeStruct((EXP_DEV, down_share, mine_down.shape[2]), f32),
        jax.ShapeDtypeStruct(x.shape, bf16),
        jax.ShapeDtypeStruct((GAIN_ROWS, MODEL_WIDTH), f32),
    ]
    scratch = [
        pltpu.VMEM((MODEL_WIDTH, MODEL_WIDTH), bf16),
        pltpu.VMEM((MODEL_WIDTH, 2 * KV_WIDTH), bf16),
        pltpu.VMEM((x.shape[0], 2 * KV_WIDTH), bf16),
        pltpu.VMEM((2, x.shape[0] // 4, MODEL_WIDTH), f32),
        pltpu.SemaphoreType.DMA((4,)),
    ]
    scratch += [
        pltpu.VMEM(a.shape, bf16) for a in (piece, down_sum, wo_sum, wq, wk, wv, x)
    ]
    scratch.append(pltpu.SemaphoreType.DMA((7,)))
    scratch += ring_buffers(n, 1, share, 2 * FF)
    scratch += [pltpu.VMEM(mine_down.shape[1:], bf16)] * 2 + [pltpu.SemaphoreType.DMA((3,))]
    for terms in (1, 2):
        scratch += ring_buffers(n, terms, down_share, mine_down.shape[2])
    for (names, rows), width in zip(plan, widths):
        for name in names:
            rows //= counts[name]
            scratch += ring_buffers(counts[name], 1, rows, width)[name == "ctx" :]
            if name != names[-1]:
                scratch.append(pltpu.VMEM((rows, width), bf16))
        shapes.append(jax.ShapeDtypeStruct((rows, width), f32 if "ctx" in names else bf16))
    for name in FULL_AXES:
        hops = counts[name] - 1
        scratch += [
            pltpu.VMEM((hops, GAIN_ROWS, MODEL_WIDTH), f32),
            pltpu.SemaphoreType.DMA((hops,)),
            pltpu.SemaphoreType.DMA((hops,)),
        ]
    vmem, hbm = pl.BlockSpec(memory_space=pltpu.VMEM), pl.BlockSpec(memory_space=pl.ANY)
    gate_up, down, dx, gains, *attention = pl.pallas_call(
        functools.partial(last_kernel, plan),
        in_specs=[hbm] * 4 + [vmem] * 3 + [hbm] * 3 + [vmem] * 2 + [hbm, vmem, hbm, vmem, hbm],
        out_specs=(vmem,) * 7,
        out_shape=tuple(shapes),
        scratch_shapes=scratch,
        compiler_params=params(collective_id=2, has_side_effects=True),
        cost_estimate=cost(1e10, 4e7),
        name="last_part",
    )(
        piece, down_sum, mine_down, other_down, dql, dkv, normed, wq, wk, wv, cosine, sine, x, gain,
        mg, ffn_gain_part, wo_sum,
    )
    if "ctx" not in full:
        attention = [
            scatter_axis(a.reshape(n, a.shape[0] // n, a.shape[1]), "ctx").astype(f32)
            for a in attention
        ]
    return gate_up, down, dx, gains, attention


def shifted(value, axis, steps):
    count = lax.axis_size(axis)
    return lax.ppermute(value, axis, [(i, (i + steps) % count) for i in range(count)])


def chip_shift(value, steps):
    count = lax.axis_size("exp")
    return lax.ppermute(value, "exp", [(i, (i + 2 * steps) % count) for i in range(count)])


def ring_part(parts, index, count, step, axis=0):
    return lax.dynamic_index_in_dim(parts, (index - 1 - step) % count, axis, keepdims=False)


def add_low(a, b):
    return (a.astype(f32) + b.astype(f32)).astype(bf16)


def ring_scatter(parts, shift, index, count, axis=0):
    total = ring_part(parts, index, count, 0, axis)
    for step in range(1, count):
        total = add_low(shift(total), ring_part(parts, index, count, step, axis))
    return total


def by_owner(array, axis):
    dp, ctx, exp = (lax.axis_size(a) for a in ("dp", "ctx", "exp"))
    size = array.shape[axis]
    before, after = array.shape[:axis], array.shape[axis + 1 :]
    parts = array.reshape(*before, dp, ctx, exp // 2, 2, size // (dp * ctx * exp), *after)
    order = list(range(axis)) + [axis + i for i in (3, 2, 0, 1, 4)]
    order += list(range(axis + 5, parts.ndim))
    return jnp.transpose(parts, order).reshape(array.shape)


def scatter_axis(parts, axis):
    return ring_scatter(
        parts, lambda v: shifted(v, axis, 1), lax.axis_index(axis), lax.axis_size(axis)
    )


def tie(*values):
    return lax.optimization_barrier(values)


def per_device(
    tokens, attn_gain, w_query, key_matrix, value_matrix, w_out, ffn_gain, expert_gate_up,
    expert_down, expert_ids, gate_weights, span_order, out_grad,
):
    ctx_size, exp_size = lax.axis_size("ctx"), lax.axis_size("exp")
    ctx_here, exp_here = lax.axis_index("ctx"), lax.axis_index("exp")
    experts = EXP_DEV * exp_size
    x, g = tokens[0], out_grad[0]
    rows = x.shape[0]
    capacity = rows * TOPK * 5 // (4 * experts)
    gain_one, gain_two = attn_gain[None, :], ffn_gain[None, :]
    offsets = jnp.arange(HALF, dtype=jnp.int32)

    def device_positions(device):
        pair = lax.dynamic_slice_in_dim(span_order[0], 2 * device, 2, 0)
        return (pair[:, None] * HALF + offsets[None, :]).reshape(-1)

    sources = [(ctx_here - s) % ctx_size for s in range(ctx_size)]
    key_positions = [device_positions(s) for s in sources]
    positions = key_positions[0]
    exponent = jnp.arange(HEAD_SIZE // 2, dtype=f32) * (-2.0 / HEAD_SIZE)
    frequency = jnp.power(f32(rope_base), exponent)
    angles = positions.astype(f32)[:, None] * frequency[None, :]
    cosine, sine = jnp.cos(angles), jnp.sin(angles)
    cosine = jnp.concatenate([cosine, cosine], axis=1)
    sine = jnp.concatenate([-sine, sine], axis=1)

    kpos_rows = jnp.stack(key_positions)[:, None, :]
    normed, q, kv, att, att_low, lse, mid, nf, g_all, *routing = forward_to_experts(
        x, gain_one, key_matrix, value_matrix, cosine, sine, positions[:, None],
        kpos_rows, gain_two, w_query, w_out, g, expert_ids[0].T,
        gate_weights[0].T,
    )

    dx_chip, y_chip, dx_far, y_far, *kept, _ = expert_blocks(
        capacity, *routing, nf, g_all, expert_gate_up, expert_down
    )
    slot_rows, hidden, slot_grad, projected_grad = (
        a.reshape(EXP_DEV, exp_size * capacity, a.shape[-1]) for a in kept
    )
    nf_grad_terms = [dx_chip] + [
        chip_shift(dx_far[s - 1], -s) for s in range(1, exp_size // 2)
    ]
    dp_size, dp_here = lax.axis_size("dp"), lax.axis_index("dp")
    theirs = weight_grad(
        0, 1, (dp_here - 1) % dp_size, MODEL_WIDTH // dp_size, slot_rows, projected_grad
    )[0]
    if not ordered_in_kernel():
        normed, att_low = by_owner(normed, 1), by_owner(att_low, 1)
    slot_rows, theirs = tie(slot_rows, theirs)
    came = shifted(theirs, "dp", 1)
    theirs_next, mine, mine_next, other_down, mine_down = other_weight_grads(
        dp_here, dp_size, slot_rows, projected_grad, hidden, slot_grad
    )
    nf_grad_terms, mine, y_far = tie(nf_grad_terms, mine, y_far)

    mid_grad, att_grad, delta, ffn_gain_part, w_out_grad = middle_backward(
        nf_grad_terms, mid, g, gain_two, w_out, att, att_low
    )
    att_grad, came = tie(att_grad, came)
    y_terms = [y_chip] + [chip_shift(y_far[s - 1], -s) for s in range(1, exp_size // 2)]

    dql, dkv, gate_up_first, gate_up_next, down_sum, w_out_sum = attention_backward(
        q, att_grad, kv, lse, delta, kpos_rows, positions[None, :],
        cosine, sine, mine, came, w_out_grad, theirs_next, mine_next, other_down, mine_down,
    )
    gate_up_second, down_share, tokens_grad, gains, attention = last_part(
        gate_up_next, down_sum, mine_down, other_down, dql, dkv, normed, w_query, key_matrix,
        value_matrix, cosine, sine, x, gain_one, mid_grad, ffn_gain_part, w_out_sum,
    )
    w_query_share, w_kv_share, w_out_share = attention
    layer_output = mid
    for term in y_terms:
        layer_output = layer_output + term.astype(f32)
    layer_output = layer_output.astype(bf16)
    owner = (lax.axis_index("dp") * ctx_size + ctx_here) * exp_size + exp_here
    gain_share = MODEL_WIDTH // (dp_size * ctx_size * exp_size)
    gains = lax.dynamic_slice_in_dim(gains, owner * gain_share, gain_share, 1)
    return (
        layer_output[None],
        tokens_grad[None],
        gains[0],
        w_query_share,
        w_kv_share[:, :KV_WIDTH],
        w_kv_share[:, KV_WIDTH:],
        w_out_share,
        gains[1],
        jnp.stack([gate_up_first, gate_up_second]),
        down_share,
    )


def solution(mesh):
    by_row = P(("dp", "exp"), "ctx", None)
    share = P(("dp", "ctx", "exp"))
    share_rows = P(("dp", "ctx", "exp"), None)
    return jax.shard_map(
        per_device,
        mesh=mesh,
        in_specs=(
            by_row, P(), P(), P(), P(), P(), P(), P("exp", None, None), P("exp", None, None),
            by_row, by_row, P(("dp", "exp"), None), by_row,
        ),
        out_specs=(
            by_row, by_row, share, share_rows, share_rows, share_rows, share_rows, share,
            P("exp", ("dp", "ctx"), None), P("exp", ("dp", "ctx"), None),
        ),
        check_vma=False,
    )
```

```python
import functools
import math

import jax
import jax.numpy as jnp
from jax import lax
from jax.experimental import pallas as pl
from jax.experimental.pallas import tpu as pltpu
from jax.sharding import PartitionSpec as P

MODEL_WIDTH = 1536
QUERY_HEADS = 12
KEY_VALUE_HEADS = 2
GROUP = QUERY_HEADS // KEY_VALUE_HEADS
HEAD_SIZE = 128
KV_WIDTH = KEY_VALUE_HEADS * HEAD_SIZE
FF = 768
TOPK = 4
EXP_DEV = 2
TOK_DEV = 512
HALF = 256

epsilon = 1e-06
rope_base = 1000000.0
masked_score = -1e30
score_scale = HEAD_SIZE ** (-0.5)
score_to_log2 = score_scale * math.log2(math.e)
gelu_c = math.sqrt(2.0 / math.pi)

f32 = jnp.float32
bf16 = jnp.bfloat16
NT = (((1,), (1,)), ((), ()))
TN = (((0,), (0,)), ((), ()))
VMEM_BYTES = 63 * 1024 * 1024
MESH = pl.DeviceIdType.MESH


def dot(a, b):
    return jnp.dot(a, b, preferred_element_type=f32)


def dot_nt(a, b):
    return lax.dot_general(a, b, NT, preferred_element_type=f32)


def dot_tn(a, b):
    return lax.dot_general(a, b, TN, preferred_element_type=f32)


def params(**more):
    return pltpu.CompilerParams(vmem_limit_bytes=VMEM_BYTES, **more)


def cost(flops, size, exps=0):
    return pl.CostEstimate(flops=int(flops), bytes_accessed=int(size), transcendentals=int(exps))


def whole(shape):
    return pl.BlockSpec(shape, lambda *_: (0,) * len(shape))


def rotate(values, cosine, signed_sine):
    return values * cosine + pltpu.roll(values, HEAD_SIZE // 2, 1) * signed_sine


def rotate_back(values, cosine, signed_sine):
    return values * cosine - pltpu.roll(values, HEAD_SIZE // 2, 1) * signed_sine


HEAD_ROWS = 16


class Gather:
    def __init__(self, own, slots, send_sem, recv_sem):
        self.own, self.slots, self.send_sem, self.recv_sem = own, slots, send_sem, recv_sem
        self.chips = lax.axis_size("exp") // 2
        exp = lax.axis_index("exp")
        core, chip = lax.rem(exp, 2), exp // 2
        self.other = {"exp": chip * 2 + 1 - core}
        self.ahead = [
            {"exp": lax.rem(chip + s, self.chips) * 2 + core} for s in range(self.chips)
        ]
        self.behind = [
            {"exp": lax.rem(chip + self.chips - s, self.chips) * 2 + core}
            for s in range(self.chips)
        ]

    def neighbours(self):
        if self.chips == 2:
            return [self.other, self.ahead[1]]
        return [self.other] + self.ahead[1:]

    def copy(self, slot):
        source, device = self.own, self.other
        if slot > 1 and slot % 2 == 0:
            source = self.slots.at[slot + 1]
        elif slot > 1:
            device = self.ahead[slot // 2]
        return remote(
            source, self.slots.at[slot], self.send_sem.at[slot], self.recv_sem.at[slot], device
        )

    def keep(self):
        return pltpu.make_async_copy(self.own, self.slots.at[0], self.recv_sem.at[0])

    def start(self):
        self.copy(1).start()
        for s in range(1, self.chips):
            self.copy(2 * s + 1).start()

    def cross(self):
        for s in range(1, self.chips):
            self.copy(2 * s + 1).wait_recv()
            self.copy(2 * s).start()

    def finish(self):
        self.copy(1).wait_recv()
        for s in range(1, self.chips):
            self.copy(2 * s).wait_recv()
        self.finish_sends()

    def finish_sends(self):
        for slot in range(1, 2 * self.chips):
            self.copy(slot).wait_send()


def routes(ids_ref, gates_ref, place_cols, routing):
    rows = ids_ref.shape[1]
    lane = lax.broadcasted_iota(jnp.int32, (rows, HEAD_SIZE), 1).astype(f32)
    both = jnp.concatenate([ids_ref[...].astype(f32), gates_ref[...]], axis=0).T
    member = jnp.zeros((rows, HEAD_SIZE), f32)
    gates = jnp.zeros((rows, HEAD_SIZE), f32)
    for k in range(TOPK):
        hit = both[:, k : k + 1] == lane
        member = jnp.where(hit, 1.0, member)
        gates = jnp.where(hit, both[:, TOPK + k : TOPK + k + 1], gates)
    later = lax.broadcasted_iota(jnp.int32, (rows, rows), 0)
    earlier = later > lax.broadcasted_iota(jnp.int32, (rows, rows), 1)
    place = dot(earlier.astype(bf16), member.astype(bf16))
    place = jnp.where(member > 0.0, place, -1.0)
    place_cols[...] = place
    routing[0] = place.T[: routing.shape[1], :]
    routing[1] = gates.T[: routing.shape[1], :]


def forward_kernel(
    n, x_ref, gain_ref, wk_ref, wv_ref, cos_ref, sin_ref, qpos_ref, kpos_ref, ffn_gain_ref, wq_hbm,
    wo_hbm, g_hbm, ids_ref, gates_ref, normed_ref, q_ref, kv_ref, att_ref, att_low_ref, lse_ref,
    mid_ref, nf_ref, g_all, place_cols_all, routing_all, wq_ref, wo_ref, tops, totals, place_cols,
    routing, load_sem, send_sem, recv_sem, *gather_sems,
):
    load_q = pltpu.make_async_copy(wq_hbm, wq_ref, load_sem.at[0])
    load_o = pltpu.make_async_copy(wo_hbm, wo_ref, load_sem.at[1])
    load_q.start()
    load_o.start()
    ctx = Axis("ctx")
    gathers = [
        Gather(g_hbm, g_all, *gather_sems[0:2]),
        Gather(place_cols, place_cols_all, *gather_sems[2:4]),
        Gather(routing, routing_all, *gather_sems[4:6]),
    ]
    signal_and_wait(ctx.neighbours() + gathers[0].neighbours())

    def pass_on(step):
        return remote(
            kv_ref.at[step], kv_ref.at[step + 1], send_sem.at[step], recv_sem.at[step], ctx.next
        )

    rows = x_ref.shape[0]
    x = x_ref[...].astype(f32)
    r = lax.rsqrt(jnp.mean(x * x, axis=-1, keepdims=True) + epsilon)
    normed_ref[...] = (x * r * gain_ref[...][None, :]).astype(bf16)
    normed = normed_ref[...]
    cosine, sine = cos_ref[...], sin_ref[...]
    keys = dot(normed, wk_ref[...])
    for head in range(KEY_VALUE_HEADS):
        span = slice(head * HEAD_SIZE, (head + 1) * HEAD_SIZE)
        kv_ref[0, :, span] = rotate(keys[:, span], cosine, sine).astype(bf16)
    kv_ref[0, :, KV_WIDTH:] = dot(normed, wv_ref[...]).astype(bf16)
    pass_on(0).start()
    routes(ids_ref, gates_ref, place_cols, routing)
    for gather in gathers:
        gather.start()
        gather.keep().start()
    load_q.wait()
    for start in range(0, MODEL_WIDTH, WIDTH_TILE):
        queries = dot(normed, wq_ref[:, start : start + WIDTH_TILE])
        for offset in range(0, WIDTH_TILE, HEAD_SIZE):
            span = slice(start + offset, start + offset + HEAD_SIZE)
            part = queries[:, offset : offset + HEAD_SIZE]
            q_ref[:, span] = rotate(part, cosine, sine).astype(bf16)

    for step in range(n):
        if step:
            pass_on(step - 1).wait_recv()
            if step < n - 1:
                pass_on(step).start()
        allowed = kpos_ref[step] <= qpos_ref[...]

        def one_group(group, carry):
            keys = kv_ref[step, :, pl.ds(pl.multiple_of(group * HEAD_SIZE, HEAD_SIZE), HEAD_SIZE)]
            start = pl.multiple_of(KV_WIDTH + group * HEAD_SIZE, HEAD_SIZE)
            values = kv_ref[step, :, pl.ds(start, HEAD_SIZE)]
            for member in range(GROUP):
                head = group * GROUP + member
                columns = pl.ds(pl.multiple_of(head * HEAD_SIZE, HEAD_SIZE), HEAD_SIZE)
                lane = slice(member, member + 1)
                scores = jnp.where(allowed, dot_nt(q_ref[:, columns], keys), masked_score)
                top = jnp.max(scores, axis=-1, keepdims=True) * score_to_log2
                if step:
                    before = tops[group, :, lane]
                    top = jnp.maximum(before, top)
                    rescale = jnp.exp2(before - top)
                weights = jnp.exp2(scores * score_to_log2 - top)
                total = jnp.sum(weights, axis=-1, keepdims=True)
                out = dot(weights.astype(bf16), values)
                if step:
                    total += totals[group, :, lane] * rescale
                    out += att_ref[:, columns] * rescale
                if step < n - 1:
                    tops[group, :, lane] = top
                    totals[group, :, lane] = total
                else:
                    out /= total
                    att_low_ref[:, columns] = out.astype(bf16)
                    tops[group, :, lane] = top + jnp.log2(total)
                att_ref[:, columns] = out
            return carry

        lax.fori_loop(0, KEY_VALUE_HEADS, one_group, 0)
    for group in range(KEY_VALUE_HEADS):
        lse_ref[group * GROUP : (group + 1) * GROUP, :] = tops[group].T[:GROUP, :]
    lse_ref[QUERY_HEADS:, :] = jnp.zeros((HEAD_ROWS - QUERY_HEADS, rows), f32)
    for gather in gathers:
        gather.cross()
    load_o.wait()
    half = rows // 2
    for part in range(2):
        band = slice(part * half, (part + 1) * half)
        mid = x_ref[band, :].astype(f32) + dot(att_low_ref[band, :], wo_ref[...])
        mid_ref[band, :] = mid
        r = lax.rsqrt(jnp.mean(mid * mid, axis=-1, keepdims=True) + epsilon)
        nf_ref[band, :] = (mid * r * ffn_gain_ref[...][None, :]).astype(bf16)
    for step in range(n - 1):
        pass_on(step).wait_send()
    for gather in gathers:
        gather.keep().wait()
        gather.finish()


def forward_to_experts(
    x, gain, wk, wv, cosine, sine, qpos_col, kpos_rows, ffn_gain, wq, wo, g, ids, gates
):
    exp_size = lax.axis_size("exp")
    routing = (2, EXP_DEV * exp_size, x.shape[0])
    rows, n = x.shape[0], kpos_rows.shape[0]
    vmem = pl.BlockSpec(memory_space=pltpu.VMEM)
    hbm = pl.BlockSpec(memory_space=pl.ANY)
    wide = (rows, MODEL_WIDTH)
    return pl.pallas_call(
        functools.partial(forward_kernel, n),
        in_specs=[vmem] * 9 + [hbm] * 3 + [vmem] * 2,
        out_specs=(vmem,) * 8 + (hbm,) * 3,
        out_shape=(
            jax.ShapeDtypeStruct(wide, bf16),
            jax.ShapeDtypeStruct(wide, bf16),
            jax.ShapeDtypeStruct((n, rows, 2 * KV_WIDTH), bf16),
            jax.ShapeDtypeStruct(wide, f32),
            jax.ShapeDtypeStruct(wide, bf16),
            jax.ShapeDtypeStruct((HEAD_ROWS, rows), f32),
            jax.ShapeDtypeStruct(wide, f32),
            jax.ShapeDtypeStruct(wide, bf16),
            jax.ShapeDtypeStruct((exp_size, *g.shape), bf16),
            jax.ShapeDtypeStruct((exp_size, rows, HEAD_SIZE), f32),
            jax.ShapeDtypeStruct((exp_size, *routing), f32),
        ),
        scratch_shapes=[
            pltpu.VMEM((MODEL_WIDTH, MODEL_WIDTH), bf16),
            pltpu.VMEM((MODEL_WIDTH, MODEL_WIDTH), bf16),
            pltpu.VMEM((KEY_VALUE_HEADS, rows, HEAD_SIZE), f32),
            pltpu.VMEM((KEY_VALUE_HEADS, rows, HEAD_SIZE), f32),
            pltpu.VMEM((rows, HEAD_SIZE), f32),
            pltpu.VMEM(routing, f32),
            pltpu.SemaphoreType.DMA((2,)),
            pltpu.SemaphoreType.DMA((n - 1,)),
            pltpu.SemaphoreType.DMA((n - 1,)),
        ]
        + [pltpu.SemaphoreType.DMA((exp_size,))] * 6,
        compiler_params=params(collective_id=3, has_side_effects=True),
        cost_estimate=cost(
            4 * n * rows * rows * MODEL_WIDTH + 5 * rows * MODEL_WIDTH * MODEL_WIDTH, 4e7,
            n * rows * rows * QUERY_HEADS,
        ),
        name="forward_to_experts",
    )(x, gain, wk, wv, cosine, sine, qpos_col, kpos_rows, ffn_gain, wq, wo, g, ids, gates)


FF_TILE = 256
WIDTH_TILE = 512


def expert_kernel(
    place_cols_ref, routing_ref, nf_hbm, g_ref, wgu_ref, wd_ref, dx_chip, y_chip, dx_far,
    y_far, rows_ref, hidden_ref, slot_grad_ref, pg_ref, x_all, x_ref, place, result, rows_grad,
    dx_out, y_out, dx_came, y_came, load_sem, gather_send, gather_recv, back_send, back_recv,
):
    block, expert = pl.program_id(0), pl.program_id(1)
    capacity = rows_ref.shape[-2]
    tokens = x_ref.shape[0]
    gather = Gather(nf_hbm, x_all, gather_send, gather_recv)
    chips = gather.chips

    def load(source):
        copy = pltpu.make_async_copy(source, x_ref, load_sem.at[0])
        copy.start()
        copy.wait()

    def back(slot):
        return [
            remote(out, came.at[slot], back_send.at[i, slot], back_recv.at[i, slot], gather.other)
            for i, (out, came) in enumerate(((dx_out, dx_came), (y_out, y_came)))
        ]

    @pl.when((block == 0) & (expert == 0))
    def _():
        signal_and_wait(gather.neighbours())
        gather.start()
        load(nf_hbm)

    @pl.when((block == 1) & (expert == 0))
    def _():
        gather.copy(1).wait_recv()
        load(x_all.at[1])

    for s in range(1, chips):

        @pl.when((block == 2 * s) & (expert == 0))
        def _():
            if s == 1:
                gather.cross()
            gather.copy(2 * s).wait_recv()
            load(x_all.at[2 * s])

        @pl.when((block == 2 * s + 1) & (expert == 0))
        def _():
            load(x_all.at[2 * s + 1])

    mine = lax.axis_index("exp") * EXP_DEV + expert
    slot_r = lax.broadcasted_iota(jnp.int32, (capacity, tokens), 0).astype(f32)
    slot_c = lax.broadcasted_iota(jnp.int32, (tokens, capacity), 1).astype(f32)
    match = slot_r == routing_ref[0, 0, pl.ds(mine, 1), :]
    pick = match.astype(bf16)
    lane = lax.broadcasted_iota(jnp.int32, (tokens, HEAD_SIZE), 1)
    place_col = jnp.sum(jnp.where(lane == mine, place_cols_ref[0], 0.0), axis=1, keepdims=True)
    place[expert] = (slot_c == place_col).astype(bf16)
    gate_row = routing_ref[0, 1, pl.ds(mine, 1), :]
    gates = jnp.sum(jnp.where(match, gate_row, 0.0), axis=1, keepdims=True)
    for start in range(0, MODEL_WIDTH, WIDTH_TILE):
        span = slice(start, start + WIDTH_TILE)
        rows_ref[0, 0, :, span] = dot(pick, x_ref[:, span]).astype(bf16)
        slot_grad_ref[0, 0, :, span] = (dot(pick, g_ref[0, :, span]) * gates).astype(bf16)
    rows = rows_ref[0, 0]
    slot_grad = slot_grad_ref[0, 0]
    for start in range(0, FF, FF_TILE):
        span = slice(start, start + FF_TILE)
        up_span = slice(FF + start, FF + start + FF_TILE)
        gate = dot(rows, wgu_ref[0, :, span])
        up = dot(rows, wgu_ref[0, :, up_span])
        hidden_grad = dot_nt(slot_grad, wd_ref[0, span, :])
        square = gate * gate
        tangent = jnp.tanh(gate * (gelu_c + (gelu_c * 0.044715) * square))
        half_plus = 0.5 + 0.5 * tangent
        activated = gate * half_plus
        slope = half_plus + activated * (1.0 - tangent) * (
            gelu_c + (3.0 * 0.044715 * gelu_c) * square
        )
        hidden_ref[0, 0, :, span] = (activated * up).astype(bf16)
        pg_ref[0, 0, :, span] = (hidden_grad * up * slope).astype(bf16)
        pg_ref[0, 0, :, up_span] = (hidden_grad * activated).astype(bf16)
    hidden = hidden_ref[0, 0]
    projected_grad = pg_ref[0, 0]
    for start in range(0, MODEL_WIDTH, WIDTH_TILE):
        span = slice(start, start + WIDTH_TILE)
        result[expert, :, span] = (dot(hidden, wd_ref[0, :, span]) * gates).astype(bf16)
        rows_grad[expert, :, span] = dot_nt(projected_grad, wgu_ref[0, span, :]).astype(bf16)

    last = expert == EXP_DEV - 1
    for sent in [1] + [2 * s for s in range(1, chips)]:

        @pl.when(last & (block == sent + 1))
        def _():
            for copy in back(sent // 2):
                copy.wait_send()

    @pl.when(last)
    def _():
        both = jnp.concatenate([place[e] for e in range(EXP_DEV)], axis=1)
        for start in range(0, MODEL_WIDTH, WIDTH_TILE):
            span = slice(start, start + WIDTH_TILE)
            for out_ref, terms in ((y_out, result), (dx_out, rows_grad)):
                stacked = terms[:, :, span].reshape(EXP_DEV * capacity, WIDTH_TILE)
                out_ref[:, span] = dot(both, stacked).astype(bf16)

    @pl.when(last & (block == 0))
    def _():
        dx_chip[...] = dx_out[...]
        y_chip[...] = y_out[...]

    for sent in [1] + [2 * s for s in range(1, chips)]:

        @pl.when(last & (block == sent))
        def _():
            for copy in back(sent // 2):
                copy.start()

    def add(target, own, came):
        for start in range(0, tokens, HEAD_SIZE):
            band = slice(start, start + HEAD_SIZE)
            total = own[band, :].astype(f32) + came[band, :].astype(f32)
            target[band, :] = total.astype(bf16)

    for s in range(1, chips):

        @pl.when(last & (block == 2 * s + 1))
        def _():
            for copy in back(s):
                copy.wait_recv()
            add(dx_far.at[s - 1], dx_out, dx_came.at[s])
            add(y_far.at[s - 1], y_out, y_came.at[s])

    @pl.when(last & (block == 2 * chips - 1))
    def _():
        for copy in back(0):
            copy.wait_recv()
        add(dx_chip, dx_chip, dx_came.at[0])
        add(y_chip, y_chip, y_came.at[0])
        gather.finish_sends()


def expert_blocks(capacity, place_cols, routing, nf, g_all, wgu, wd):
    blocks, tokens, _ = g_all.shape
    chips = blocks // 2
    kept_shapes = tuple(
        jax.ShapeDtypeStruct((EXP_DEV, blocks, capacity, width), bf16)
        for width in (MODEL_WIDTH, FF, MODEL_WIDTH, 2 * FF)
    )
    kept_specs = tuple(
        pl.BlockSpec((1, 1, capacity, s.shape[-1]), lambda b, e: (e, b, 0, 0)) for s in kept_shapes
    )
    flops = blocks * EXP_DEV * 2 * capacity * (4 * tokens * MODEL_WIDTH + 9 * MODEL_WIDTH * FF)
    wide = (tokens, MODEL_WIDTH)
    result = jax.ShapeDtypeStruct(wide, bf16)
    far = jax.ShapeDtypeStruct((chips - 1, *wide), bf16)
    hbm = pl.BlockSpec(memory_space=pl.ANY)

    def once(shape):
        return pl.BlockSpec(
            shape, lambda b, e: (0,) * len(shape), pipeline_mode=pl.Buffered(1)
        )

    return pl.pallas_call(
        expert_kernel,
        grid=(blocks, EXP_DEV),
        in_specs=[
            pl.BlockSpec((1, tokens, HEAD_SIZE), lambda b, e: (b, 0, 0)),
            pl.BlockSpec((1, *routing.shape[1:]), lambda b, e: (b, 0, 0, 0)),
            hbm,
            pl.BlockSpec((1, tokens, MODEL_WIDTH), lambda b, e: (b, 0, 0)),
            pl.BlockSpec((1, MODEL_WIDTH, 2 * FF), lambda b, e: (e, 0, 0)),
            pl.BlockSpec((1, FF, MODEL_WIDTH), lambda b, e: (e, 0, 0)),
        ],
        out_specs=(once(wide), once(wide), once(far.shape), once(far.shape)) + kept_specs + (hbm,),
        out_shape=(result, result, far, far)
        + kept_shapes
        + (jax.ShapeDtypeStruct((blocks, *wide), bf16),),
        scratch_shapes=[
            pltpu.VMEM(wide, bf16),
            pltpu.VMEM((EXP_DEV, tokens, capacity), bf16),
            pltpu.VMEM((EXP_DEV, capacity, MODEL_WIDTH), bf16),
            pltpu.VMEM((EXP_DEV, capacity, MODEL_WIDTH), bf16),
            pltpu.VMEM(wide, bf16),
            pltpu.VMEM(wide, bf16),
            pltpu.VMEM((chips, *wide), bf16),
            pltpu.VMEM((chips, *wide), bf16),
            pltpu.SemaphoreType.DMA((1,)),
            pltpu.SemaphoreType.DMA((blocks,)),
            pltpu.SemaphoreType.DMA((blocks,)),
            pltpu.SemaphoreType.DMA((2, chips)),
            pltpu.SemaphoreType.DMA((2, chips)),
        ],
        compiler_params=params(collective_id=4, has_side_effects=True),
        cost_estimate=cost(flops, 6e7),
        name="expert_blocks",
    )(place_cols, routing, nf, g_all, wgu, wd)


GRAD_TILE = 384


def weight_grad_kernel(chunk_ref, a_ref, b_ref, out_ref):
    out_ref[0] = dot_tn(a_ref[0], b_ref[0]).astype(bf16)


def weight_grad(first, experts, chunk, size, a, b):
    slots, width = a.shape[1], b.shape[-1]
    tiles = size // GRAD_TILE
    return pl.pallas_call(
        weight_grad_kernel,
        grid_spec=pltpu.PrefetchScalarGridSpec(
            num_scalar_prefetch=1,
            grid=(experts, tiles),
            in_specs=[
                pl.BlockSpec((1, slots, GRAD_TILE), lambda e, t, c: (first + e, 0, c[0] * tiles + t)),
                pl.BlockSpec((1, slots, width), lambda e, t, c: (first + e, 0, 0)),
            ],
            out_specs=pl.BlockSpec((1, GRAD_TILE, width), lambda e, t, c: (e, t, 0)),
        ),
        out_shape=jax.ShapeDtypeStruct((experts, size, width), bf16),
        compiler_params=params(),
        cost_estimate=cost(2 * experts * slots * size * width, 2e7),
        name="weight_grad",
    )(chunk.reshape(1).astype(jnp.int32), a, b)


def other_weight_grads_kernel(
    dp_ref, rows_ref, pg_ref, hidden_ref, slot_grad_ref, theirs_ref, mine0_ref, mine1_ref,
    other_down_ref, mine_down_ref,
):
    step = pl.program_id(0)
    for first, out_ref in ((0, theirs_ref), (2, mine0_ref), (4, mine1_ref)):

        @pl.when((step == first) | (step == first + 1))
        def _():
            out_ref[...] = dot_tn(rows_ref[0], pg_ref[0]).astype(bf16)

    for place, out_ref in enumerate((other_down_ref, mine_down_ref)):

        @pl.when((step == 6 + place) | (step == 8 + place))
        def _():
            out_ref[0] = dot_tn(hidden_ref[0], slot_grad_ref[0]).astype(bf16)


def other_weight_grads(dp_here, dp_size, slot_rows, pg, hidden, slot_grad):
    assert dp_size == 2 and MODEL_WIDTH // dp_size == 2 * GRAD_TILE and FF // dp_size == GRAD_TILE
    slots = slot_rows.shape[1]
    half = (2 * GRAD_TILE, 2 * FF)

    def gate_up_rows(t, d):
        t = jnp.minimum(t, 5)
        expert = jnp.where((t == 2) | (t == 3), 0, 1)
        place = jnp.where(t < 2, 1 - d[0], d[0])
        return expert, 0, place * 2 + t % 2

    def gate_up_right(t, d):
        return gate_up_rows(t, d)[0], 0, 0

    def down_rows(t, d):
        t = jnp.maximum(t, 6) - 6
        return t // 2, 0, jnp.where(t % 2 == 0, 1 - d[0], d[0])

    def down_right(t, d):
        return down_rows(t, d)[0], 0, 0

    def piece(first):
        return pl.BlockSpec((GRAD_TILE, 2 * FF), lambda t, d: (jnp.clip(t - first, 0, 1), 0))

    def down(first):
        return pl.BlockSpec(
            (1, GRAD_TILE, MODEL_WIDTH), lambda t, d: (jnp.clip((t - first) // 2, 0, 1), 0, 0)
        )

    return pl.pallas_call(
        other_weight_grads_kernel,
        grid_spec=pltpu.PrefetchScalarGridSpec(
            num_scalar_prefetch=1,
            grid=(10,),
            in_specs=[
                pl.BlockSpec((1, slots, GRAD_TILE), gate_up_rows),
                pl.BlockSpec((1, slots, 2 * FF), gate_up_right),
                pl.BlockSpec((1, slots, GRAD_TILE), down_rows),
                pl.BlockSpec((1, slots, MODEL_WIDTH), down_right),
            ],
            out_specs=(piece(0), piece(2), piece(4), down(6), down(7)),
        ),
        out_shape=(jax.ShapeDtypeStruct(half, bf16),) * 3
        + (jax.ShapeDtypeStruct((EXP_DEV, GRAD_TILE, MODEL_WIDTH), bf16),) * 2,
        compiler_params=params(),
        cost_estimate=cost(10 * 2 * slots * GRAD_TILE * 2 * FF, 5e7),
        name="other_weight_grads",
    )(dp_here.reshape(1).astype(jnp.int32), slot_rows, pg, hidden, slot_grad)


def middle_kernel(*refs):
    count = len(refs) - 13
    parts = refs[:count]
    mid_ref, g_ref, gain_ref, wo_ref, att_ref, att_low_ref = refs[count : count + 6]
    mg_ref, ag_ref, delta_ref, dgain_ref, wo_grad_ref, mgl_ref, delta_cols = refs[count + 6 :]
    rows = mid_ref.shape[0]
    half = rows // 2
    lane = lax.broadcasted_iota(jnp.int32, (half, HEAD_SIZE), 1)
    dgain = jnp.zeros((1, MODEL_WIDTH), f32)
    for part in range(2):
        band = slice(part * half, (part + 1) * half)
        nf_grad = parts[0][band, :].astype(f32)
        for other in parts[1:]:
            nf_grad += other[band, :].astype(f32)
        mid = mid_ref[band, :]
        r = lax.rsqrt(jnp.mean(mid * mid, axis=-1, keepdims=True) + epsilon)
        u = nf_grad * gain_ref[...][None, :]
        inner = jnp.mean(u * mid, axis=-1, keepdims=True)
        grad = g_ref[band, :].astype(f32) + r * u - mid * (r * r * r * inner)
        dgain += jnp.sum(nf_grad * mid * r, axis=0, keepdims=True)
        mg_ref[band, :] = grad
        low = grad.astype(bf16)
        mgl_ref[band, :] = low
        att_grad = dot_nt(low, wo_ref[...]).astype(bf16)
        ag_ref[band, :] = att_grad
        delta = jnp.zeros((half, HEAD_SIZE), f32)
        for head in range(QUERY_HEADS):
            span = slice(head * HEAD_SIZE, (head + 1) * HEAD_SIZE)
            one = jnp.sum(att_grad[:, span].astype(f32) * att_ref[band, span], axis=-1, keepdims=True)
            delta = jnp.where(lane == head, one, delta)
        delta_cols[band, :] = delta
    dgain_ref[...] = dgain
    delta_ref[...] = delta_cols[...].T[: delta_ref.shape[0], :]
    store_by_owner(wo_grad_ref, att_low_ref, mgl_ref[...])


def middle_backward(parts, mid, g, gain, wo, att, att_low):
    rows = mid.shape[0]
    return pl.pallas_call(
        middle_kernel,
        out_shape=(
            jax.ShapeDtypeStruct((rows, MODEL_WIDTH), f32),
            jax.ShapeDtypeStruct((rows, MODEL_WIDTH), bf16),
            jax.ShapeDtypeStruct((HEAD_ROWS, rows), f32),
            jax.ShapeDtypeStruct((1, MODEL_WIDTH), f32),
            jax.ShapeDtypeStruct((MODEL_WIDTH, MODEL_WIDTH), bf16),
        ),
        scratch_shapes=[
            pltpu.VMEM((rows, MODEL_WIDTH), bf16),
            pltpu.VMEM((rows, HEAD_SIZE), f32),
        ],
        compiler_params=params(),
        cost_estimate=cost(4 * rows * MODEL_WIDTH * MODEL_WIDTH, 3e7),
        name="middle_backward",
    )(*parts, mid, g, gain, wo, att, att_low)


def signal_and_wait(neighbours):
    barrier = pltpu.get_barrier_semaphore()
    for neighbour in neighbours:
        pl.semaphore_signal(barrier, inc=1, device_id=neighbour, device_id_type=MESH)
    pl.semaphore_wait(barrier, len(neighbours))


def remote(source, target, send_sem, recv_sem, device):
    return pltpu.make_async_remote_copy(
        src_ref=source, dst_ref=target, send_sem=send_sem, recv_sem=recv_sem,
        device_id=device, device_id_type=MESH,
    )


class Axis:
    def __init__(self, name):
        if name in ("dp", "ctx"):
            self.count, self.me = lax.axis_size(name), lax.axis_index(name)
            place = lambda i: {name: i}
        else:
            exp = lax.axis_index("exp")
            core, chip = lax.rem(exp, 2), exp // 2
            if name == "core":
                self.count, self.me = 2, core
                place = lambda i: {"exp": chip * 2 + i}
            else:
                self.count, self.me = lax.axis_size("exp") // 2, chip
                place = lambda i: {"exp": i * 2 + core}
        self.place = place
        self.next = place(lax.rem(self.me + 1, self.count))
        self.last = place(lax.rem(self.me + self.count - 1, self.count))

    def neighbours(self):
        return [self.next] if self.count == 2 else [self.next, self.last]

    def others(self):
        return [self.place(lax.rem(self.me + s, self.count)) for s in range(1, self.count)]


class Direct:
    def __init__(self, axis, source, rows, recv, send_sem, recv_sem):
        self.axis, self.count, self.source, self.rows = axis, 2, source, rows
        self.recv, self.send_sem, self.recv_sem = recv, send_sem, recv_sem

    def part(self, place):
        return pl.ds(pl.multiple_of(place * self.rows, self.rows), self.rows)

    def copies(self):
        axis, out = self.axis, []
        for s in range(1, axis.count):
            place = lax.rem(axis.me + s, axis.count)
            out.append(
                remote(
                    self.source.at[self.part(place), :], self.recv.at[s - 1],
                    self.send_sem.at[s - 1], self.recv_sem.at[s - 1], axis.place(place),
                )
            )
        return out

    def hop(self, hop):
        if hop == 0:
            for copy in self.copies():
                copy.start()
            return None
        total = self.source[self.part(self.axis.me), :].astype(f32)
        for i, copy in enumerate(self.copies()):
            copy.wait_recv()
            total += self.recv[i].astype(f32)
        return total

    def finish(self):
        for copy in self.copies():
            copy.wait_send()


class Ring:
    def __init__(self, axis, terms, rows, send, recv, send_sem, recv_sem, first=None, own=False):
        self.axis, self.count, self.terms, self.rows = axis, axis.count, terms, rows
        self.first, self.own = terms[0] if first is None else first, own
        self.send, self.recv, self.send_sem, self.recv_sem = send, recv, send_sem, recv_sem

    def here(self, hop):
        part = lax.rem(self.axis.me + self.count - 1 - hop, self.count)
        return pl.ds(pl.multiple_of(part * self.rows, self.rows), self.rows)

    def copy(self, hop):
        if len(self.terms) > 1:
            source = self.send.at[hop]
        elif hop == 0:
            source = self.first.at[self.here(0), :]
        else:
            source = self.send.at[hop - 1]
        return remote(
            source, self.recv.at[hop], self.send_sem.at[hop], self.recv_sem.at[hop], self.axis.next
        )

    def hop(self, hop):
        if hop == 0 and len(self.terms) == 1:
            self.copy(0).start()
            return None
        here = slice(0, self.rows) if self.own else self.here(hop)
        total = self.terms[0][here, :].astype(f32)
        for term in self.terms[1:]:
            total += term[here, :].astype(f32)
        if hop:
            self.copy(hop - 1).wait_recv()
            total += self.recv[hop - 1].astype(f32)
        if hop < self.count - 1:
            self.send[hop - (len(self.terms) == 1)] = total.astype(bf16)
            self.copy(hop).start()
        return total

    def finish(self):
        for hop in range(self.count - 1):
            self.copy(hop).wait_send()


def attention_back_kernel(
    n, q_ref, ag_ref, kv_ref, lse_ref, delta_ref, kpos_ref, qpos_ref, cos_ref, sin_ref, mine_hbm,
    came_hbm, wo_grad_hbm, next_ref, next_mine_ref, down_ref, down_mine_ref, dql_ref, dkv_ref,
    share_ref, next_sum_ref, down_sum_ref, wo_sum_ref, next_came, down_came, next_mine, down_mine,
    mine_ref, came_ref, wo_grad_ref, dq_acc, held, send, recv, send_sem, recv_sem, next_sem,
    load_sem, *scratch,
):
    ctx, core, chip = Axis("ctx"), Axis("core"), Axis("chip")
    right, across = ctx.next, Axis("dp").next
    signal_and_wait(ctx.neighbours() + core.neighbours() + chip.neighbours() + [across])
    core_rows = wo_grad_ref.shape[0]
    own_rows = pl.ds(pl.multiple_of(core.me * core_rows, core_rows), core_rows)
    wo_chain = Chain(
        [
            Ring(core, [wo_grad_ref], core_rows, *scratch[:4], wo_grad_hbm, True),
            Ring(chip, [scratch[4]], core_rows // chip.count, *scratch[5:9]),
        ],
        [scratch[4], wo_sum_ref],
    )
    ring = Ring(ctx, [mine_ref, came_ref], share_ref.shape[0], *scratch[9:])
    first_loads = [
        pltpu.make_async_copy(source, target, load_sem.at[i])
        for i, (source, target) in enumerate(
            ((mine_hbm, mine_ref), (came_hbm, came_ref), (wo_grad_hbm.at[own_rows, :], wo_grad_ref))
        )
    ]
    for load in first_loads:
        load.start()
    exchanges, loads = [], []
    for i, (source, target, mine_hbm, mine) in enumerate(
        (
            (next_ref, next_came, next_mine_ref, next_mine),
            (down_ref.at[0], down_came, down_mine_ref.at[0], down_mine),
        )
    ):
        exchanges.append(remote(source, target, next_sem.at[i, 0], next_sem.at[i, 1], across))
        loads.append(pltpu.make_async_copy(mine_hbm, mine, next_sem.at[i, 2]))
        exchanges[i].start()
        loads[i].start()
    wo_chain.step()
    for load in first_loads:
        load.wait()
    ring.hop(0)

    def dkv_copy(step, group):
        return remote(
            send.at[group, step], recv.at[group, step], send_sem.at[group, step],
            recv_sem.at[group, step], right,
        )

    qpos = qpos_ref[...].astype(f32)
    for step in range(n):
        back = (step + 1) % n
        kpos = jnp.broadcast_to(kpos_ref[back].astype(f32), (8, kpos_ref.shape[-1])).T[:, :1]

        def one_group(group, carry):
            keys = kv_ref[back, :, pl.ds(pl.multiple_of(group * HEAD_SIZE, HEAD_SIZE), HEAD_SIZE)]
            start = pl.multiple_of(KV_WIDTH + group * HEAD_SIZE, HEAD_SIZE)
            values = kv_ref[back, :, pl.ds(start, HEAD_SIZE)]
            dk = dv = None
            for member in range(GROUP):
                head = group * GROUP + member
                columns = pl.ds(pl.multiple_of(head * HEAD_SIZE, HEAD_SIZE), HEAD_SIZE)
                q, ag = q_ref[:, columns], ag_ref[:, columns]
                scores = dot_nt(keys, q)
                weights = jnp.exp2(scores * score_to_log2 - lse_ref[pl.ds(head, 1), :])
                weights = jnp.where(kpos <= qpos, weights, 0.0)
                weights_grad = dot_nt(values, ag)
                score_grad = weights * (weights_grad - delta_ref[pl.ds(head, 1), :]) * score_scale
                score_grad = score_grad.astype(bf16)
                dv_part = dot(weights.astype(bf16), ag)
                dk_part = dot(score_grad, q)
                dv = dv_part if dv is None else dv + dv_part
                dk = dk_part if dk is None else dk + dk_part
                dq = dot_tn(score_grad, keys)
                if step:
                    dq += dq_acc[:, columns]
                dq_acc[:, columns] = dq
            held[group] = jnp.concatenate([dk, dv], axis=1)
            return carry

        lax.fori_loop(0, KEY_VALUE_HEADS, one_group, 0)
        for group in range(KEY_VALUE_HEADS):
            dkv = held[group]
            if step:
                dkv_copy(step - 1, group).wait_recv()
                dkv += recv[group, step - 1].astype(f32)
            if step < n - 1:
                send[group, step] = dkv.astype(bf16)
                dkv_copy(step, group).start()
            else:
                for place in range(2):
                    start = place * KV_WIDTH + group * HEAD_SIZE
                    part = dkv[:, place * HEAD_SIZE : (place + 1) * HEAD_SIZE]
                    dkv_ref[:, start : start + HEAD_SIZE] = part.astype(bf16)
        if step < n - 2:
            ring.hop(step + 1)
        wo_chain.step(2 if step == 0 else 1)
    cosine, sine = cos_ref[...], sin_ref[...]
    for head in range(QUERY_HEADS):
        span = slice(head * HEAD_SIZE, (head + 1) * HEAD_SIZE)
        dql_ref[:, span] = rotate_back(dq_acc[:, span], cosine, sine).astype(bf16)
    share_ref[...] = ring.hop(n - 1)
    ring.finish()
    for step in range(n - 1):
        for group in range(KEY_VALUE_HEADS):
            dkv_copy(step, group).wait_send()
    wo_chain.step(len(wo_chain.hops))
    wo_chain.finish()
    for i, (sum_ref, mine, came) in enumerate(
        ((next_sum_ref, next_mine, next_came), (down_sum_ref, down_mine, down_came))
    ):
        loads[i].wait()
        exchanges[i].wait()
        for start in range(0, sum_ref.shape[0], HEAD_SIZE):
            band = slice(start, start + HEAD_SIZE)
            total = mine[band, :].astype(f32) + came[band, :].astype(f32)
            sum_ref[band, :] = total.astype(bf16)


def attention_backward(
    q, ag, kv, lse, delta, kpos, qpos_row, cosine, sine, mine, came, w_out_grad, following,
    following_mine, other_down, mine_down,
):
    n, keys, _ = kv.shape
    rows = q.shape[0]
    chips = sizes()["chip"]
    wo_rows = w_out_grad.shape[0] // 2
    vmem = pl.BlockSpec(memory_space=pltpu.VMEM)
    hbm = pl.BlockSpec(memory_space=pl.ANY)
    return pl.pallas_call(
        functools.partial(attention_back_kernel, n),
        in_specs=[vmem] * 9 + [hbm] * 7,
        out_specs=(vmem,) * 6,
        out_shape=(
            jax.ShapeDtypeStruct((rows, MODEL_WIDTH), bf16),
            jax.ShapeDtypeStruct((keys, 2 * KV_WIDTH), bf16),
            jax.ShapeDtypeStruct((mine.shape[0] // n, mine.shape[1]), f32),
            jax.ShapeDtypeStruct(following.shape, bf16),
            jax.ShapeDtypeStruct(other_down.shape[1:], bf16),
            jax.ShapeDtypeStruct((wo_rows // chips, MODEL_WIDTH), bf16),
        ),
        scratch_shapes=[
            pltpu.VMEM(following.shape, bf16),
            pltpu.VMEM(other_down.shape[1:], bf16),
            pltpu.VMEM(following.shape, bf16),
            pltpu.VMEM(other_down.shape[1:], bf16),
            pltpu.VMEM(mine.shape, bf16),
            pltpu.VMEM(came.shape, bf16),
            pltpu.VMEM((wo_rows, MODEL_WIDTH), bf16),
            pltpu.VMEM((rows, MODEL_WIDTH), f32),
            pltpu.VMEM((KEY_VALUE_HEADS, keys, 2 * HEAD_SIZE), f32),
            pltpu.VMEM((KEY_VALUE_HEADS, n - 1, keys, 2 * HEAD_SIZE), bf16),
            pltpu.VMEM((KEY_VALUE_HEADS, n - 1, keys, 2 * HEAD_SIZE), bf16),
            pltpu.SemaphoreType.DMA((KEY_VALUE_HEADS, n - 1)),
            pltpu.SemaphoreType.DMA((KEY_VALUE_HEADS, n - 1)),
            pltpu.SemaphoreType.DMA((2, 3)),
            pltpu.SemaphoreType.DMA((3,)),
        ]
        + ring_buffers(2, 1, wo_rows, MODEL_WIDTH)
        + [pltpu.VMEM((wo_rows, MODEL_WIDTH), bf16)]
        + ring_buffers(chips, 1, wo_rows // chips, MODEL_WIDTH)
        + ring_buffers(n, 2, mine.shape[0] // n, mine.shape[1]),
        compiler_params=params(collective_id=1, has_side_effects=True),
        cost_estimate=cost(10 * n * rows * keys * MODEL_WIDTH, 4e7, n * rows * keys * QUERY_HEADS),
        name="attention_backward",
    )(
        q, ag, kv, lse, delta, kpos, qpos_row, cosine, sine, mine, came, w_out_grad, following,
        following_mine, other_down, mine_down,
    )


def ring_buffers(count, terms, rows, width):
    sends = count - 1 if terms > 1 else count - 2
    return [
        pltpu.VMEM((sends, rows, width) if sends else (16, HEAD_SIZE), bf16),
        pltpu.VMEM((count - 1, rows, width), bf16),
        pltpu.SemaphoreType.DMA((count - 1,)),
        pltpu.SemaphoreType.DMA((count - 1,)),
    ]


class Chain:
    def __init__(self, rings, stores):
        self.hops = [(r, h) for r in range(len(rings)) for h in range(rings[r].count)]
        self.rings, self.stores, self.done = rings, stores, 0

    def step(self, times=1):
        for _ in range(times):
            if self.done == len(self.hops):
                return
            index, hop = self.hops[self.done]
            self.done += 1
            ring = self.rings[index]
            total = ring.hop(hop)
            if hop == ring.count - 1:
                store = self.stores[index]
                store[...] = total.astype(store.dtype)

    def finish(self):
        assert self.done == len(self.hops)
        for ring in self.rings:
            ring.finish()


FULL_AXES = ("core", "chip", "dp", "ctx")
OWNER_TILE = 384


def owner_rows():
    counts = sizes()
    return MODEL_WIDTH // (2 * counts["chip"] * counts["dp"] * counts["ctx"])


def ordered_in_kernel():
    return owner_rows() % 16 == 0


def store_by_owner(target, a, b):
    share, counts = owner_rows(), sizes()
    for start in range(0, MODEL_WIDTH, OWNER_TILE):
        rows = dot_tn(a[:, start : start + OWNER_TILE], b).astype(bf16)
        if not ordered_in_kernel():
            target[start : start + OWNER_TILE, :] = rows
            continue
        for offset in range(0, OWNER_TILE, share):
            device = (start + offset) // share
            device, core = divmod(device, 2)
            device, chip = divmod(device, counts["chip"])
            dp, ctx = divmod(device, counts["ctx"])
            place = ((core * counts["chip"] + chip) * counts["dp"] + dp) * counts["ctx"] + ctx
            target[place * share : (place + 1) * share, :] = rows[offset : offset + share, :]


def sizes():
    exp = lax.axis_size("exp")
    return {"core": 2, "chip": exp // 2, "dp": lax.axis_size("dp"), "ctx": lax.axis_size("ctx")}


class Total:
    def __init__(self, axis, value, recv, send_sem, recv_sem):
        self.axis, self.count, self.value, self.recv = axis, axis.count, value, recv
        self.send_sem, self.recv_sem = send_sem, recv_sem

    def copy(self, hop):
        source = self.recv.at[hop - 1] if hop else self.value
        return remote(
            source, self.recv.at[hop], self.send_sem.at[hop], self.recv_sem.at[hop], self.axis.next
        )

    def hop(self, hop):
        if hop == 0:
            self.copy(0).start()
            self.total = self.value[...]
            return None
        self.copy(hop - 1).wait_recv()
        self.total += self.recv[hop - 1]
        if hop < self.count - 1:
            self.copy(hop).start()
        else:
            for sent in range(hop):
                self.copy(sent).wait_send()
        return self.total

    def finish(self):
        pass


GAIN_ROWS = 8


def last_kernel(
    plan, piece_hbm, down_sum_hbm, mine_down_ref, other_down_ref, dql_ref, dkv_ref, normed_ref, wq_hbm,
    wk_hbm, wv_hbm, cos_ref, sin_ref, x_hbm, gain_ref, mg_hbm, ffn_gain_ref, wo_sum_hbm,
    gate_up_ref, down_ref, dx_ref, gains_ref, wq_out, wkv_out, wo_out, wq_grad, wkv_grad, dkvl,
    mg_band, mg_sem, *scratch,
):
    scratch = list(scratch)

    def take(number):
        taken = scratch[:number]
        del scratch[:number]
        return taken

    piece_ref, down_sum_ref, wo_sum_ref, wq_ref, wk_ref, wv_ref, x_ref, load_sem = take(8)
    loads = [
        pltpu.make_async_copy(source, target, load_sem.at[i])
        for i, (source, target) in enumerate(
            (
                (piece_hbm, piece_ref), (down_sum_hbm, down_sum_ref), (wq_hbm, wq_ref),
                (wk_hbm, wk_ref), (wv_hbm, wv_ref), (x_hbm, x_ref), (wo_sum_hbm, wo_sum_ref),
            )
        )
    ]
    axes = {name: Axis(name) for name in FULL_AXES}
    across = axes["dp"].next
    piece = Chain(
        [Ring(axes["ctx"], [piece_ref], gate_up_ref.shape[0], *take(4), piece_hbm)],
        [gate_up_ref],
    )
    came_down, mine_down, down_sem = take(3)
    exchange = remote(
        other_down_ref.at[1], came_down, down_sem.at[0], down_sem.at[1], across
    )
    load_down = pltpu.make_async_copy(mine_down_ref.at[1], mine_down, down_sem.at[2])
    downs = [
        Chain([Ring(axes["ctx"], terms, down_ref.shape[1], *take(4), first)], [down_ref.at[expert]])
        for expert, (terms, first) in enumerate(
            (([down_sum_ref], down_sum_hbm), ([mine_down, came_down], None))
        )
    ]
    chains = []
    for (names, rows), array, out in zip(
        plan, (wq_grad, wkv_grad, wo_sum_ref), (wq_out, wkv_out, wo_out)
    ):
        rings, stores, source = [], [], array
        for name in names:
            rows //= axes[name].count
            if name == "ctx":
                rings.append(Direct(axes[name], source, rows, *take(3)))
            else:
                first = wo_sum_hbm if source is wo_sum_ref else None
                rings.append(Ring(axes[name], [source], rows, *take(4), first))
            source = out if name == names[-1] else take(1)[0]
            stores.append(source)
        chains.append(Chain(rings, stores))
    query, kv, out_chain = chains
    gains = Chain(
        [Total(axes[name], gains_ref, *take(3)) for name in FULL_AXES], [gains_ref] * len(FULL_AXES)
    )
    signal_and_wait([device for axis in axes.values() for device in axis.others()])

    quarter = x_hbm.shape[0] // 4

    def load_mid_grad(part):
        band = slice(part * quarter, (part + 1) * quarter)
        return pltpu.make_async_copy(mg_hbm.at[band, :], mg_band.at[part % 2], mg_sem.at[part])

    piece.step()
    exchange.start()
    out_chain.step()
    downs[0].step()
    for load in loads:
        load.start()
    load_mid_grad(0).start()
    load_mid_grad(1).start()
    load_down.start()
    store_by_owner(wq_grad, normed_ref, dql_ref[...])
    query.step()
    cosine, sine = cos_ref[...], sin_ref[...]
    for head in range(KEY_VALUE_HEADS):
        span = slice(head * HEAD_SIZE, (head + 1) * HEAD_SIZE)
        dkvl[:, span] = rotate_back(dkv_ref[:, span].astype(f32), cosine, sine).astype(bf16)
    dkvl[:, KV_WIDTH:] = dkv_ref[:, KV_WIDTH:]
    store_by_owner(wkv_grad, normed_ref, dkvl[...])
    query.step(2)
    kv.step()
    for load in loads:
        load.wait()
    piece.step()
    downs[0].step()
    dgain = jnp.zeros((1, MODEL_WIDTH), f32)
    for part in range(4):
        band = slice(part * quarter, (part + 1) * quarter)
        grad = dot_nt(dql_ref[band, :], wq_ref[...])
        grad += dot_nt(dkvl[band, :KV_WIDTH], wk_ref[...])
        grad += dot_nt(dkvl[band, KV_WIDTH:], wv_ref[...])
        x = x_ref[band, :].astype(f32)
        r = lax.rsqrt(jnp.mean(x * x, axis=-1, keepdims=True) + epsilon)
        v = grad * gain_ref[...][None, :]
        inner = jnp.mean(v * x, axis=-1, keepdims=True)
        dgain += jnp.sum(grad * x * r, axis=0, keepdims=True)
        load_mid_grad(part).wait()
        mid_grad = mg_band[part % 2]
        dx_ref[band, :] = (mid_grad + r * v - x * (r * r * r * inner)).astype(bf16)
        if part < 2:
            load_mid_grad(part + 2).start()
        if part == 1:
            kv.step()
    gains_ref[0:1, :] = dgain
    gains_ref[1:2, :] = ffn_gain_ref[...]
    gains_ref[2:, :] = jnp.zeros((GAIN_ROWS - 2, MODEL_WIDTH), f32)
    gains.step()
    out_chain.step(2)
    piece.step()
    gains.step(2)
    downs[0].step()
    query.step(2)
    kv.step()
    load_down.wait()
    exchange.wait_recv()
    gains.step(2)
    downs[1].step()
    out_chain.step()
    kv.step(2)
    query.step(2)
    gains.step(2)
    out_chain.step()
    downs[1].step()
    kv.step(2)
    piece.step()
    gains.step()
    downs[0].step()
    query.step()
    downs[1].step()
    kv.step()
    everything = [query, kv, downs[1], downs[0], out_chain, piece, gains]
    while any(chain.done < len(chain.hops) for chain in everything):
        for chain in everything:
            chain.step()
    for chain in everything:
        chain.finish()
    exchange.wait_send()


def last_part(
    piece, down_sum, mine_down, other_down, dql, dkv, normed, wq, wk, wv, cosine, sine, x, gain,
    mg, ffn_gain_part, wo_sum,
):
    counts = sizes()
    n = counts["ctx"]
    full = FULL_AXES if ordered_in_kernel() else FULL_AXES[:3]
    widths = (MODEL_WIDTH, 2 * KV_WIDTH, MODEL_WIDTH)
    plan = [(full, MODEL_WIDTH), (full, MODEL_WIDTH), (full[2:], wo_sum.shape[0])]
    share, down_share = piece.shape[0] // n, mine_down.shape[1] // n
    shapes = [
        jax.ShapeDtypeStruct((share, 2 * FF), f32),
        jax.ShapeDtypeStruct((EXP_DEV, down_share, mine_down.shape[2]), f32),
        jax.ShapeDtypeStruct(x.shape, bf16),
        jax.ShapeDtypeStruct((GAIN_ROWS, MODEL_WIDTH), f32),
    ]
    scratch = [
        pltpu.VMEM((MODEL_WIDTH, MODEL_WIDTH), bf16),
        pltpu.VMEM((MODEL_WIDTH, 2 * KV_WIDTH), bf16),
        pltpu.VMEM((x.shape[0], 2 * KV_WIDTH), bf16),
        pltpu.VMEM((2, x.shape[0] // 4, MODEL_WIDTH), f32),
        pltpu.SemaphoreType.DMA((4,)),
    ]
    scratch += [
        pltpu.VMEM(a.shape, bf16) for a in (piece, down_sum, wo_sum, wq, wk, wv, x)
    ]
    scratch.append(pltpu.SemaphoreType.DMA((7,)))
    scratch += ring_buffers(n, 1, share, 2 * FF)
    scratch += [pltpu.VMEM(mine_down.shape[1:], bf16)] * 2 + [pltpu.SemaphoreType.DMA((3,))]
    for terms in (1, 2):
        scratch += ring_buffers(n, terms, down_share, mine_down.shape[2])
    for (names, rows), width in zip(plan, widths):
        for name in names:
            rows //= counts[name]
            scratch += ring_buffers(counts[name], 1, rows, width)[name == "ctx" :]
            if name != names[-1]:
                scratch.append(pltpu.VMEM((rows, width), bf16))
        shapes.append(jax.ShapeDtypeStruct((rows, width), f32 if "ctx" in names else bf16))
    for name in FULL_AXES:
        hops = counts[name] - 1
        scratch += [
            pltpu.VMEM((hops, GAIN_ROWS, MODEL_WIDTH), f32),
            pltpu.SemaphoreType.DMA((hops,)),
            pltpu.SemaphoreType.DMA((hops,)),
        ]
    vmem, hbm = pl.BlockSpec(memory_space=pltpu.VMEM), pl.BlockSpec(memory_space=pl.ANY)
    gate_up, down, dx, gains, *attention = pl.pallas_call(
        functools.partial(last_kernel, plan),
        in_specs=[hbm] * 4 + [vmem] * 3 + [hbm] * 3 + [vmem] * 2 + [hbm, vmem, hbm, vmem, hbm],
        out_specs=(vmem,) * 7,
        out_shape=tuple(shapes),
        scratch_shapes=scratch,
        compiler_params=params(collective_id=2, has_side_effects=True),
        cost_estimate=cost(1e10, 4e7),
        name="last_part",
    )(
        piece, down_sum, mine_down, other_down, dql, dkv, normed, wq, wk, wv, cosine, sine, x, gain,
        mg, ffn_gain_part, wo_sum,
    )
    if "ctx" not in full:
        attention = [
            scatter_axis(a.reshape(n, a.shape[0] // n, a.shape[1]), "ctx").astype(f32)
            for a in attention
        ]
    return gate_up, down, dx, gains, attention


def shifted(value, axis, steps):
    count = lax.axis_size(axis)
    return lax.ppermute(value, axis, [(i, (i + steps) % count) for i in range(count)])


def chip_shift(value, steps):
    count = lax.axis_size("exp")
    return lax.ppermute(value, "exp", [(i, (i + 2 * steps) % count) for i in range(count)])


def ring_part(parts, index, count, step, axis=0):
    return lax.dynamic_index_in_dim(parts, (index - 1 - step) % count, axis, keepdims=False)


def add_low(a, b):
    return (a.astype(f32) + b.astype(f32)).astype(bf16)


def ring_scatter(parts, shift, index, count, axis=0):
    total = ring_part(parts, index, count, 0, axis)
    for step in range(1, count):
        total = add_low(shift(total), ring_part(parts, index, count, step, axis))
    return total


def by_owner(array, axis):
    dp, ctx, exp = (lax.axis_size(a) for a in ("dp", "ctx", "exp"))
    size = array.shape[axis]
    before, after = array.shape[:axis], array.shape[axis + 1 :]
    parts = array.reshape(*before, dp, ctx, exp // 2, 2, size // (dp * ctx * exp), *after)
    order = list(range(axis)) + [axis + i for i in (3, 2, 0, 1, 4)]
    order += list(range(axis + 5, parts.ndim))
    return jnp.transpose(parts, order).reshape(array.shape)


def scatter_axis(parts, axis):
    return ring_scatter(
        parts, lambda v: shifted(v, axis, 1), lax.axis_index(axis), lax.axis_size(axis)
    )


def tie(*values):
    return lax.optimization_barrier(values)


def per_device(
    tokens, attn_gain, w_query, key_matrix, value_matrix, w_out, ffn_gain, expert_gate_up,
    expert_down, expert_ids, gate_weights, span_order, out_grad,
):
    ctx_size, exp_size = lax.axis_size("ctx"), lax.axis_size("exp")
    ctx_here, exp_here = lax.axis_index("ctx"), lax.axis_index("exp")
    experts = EXP_DEV * exp_size
    x, g = tokens[0], out_grad[0]
    rows = x.shape[0]
    capacity = rows * TOPK * 5 // (4 * experts)
    offsets = jnp.arange(HALF, dtype=jnp.int32)

    def device_positions(device):
        pair = lax.dynamic_slice_in_dim(span_order[0], 2 * device, 2, 0)
        return (pair[:, None] * HALF + offsets[None, :]).reshape(-1)

    sources = [(ctx_here - s) % ctx_size for s in range(ctx_size)]
    key_positions = [device_positions(s) for s in sources]
    positions = key_positions[0]
    exponent = jnp.arange(HEAD_SIZE // 2, dtype=f32) * (-2.0 / HEAD_SIZE)
    frequency = jnp.power(f32(rope_base), exponent)
    angles = positions.astype(f32)[:, None] * frequency[None, :]
    cosine, sine = jnp.cos(angles), jnp.sin(angles)
    cosine = jnp.concatenate([cosine, cosine], axis=1)
    sine = jnp.concatenate([-sine, sine], axis=1)

    kpos_rows = jnp.stack(key_positions)[:, None, :]
    normed, q, kv, att, att_low, lse, mid, nf, g_all, *routing = forward_to_experts(
        x, attn_gain, key_matrix, value_matrix, cosine, sine, positions[:, None],
        kpos_rows, ffn_gain, w_query, w_out, g, expert_ids[0].T,
        gate_weights[0].T,
    )

    dx_chip, y_chip, dx_far, y_far, *kept, _ = expert_blocks(
        capacity, *routing, nf, g_all, expert_gate_up, expert_down
    )
    slot_rows, hidden, slot_grad, projected_grad = (
        a.reshape(EXP_DEV, exp_size * capacity, a.shape[-1]) for a in kept
    )
    nf_grad_terms = [dx_chip] + [
        chip_shift(dx_far[s - 1], -s) for s in range(1, exp_size // 2)
    ]
    dp_size, dp_here = lax.axis_size("dp"), lax.axis_index("dp")
    theirs = weight_grad(
        0, 1, (dp_here - 1) % dp_size, MODEL_WIDTH // dp_size, slot_rows, projected_grad
    )[0]
    if not ordered_in_kernel():
        normed, att_low = by_owner(normed, 1), by_owner(att_low, 1)
    slot_rows, theirs = tie(slot_rows, theirs)
    came = shifted(theirs, "dp", 1)
    theirs_next, mine, mine_next, other_down, mine_down = other_weight_grads(
        dp_here, dp_size, slot_rows, projected_grad, hidden, slot_grad
    )
    nf_grad_terms, mine, y_far = tie(nf_grad_terms, mine, y_far)

    mid_grad, att_grad, delta, ffn_gain_part, w_out_grad = middle_backward(
        nf_grad_terms, mid, g, ffn_gain, w_out, att, att_low
    )
    att_grad, came = tie(att_grad, came)
    y_terms = [y_chip] + [chip_shift(y_far[s - 1], -s) for s in range(1, exp_size // 2)]

    dql, dkv, gate_up_first, gate_up_next, down_sum, w_out_sum = attention_backward(
        q, att_grad, kv, lse, delta, kpos_rows, positions[None, :],
        cosine, sine, mine, came, w_out_grad, theirs_next, mine_next, other_down, mine_down,
    )
    gate_up_second, down_share, tokens_grad, gains, attention = last_part(
        gate_up_next, down_sum, mine_down, other_down, dql, dkv, normed, w_query, key_matrix,
        value_matrix, cosine, sine, x, attn_gain, mid_grad, ffn_gain_part, w_out_sum,
    )
    w_query_share, w_kv_share, w_out_share = attention
    layer_output = mid
    for term in y_terms:
        layer_output = layer_output + term.astype(f32)
    layer_output = layer_output.astype(bf16)
    owner = (lax.axis_index("dp") * ctx_size + ctx_here) * exp_size + exp_here
    gain_share = MODEL_WIDTH // (dp_size * ctx_size * exp_size)
    gains = lax.dynamic_slice_in_dim(gains, owner * gain_share, gain_share, 1)
    return (
        layer_output[None],
        tokens_grad[None],
        gains[0],
        w_query_share,
        w_kv_share[:, :KV_WIDTH],
        w_kv_share[:, KV_WIDTH:],
        w_out_share,
        gains[1],
        jnp.stack([gate_up_first, gate_up_second]),
        down_share,
    )


def solution(mesh):
    by_row = P(("dp", "exp"), "ctx", None)
    share = P(("dp", "ctx", "exp"))
    share_rows = P(("dp", "ctx", "exp"), None)
    return jax.shard_map(
        per_device,
        mesh=mesh,
        in_specs=(
            by_row, P(), P(), P(), P(), P(), P(), P("exp", None, None), P("exp", None, None),
            by_row, by_row, P(("dp", "exp"), None), by_row,
        ),
        out_specs=(
            by_row, by_row, share, share_rows, share_rows, share_rows, share_rows, share,
            P("exp", ("dp", "ctx"), None), P("exp", ("dp", "ctx"), None),
        ),
        check_vma=False,
    )
```
